32 devices in a mesh: dp: 8 (over z, y), grp: 4 (over x, core).
Axes of the slice: x: 2, y: 2, z: 4, core: 2. Of those that a mesh axis runs over, the one named last changes fastest.
Arguments:
- patches: bfloat16 [27648, 1728], P(('dp', 'grp')), may hold values from -6 to 6
- segments: int32 [27648], P(('dp', 'grp')), may hold values from -1 to 73, as said below
- visible: int32 [3072], P(('dp', 'grp')), may hold values from 0 to 3455, as said below
- enc_params: float32 [66048, 128], P('dp')
- enc_first: float32 [66048, 128], P('dp'), may hold values from -8.34465e-07 to 8.34465e-07
- enc_second: float32 [66048, 128], P('dp'), may hold values from 3.0982314e-15 to 1.23929255e-14
- enc_average: float32 [66048, 128], P('dp')
- dec_params: float32 [34816, 128], P('dp')
- dec_first: float32 [34816, 128], P('dp'), may hold values from -8.34465e-07 to 8.34465e-07
- dec_second: float32 [34816, 128], P('dp'), may hold values from 3.0982314e-15 to 1.23929255e-14
- step_count: int32 [1], replicated, may hold values from 1 to 20
Outputs:
- new_enc_params: float32 [66048, 128], P('dp')
- new_enc_first: float32 [66048, 128], P('dp')
- new_enc_second: float32 [66048, 128], P('dp')
- new_enc_copy: bfloat16 [66048, 128], P('dp')
- new_dec_params: float32 [34816, 128], P('dp')
- new_dec_first: float32 [34816, 128], P('dp')
- new_dec_second: float32 [34816, 128], P('dp')
- new_dec_copy: bfloat16 [34816, 128], P('dp')
- new_enc_average: float32 [66048, 128], P('dp')
- grad_norm: float32 [], replicated
- loss: float32 [], replicated
- count: float32 [], replicated
The draws below stay inside these ranges and needn't reach their ends.
Inputs may be any that keep to these rules, and one draw needn't show every extreme that they name: `segments`: within a group, each of the 2 sequences holds whole tiles of 48 to 192 slots from its start, and padding (-1) only after its last tile. The tiles of sequence s are numbered consecutively, ending with (s + 1) * 37 - 1. `visible`: slots of the device's group, distinct over the group, never padding. Each device has exactly 96 encoder rows; at most 48 of one device's rows name slots held by one device of its group, and in every group some such pair has exactly 48; every device of a group holds exactly 96 named slots.
All inputs are finite; a program needn't handle non-finite values.
Results may differ from the reference program's by a relative error of at most 0.00065.
The reference program's roundings to bfloat16 on the way count: a program that leaves them out, or rounds other values in their place, can miss the bound.
Values may be sent and summed in bfloat16 or wider, within the bound.
No kernel may reach another device: no remote copies, remote signals or barrier semaphores. Data moves between devices by JAX's collectives and lax.ppermute only.
A program may use at most 320 MiB of HBM per device.

```python
import math
import jax
import jax.numpy as jnp
from jax import lax

D = 768
H = 12
F = 3072
E = 512
EH = 16
FE = 2048
PATCH = 1728
L = 1728
SEQ = 2
TILE_LO = 48
TILE_HI = 192
TILES = 37
CAPV = 48
VIS = 96
SLOTS = 27648
ER = 66048
DR = 34816


def group_visible(group_key, group_ids):
    slot_dev = SEQ * L // 4
    capacity = CAPV
    subkeys = jax.random.split(group_key, 7)
    base_counts = jnp.array([capacity, capacity // 2, capacity // 4, capacity - capacity // 2 - capacity // 4], dtype=jnp.int32)
    counts = base_counts[jax.random.permutation(subkeys[0], 4)]
    offset = jax.random.randint(subkeys[1], (), 0, 4)
    dest_ids = jnp.arange(4, dtype=jnp.int32)[:, None]
    source_ids = jnp.arange(4, dtype=jnp.int32)[None, :]
    pairing = counts[(source_ids - dest_ids + offset) % 4]
    seg_dev = group_ids.reshape(4, slot_dev)
    scores = jax.random.randint(subkeys[2], (4, slot_dev), 0, 1024) * slot_dev + jnp.arange(slot_dev, dtype=jnp.int32)[None, :] + jnp.where(seg_dev < 0, 2 ** 29, 0)
    chosen = jnp.argsort(scores, axis=1)[:, :VIS]
    starting = jnp.cumsum(pairing, axis=0) - pairing
    row_end = jnp.cumsum(pairing, axis=1)
    row_ids = jnp.arange(VIS, dtype=jnp.int32)
    row_source = jnp.sum((row_end[:, None, :] <= row_ids[None, :, None]).astype(jnp.int32), axis=2)
    before = jnp.take_along_axis(row_end - pairing, row_source, axis=1)
    placing = jnp.take_along_axis(starting, row_source, axis=1) + row_ids[None, :] - before
    slot_ids = row_source * slot_dev + chosen[row_source, placing]
    orders = jnp.stack([jax.random.permutation(subkeys[3 + index], VIS) for index in range(4)])
    return jnp.take_along_axis(slot_ids, orders, axis=1)


def layout_draw(key):
    base = jax.random.fold_in(key, 7)
    group_slots = SEQ * L
    groups = SLOTS // group_slots
    seq_keys = jax.random.split(jax.random.fold_in(base, 1), groups * SEQ)
    spots = jnp.arange(L, dtype=jnp.int32)

    def one_sequence(seq_key):
        lengths = jax.random.randint(seq_key, (TILES,), TILE_LO, TILE_HI + 1)
        ends = jnp.cumsum(lengths)
        ident = jnp.sum((ends[None, :] <= spots[:, None]).astype(jnp.int32), axis=1)
        last_end = jnp.max(jnp.where(ends <= L, ends, 0))
        whole_tiles = jnp.sum((ends <= L).astype(jnp.int32))
        return jnp.where(spots < last_end, ident + TILES - whole_tiles, -1)
    seq_ids = jax.vmap(one_sequence)(seq_keys).reshape(groups, SEQ, L)
    offsets = (jnp.arange(SEQ, dtype=jnp.int32) * TILES)[None, :, None]
    group_ids = jnp.where(seq_ids >= 0, seq_ids + offsets, -1).reshape(groups, group_slots)
    group_keys = jax.random.split(jax.random.fold_in(base, 2), groups)
    visible_ids = jax.vmap(group_visible)(group_keys, group_ids)
    return (group_ids.reshape(-1), visible_ids.reshape(-1))


def draw_segments(key, part):
    return layout_draw(key)[0]


def draw_visible(key, part):
    return layout_draw(key)[1]


def enc_list():
    return [((PATCH, D), PATCH ** (-0.5), 0.0), ((D, 3 * D), D ** (-0.5), 0.0), ((D, D), 3.0 * D ** (-0.5), 0.0), ((D, F), D ** (-0.5), 0.0), ((F, D), F ** (-0.5), 0.0), ((D,), 0.2, 0.0), ((D,), 0.2, 0.0), ((F,), 0.2, 0.0), ((D,), 0.2, 0.0), ((3, D), 0.1, 1.0), ((3, D), 0.2, 0.0)]


def dec_list():
    return [((D, E), D ** (-0.5), 0.0), ((E, 3 * E), E ** (-0.5), 0.0), ((E, E), 6.0 * E ** (-0.5), 0.0), ((E, FE), E ** (-0.5), 0.0), ((FE, E), FE ** (-0.5), 0.0), ((E, PATCH), E ** (-0.5), 0.0), ((E,), 0.2, 0.0), ((E,), 1.0, 0.0), ((E,), 0.2, 0.0), ((FE,), 0.2, 0.0), ((E,), 0.2, 0.0), ((PATCH,), 0.2, 0.0), ((3, E), 0.1, 1.0), ((3, E), 0.2, 0.0)]


def draw_buffer(key, listing, total_rows):
    members = []
    for position, entry in enumerate(listing):
        piece_dims, scale, center = entry
        values = jax.random.normal(jax.random.fold_in(key, 100 + position), piece_dims, jnp.float32) * scale + center
        members.append(values.reshape(-1))
    joined = jnp.concatenate(members)
    return jnp.pad(joined, (0, total_rows * 128 - joined.shape[0])).reshape(total_rows, 128)


def draw_enc_params(key, part):
    return draw_buffer(jax.random.fold_in(key, 1), enc_list(), ER)


def draw_enc_average(key, part):
    return draw_buffer(jax.random.fold_in(key, 2), enc_list(), ER)


def draw_dec_params(key, part):
    return draw_buffer(jax.random.fold_in(key, 3), dec_list(), DR)


def shard_levels(stream_key, extent, cuts, least, top_value):
    def one(dim, blocks):
        draws = jax.random.uniform(jax.random.fold_in(jax.random.fold_in(stream_key, 6), dim), (blocks,), jnp.float32, least / len(cuts), top_value / len(cuts))
        return jnp.repeat(jnp.exp(draws), extent[dim] // blocks).reshape((-1,) + (1,) * (len(extent) - dim - 1))

    level = one(*cuts[0])
    for cut in cuts[1:]:
        level = level * one(*cut)
    return level


def gaussian(key, dims, deviation, bound, cuts=(), kind=jnp.bfloat16):
    loudness = shard_levels(key, dims, cuts, -0.22, 0.18) if cuts else 1.0
    drawn = jax.random.normal(key, dims, jnp.float32) * deviation * loudness
    return jnp.minimum(jnp.maximum(drawn, -bound), bound).astype(kind)


def setup_inputs(seed: int = 0) -> dict:
    seeds = jax.random.split(jax.random.key(seed), 12)
    patches = gaussian(seeds[0], (SLOTS, PATCH), 1.0, 6.0, ((0, 32),))
    segments = draw_segments(jax.random.fold_in(seeds[11], 71), 0)
    visible = draw_visible(jax.random.fold_in(seeds[11], 71), 0)
    enc_params = draw_enc_params(jax.random.fold_in(seeds[11], 71), 0)
    enc_first = gaussian(seeds[4], (ER, 128), (0.0002 / ((ER + DR) * 128) ** 0.5), 8.344650268554688e-07, ((0, 8),), jnp.float32)
    enc_second = jnp.clip(jnp.exp(math.log(1.2392925498750512e-14) - 1.3862944 * jax.random.uniform(seeds[5], (ER, 128), jnp.float32) ** shard_levels(seeds[5], (ER, 128), ((0, 8),), -0.2, 0.2)), 3.098231374687628e-15, 1.2392925498750512e-14)
    enc_average = draw_enc_average(jax.random.fold_in(seeds[11], 71), 0)
    dec_params = draw_dec_params(jax.random.fold_in(seeds[11], 71), 0)
    dec_first = gaussian(seeds[8], (DR, 128), (0.0002 / ((ER + DR) * 128) ** 0.5), 8.344650268554688e-07, ((0, 8),), jnp.float32)
    dec_second = jnp.clip(jnp.exp(math.log(1.2392925498750512e-14) - 1.3862944 * jax.random.uniform(seeds[9], (DR, 128), jnp.float32) ** shard_levels(seeds[9], (DR, 128), ((0, 8),), -0.2, 0.2)), 3.098231374687628e-15, 1.2392925498750512e-14)
    step_count = jax.random.randint(seeds[10], (1,), 1, 21).astype(jnp.int32)
    return dict(patches=patches, segments=segments, visible=visible, enc_params=enc_params, enc_first=enc_first, enc_second=enc_second, enc_average=enc_average, dec_params=dec_params, dec_first=dec_first, dec_second=dec_second, step_count=step_count)


NORM_EPS = 1e-06
MASK_FILL = -1e+30
CLIP_LIMIT = 0.0002
LEARN_RATE = 0.02
BETA_ONE = 0.5
BETA_TWO = 0.5
ADAM_EPS = 1e-08
WEIGHT_DECAY = 0.05
EMA_RATE = 0.9

@jax.custom_vjp
def low(v):
    return lax.optimization_barrier(v.astype(jnp.bfloat16)).astype(jnp.float32)

@jax.custom_vjp
def low_back(v):
    return v

def low_keep(v):
    return (low(v), None)

def low_pass(kept, grad):
    return (grad,)

def back_keep(v):
    return (v, None)

def back_low(kept, grad):
    return (low(grad),)
low.defvjp(low_keep, low_pass)
low_back.defvjp(back_keep, back_low)

def enc_pieces():
    return [('patch_w', (PATCH, D)), ('qkv_w', (D, 3 * D)), ('out_w', (D, D)), ('up_w', (D, F)), ('down_w', (F, D)), ('patch_b', (D,)), ('out_b', (D,)), ('up_b', (F,)), ('down_b', (D,)), ('norm_g', (3, D)), ('norm_b', (3, D))]

def dec_pieces():
    return [('embed_w', (D, E)), ('qkv_w', (E, 3 * E)), ('out_w', (E, E)), ('up_w', (E, FE)), ('down_w', (FE, E)), ('pix_w', (E, PATCH)), ('embed_b', (E,)), ('mask_token', (E,)), ('out_b', (E,)), ('up_b', (FE,)), ('down_b', (E,)), ('pix_b', (PATCH,)), ('norm_g', (3, E)), ('norm_b', (3, E))]

def unpack(flat_vec, pieces):
    table = {}
    offset = 0
    for piece_name, piece_dims in pieces:
        amount = math.prod(piece_dims)
        table[piece_name] = flat_vec[offset:offset + amount].reshape(piece_dims)
        offset += amount
    return table

def mul(left, right):
    return jnp.dot(left, right, precision=lax.Precision.HIGHEST)

def sincos(positions, width):
    half_width = width // 2
    freq_row = jnp.exp(jnp.arange(half_width, dtype=jnp.float32) * (-2.0 * math.log(10000.0) / width))
    angles = positions.astype(jnp.float32)[:, None] * freq_row[None, :]
    return jnp.concatenate([jnp.sin(angles), jnp.cos(angles)], axis=1)

def layer_norm(inputs, gain, shift):
    center = inputs - lax.optimization_barrier(jnp.mean(inputs, axis=-1, keepdims=True))
    return center * lax.rsqrt(lax.optimization_barrier(jnp.mean(center * center, axis=-1, keepdims=True)) + NORM_EPS) * gain + shift

def attention(query, keys, values, allowed, heads):
    width = query.shape[1] // heads
    scale = width ** (-0.5)

    def one_head(index):
        query_head = lax.dynamic_slice_in_dim(query, index * width, width, 1)
        key_head = lax.dynamic_slice_in_dim(keys, index * width, width, 1)
        value_head = lax.dynamic_slice_in_dim(values, index * width, width, 1)
        scores = low_back(mul(query_head, key_head.T) * scale)
        scores = jnp.where(allowed, scores, MASK_FILL)
        shifted = jnp.exp(scores - lax.optimization_barrier(jnp.max(scores, axis=1, keepdims=True)))
        probs = low(shifted / lax.optimization_barrier(jnp.sum(shifted, axis=1, keepdims=True)))
        return mul(probs, value_head)
    outputs = lax.map(jax.checkpoint(one_head), jnp.arange(heads, dtype=jnp.int32))
    return outputs.transpose(1, 0, 2).reshape(query.shape[0], -1)

def block(inputs, table, heads, allowed):
    gains = table['norm_g']
    shifts = table['norm_b']
    width = inputs.shape[1]
    normed_one = low(layer_norm(inputs, gains[0], shifts[0]))
    qkv = low(low_back(mul(normed_one, table['qkv_w'])))
    attended = low(low_back(attention(qkv[:, :width], qkv[:, width:2 * width], qkv[:, 2 * width:], allowed, heads)))
    mixed = inputs + low_back(mul(attended, table['out_w']) + table['out_b'])
    normed_two = low(layer_norm(mixed, gains[1], shifts[1]))
    hidden = low_back(mul(normed_two, table['up_w']) + table['up_b'])
    activated = low(jax.nn.gelu(hidden, approximate=False))
    return mixed + low_back(mul(activated, table['down_w']) + table['down_b'])

def group_loss(enc_table, dec_table, pixels, group_seg, group_vis):
    slot_total = group_seg.shape[0]
    vis_seg = group_seg[group_vis]
    enc_allowed = vis_seg[:, None] == vis_seg[None, :]
    enc_start = low_back(mul(pixels[group_vis], enc_table['patch_w']) + enc_table['patch_b']) + sincos(group_vis % L, D)
    enc_out = block(enc_start, enc_table, H, enc_allowed)
    enc_final = low(layer_norm(enc_out, enc_table['norm_g'][2], enc_table['norm_b'][2]))
    latent = low(low_back(mul(enc_final, dec_table['embed_w']) + dec_table['embed_b']))
    seen = jnp.zeros((slot_total,), jnp.float32).at[group_vis].set(1.0)
    placed = jnp.zeros((slot_total, E), jnp.float32).at[group_vis].set(latent)
    positions = jnp.arange(slot_total, dtype=jnp.int32) % L
    dec_start = jnp.where(seen[:, None] > 0.5, placed, dec_table['mask_token'][None, :]) + sincos(positions, E)
    dec_allowed = group_seg[:, None] == group_seg[None, :]
    dec_out = block(dec_start, dec_table, EH, dec_allowed)
    dec_final = low(layer_norm(dec_out, dec_table['norm_g'][2], dec_table['norm_b'][2]))
    predicted = low_back(mul(dec_final, dec_table['pix_w']) + dec_table['pix_b'])
    centered = pixels - lax.optimization_barrier(jnp.mean(pixels, axis=1, keepdims=True))
    target = centered * lax.rsqrt(lax.optimization_barrier(jnp.mean(centered * centered, axis=1, keepdims=True)) + NORM_EPS)
    counted = jnp.where((group_seg >= 0) & (seen < 0.5), 1.0, 0.0)
    errors = predicted - target
    return jnp.sum(counted * lax.optimization_barrier(jnp.mean(errors * errors, axis=1)))

def adamw(weights, first, second, gradient, factor, steps_done):
    clipped = gradient * factor
    first_new = BETA_ONE * first + (1.0 - BETA_ONE) * clipped
    second_new = BETA_TWO * second + (1.0 - BETA_TWO) * clipped * clipped
    first_hat = first_new / (1.0 - BETA_ONE ** steps_done)
    second_hat = second_new / (1.0 - BETA_TWO ** steps_done)
    weights_new = weights * (1.0 - LEARN_RATE * WEIGHT_DECAY) - LEARN_RATE * first_hat / (jnp.sqrt(second_hat) + ADAM_EPS)
    return (weights_new, first_new, second_new)

def reference(patches, segments, visible, enc_params, enc_first, enc_second, enc_average, dec_params, dec_first, dec_second, step_count):
    group_slots = SEQ * L
    groups = segments.shape[0] // group_slots
    pixel_groups = patches.astype(jnp.float32).reshape(groups, group_slots, PATCH)
    seg_groups = segments.reshape(groups, group_slots)
    vis_groups = visible.reshape(groups, -1)
    total_count = (jnp.sum((segments >= 0).astype(jnp.int32)) - visible.shape[0]).astype(jnp.float32)

    def loss_fn(enc_flat, dec_flat):
        enc_table = unpack(low(enc_flat).reshape(-1), enc_pieces())
        dec_table = unpack(low(dec_flat).reshape(-1), dec_pieces())

        def step_fn(carry, items):
            return (carry + group_loss(enc_table, dec_table, items[0], items[1], items[2]), None)
        total, _ = lax.scan(jax.checkpoint(step_fn), jnp.zeros((), jnp.float32), (pixel_groups, seg_groups, vis_groups))
        return (total / total_count, total)
    mean_value, pull, loss_sum = jax.vjp(loss_fn, enc_params, dec_params, has_aux=True)
    enc_grad, dec_grad = pull(jnp.ones((), jnp.float32))
    grad_norm = jnp.sqrt(jnp.sum(enc_grad * enc_grad) + jnp.sum(dec_grad * dec_grad))
    factor = jnp.minimum(1.0, CLIP_LIMIT / (grad_norm + NORM_EPS))
    steps_done = step_count[0].astype(jnp.float32)
    enc_new, enc_first_new, enc_second_new = adamw(enc_params, enc_first, enc_second, enc_grad, factor, steps_done)
    dec_new, dec_first_new, dec_second_new = adamw(dec_params, dec_first, dec_second, dec_grad, factor, steps_done)
    average_new = EMA_RATE * enc_average + (1.0 - EMA_RATE) * enc_new
    return (enc_new, enc_first_new, enc_second_new, enc_new.astype(jnp.bfloat16), dec_new, dec_first_new, dec_second_new, dec_new.astype(jnp.bfloat16), average_new, grad_norm, loss_sum, total_count)
```

```python
import functools
import math

import jax
import jax.numpy as jnp
from jax import lax
from jax.experimental import pallas as pl
from jax.experimental.pallas import tpu as pltpu
from jax.sharding import PartitionSpec as P

D = 768
H = 12
F = 3072
E = 512
EH = 16
FE = 2048
PATCH = 1728
L = 1728
TILE_HI = 192
ER = 66048
DR = 34816


NORM_EPS = 1e-06
MASK_FILL = -1e30
CLIP_LIMIT = 0.0002
LEARN_RATE = 0.02
BETA_ONE = 0.5
BETA_TWO = 0.5
ADAM_EPS = 1e-08
WEIGHT_DECAY = 0.05
EMA_RATE = 0.9


def swap(block, axis, bit):
    count = lax.axis_size(axis)
    return lax.ppermute(block, axis, [(i, i ^ bit) for i in range(count)])


def bit_of(axis, bit):
    return (lax.axis_index(axis) // bit) % 2


def double(block, dim, axis, bit):
    mine = bit_of(axis, bit)
    other = swap(block, axis, bit)
    first = jnp.where(mine == 0, block, other)
    second = jnp.where(mine == 0, other, block)
    return jnp.stack([first, second], axis=dim)


def total(values):
    for axis in ("grp", "dp"):
        bit = 1
        while bit < lax.axis_size(axis):
            values = values + swap(values, axis, bit)
            bit *= 2
    return values


def dp_bits():
    bits = [1]
    while bits[-1] * 2 < lax.axis_size("dp"):
        bits.append(bits[-1] * 2)
    return bits


def routes():
    bits = [("dp", bit) for bit in dp_bits()]
    side = [("grp", 2)]
    return [side + bits, bits + side, bits[1:] + side + bits[:1]]


def cut(rows, shares):
    unit = 16 if rows % 16 == 0 else 2
    units = rows // unit
    first = int(round(units * shares[0]))
    second = int(round(units * shares[1]))
    return [first * unit, second * unit, (units - first - second) * unit]


GATHER_SHARES = (0.36, 0.34)
REDUCE_SHARES = (0.333, 0.333)


def gather_chunk(block, route):
    blocks = [block]
    for order, stage in enumerate(reversed(route)):
        blocks = blocks + [swap(part, *stage) for part in blocks]
        if order < 2:
            blocks = [jnp.concatenate(blocks, axis=0)]
    return blocks


def place_kernel(route, rows, offset, part, *refs):
    sources, out_ref, sems = refs[:-2], refs[-2], refs[-1]
    stages = list(reversed(route))
    count = 2 ** len(stages)
    place = lax.axis_index("dp")
    lane = lax.axis_index("grp")
    arrays = count // 4
    for side in range(2):
        for index in range(count):
            shard, member = place, lane ^ side
            for order, (axis, bit) in enumerate(stages):
                differs = ((index >> order) & 1) * bit
                if axis == "dp":
                    shard = shard ^ differs
                else:
                    member = member ^ differs
            target = pl.multiple_of((shard * 4 + member) * part + offset, 16)
            pltpu.make_async_copy(
                sources[side * arrays + index // 4].at[pl.ds(index % 4 * rows, rows)],
                out_ref.at[pl.ds(target, rows)],
                sems.at[side * arrays + index // 4],
            ).start()
    for index in range(2 * arrays):
        pltpu.make_async_copy(
            sources[index], out_ref.at[pl.ds(0, 4 * rows)], sems.at[index]
        ).wait()


def gather_place(chunks, shard_rows):
    part = shard_rows // 4
    total_rows = shard_rows * lax.axis_size("dp")
    result = None
    offset = 0
    for route, rows, blocks in zip(routes(), cut(part, GATHER_SHARES), chunks):
        operands = blocks + [swap(block, "grp", 1) for block in blocks]
        count = len(operands)
        specs = [pl.BlockSpec(memory_space=pltpu.VMEM)] * count
        kernel = functools.partial(place_kernel, route, rows, offset, part)
        if result is not None:
            operands = operands + [result]
            specs = specs + [pl.BlockSpec(memory_space=pl.ANY)]
            kernel = functools.partial(skip_last_input, kernel, count)
        result = pl.pallas_call(
            kernel,
            in_specs=specs,
            out_specs=pl.BlockSpec(memory_space=pl.ANY),
            out_shape=jax.ShapeDtypeStruct((total_rows, 128), blocks[0].dtype),
            scratch_shapes=[pltpu.SemaphoreType.DMA((count,))],
            input_output_aliases={count: 0} if len(operands) > count else {},
        )(*operands)
        offset += rows
    return result


def skip_last_input(kernel, count, *refs):
    kernel(*refs[:count], *refs[count + 1 :])


def gather_both(enc_shard, dec_shard):
    if enc_shard.shape[0] % 64 or dec_shard.shape[0] % 64:
        return tuple(
            lax.all_gather(shard, "dp", axis=0, tiled=True) for shard in (enc_shard, dec_shard)
        )
    quarters = []
    for shard in (enc_shard, dec_shard):
        part = shard.shape[0] // 4
        quarters.append(
            lax.dynamic_slice_in_dim(shard, lax.axis_index("grp") * part, part, 0)
        )
    chunks = ([], [])
    start = [0, 0]
    for index, route in enumerate(routes()):
        blocks = None
        for which, quarter in enumerate(quarters):
            rows = cut(quarter.shape[0], GATHER_SHARES)[index]
            block = lax.slice_in_dim(quarter, start[which], start[which] + rows, axis=0)
            start[which] += rows
            if which:
                blocks, block = lax.optimization_barrier((blocks, block))
                chunks[0].append(blocks)
            blocks = gather_chunk(block, route)
        chunks[1].append(blocks)
    return gather_place(chunks[0], enc_shard.shape[0]), gather_place(chunks[1], dec_shard.shape[0])


def section(cells, dim, start, size):
    return lax.dynamic_slice_in_dim(cells, start, size, dim)


def reduce_bit(cells, dim, axis, bit, start=0, size=None):
    half = (cells.shape[dim] if size is None else size) // 2
    mine = bit_of(axis, bit)
    sent = section(cells, dim, start + (1 - mine) * half, half)
    return section(cells, dim, start + mine * half, half) + swap(sent, axis, bit)


def reduce_routes():
    low, rest = dp_bits()[:1], dp_bits()[1:]
    side, low = [("grp", 2)], [("dp", bit) for bit in low]
    rest = [("dp", bit) for bit in rest]
    return [side + low + rest, low + rest[:1] + side + rest[1:], rest[:1] + side + rest[1:] + low]


def reduce_stages(half):
    shards = lax.axis_size("dp")
    half_rows = half.shape[0] // shards
    bits = dp_bits()
    names = [("dp", bit) for bit in reversed(bits)]
    cells = half.reshape([2] * len(bits) + [half_rows, 128])
    blocks = []
    start = 0
    for route, rows in zip(reduce_routes(), cut(half_rows, REDUCE_SHARES)):
        axis, bit = route[0]
        if axis == "grp":
            block = reduce_bit(cells, len(bits), axis, bit, start, rows)
        else:
            dim = names.index(route[0])
            mine = bit_of(axis, bit)

            def pick(index, dim=dim, start=start, rows=rows):
                corner = [0] * dim + [index] + [0] * (len(bits) - dim - 1) + [start, 0]
                sizes = [2] * dim + [1] + [2] * (len(bits) - dim - 1) + [rows, 128]
                return lax.dynamic_slice(cells, corner, sizes)

            block = pick(mine) + swap(pick(1 - mine), axis, bit)
        blocks.append(block)
        start += rows
    for step in range(1, len(bits) + 1):
        for index, route in enumerate(reduce_routes()):
            axis, bit = route[step]
            dim = len(bits) if axis == "grp" else names.index(route[step])
            blocks[index] = reduce_bit(blocks[index], dim, axis, bit)
    return [block.reshape(-1, 128) for block in blocks]


def spread_pieces(pieces):
    wide = [double(piece, 0, "grp", 2).reshape(-1, 128) for piece in pieces]
    mine = jnp.concatenate(wide, axis=0)
    return mine, swap(mine, "grp", 1)


def group_rows(block):
    across = swap(block, "grp", 2)
    near, far = (
        swap(block, "grp", 1),
        swap(across, "grp", 1),
    )
    return jnp.concatenate([block, near, across, far], axis=0)


def own_rows(blocks):
    count = blocks.shape[0] // 4
    parts = [lax.slice_in_dim(blocks, i * count, (i + 1) * count, axis=0) for i in range(4)]
    sent = jnp.concatenate([parts[1], parts[3]], axis=0)
    arrived = swap(sent, "grp", 1)
    kept = parts[0] + arrived[:count]
    other = parts[2] + arrived[count:]
    return kept + swap(other, "grp", 2)


def extended(cells, width):
    count = lax.axis_size("grp")
    ends = count - 1
    head = cells[:width]
    tail = cells[cells.shape[0] - width :]
    return jnp.concatenate(
        [
            lax.ppermute(tail, "grp", [(i, i + 1) for i in range(ends)]),
            cells,
            lax.ppermute(head, "grp", [(i + 1, i) for i in range(ends)]),
        ],
        axis=0,
    )


def passed_along(block, axis, distance):
    devices = range(lax.axis_size(axis))
    route = [(i - distance, i) for i in devices if i - distance in devices]
    return lax.ppermute(block, axis, route)


def enc_pieces():
    return [
        ("patch_w", (PATCH, D)),
        ("qkv_w", (D, 3 * D)),
        ("out_w", (D, D)),
        ("up_w", (D, F)),
        ("down_w", (F, D)),
        ("patch_b", (D,)),
        ("out_b", (D,)),
        ("up_b", (F,)),
        ("down_b", (D,)),
        ("norm_g", (3, D)),
        ("norm_b", (3, D)),
    ]


def dec_pieces():
    return [
        ("embed_w", (D, E)),
        ("qkv_w", (E, 3 * E)),
        ("out_w", (E, E)),
        ("up_w", (E, FE)),
        ("down_w", (FE, E)),
        ("pix_w", (E, PATCH)),
        ("embed_b", (E,)),
        ("mask_token", (E,)),
        ("out_b", (E,)),
        ("up_b", (FE,)),
        ("down_b", (E,)),
        ("pix_b", (PATCH,)),
        ("norm_g", (3, E)),
        ("norm_b", (3, E)),
    ]


def unpack(rows, pieces):
    table = {}
    offset = 0
    vectors = sum(1 for _, dims in pieces if len(dims) == 2 and dims[0] > 3)
    for piece_name, piece_dims in pieces[:vectors]:
        amount = math.prod(piece_dims) // 128
        table[piece_name] = rows[offset : offset + amount].reshape(piece_dims)
        offset += amount
    small = rows[offset:].reshape(-1)
    offset = 0
    for piece_name, piece_dims in pieces[vectors:]:
        amount = math.prod(piece_dims)
        table[piece_name] = small[offset : offset + amount].reshape(piece_dims)
        offset += amount
    return table


def matmul(left, right):
    return jnp.dot(left, right, preferred_element_type=jnp.float32)


def mul_trans(left, right):
    return lax.dot_general(
        left, right, (((1,), (1,)), ((), ())), preferred_element_type=jnp.float32
    )


def trans_mul(left, right):
    return lax.dot_general(
        left, right, (((0,), (0,)), ((), ())), preferred_element_type=jnp.float32
    )


def sincos(positions, width):
    half_width = width // 2
    freq_row = jnp.exp(
        jnp.arange(half_width, dtype=jnp.float32) * (-2.0 * math.log(10000.0) / width)
    )
    angles = positions.astype(jnp.float32)[:, None] * freq_row[None, :]
    return jnp.concatenate([jnp.sin(angles), jnp.cos(angles)], axis=1)


def layer_norm(inputs, gain, shift):
    center = inputs - jnp.mean(inputs, axis=-1, keepdims=True)
    return (
        center * lax.rsqrt(jnp.mean(center * center, axis=-1, keepdims=True) + NORM_EPS) * gain
        + shift
    )


def norm_back(inputs, gain, shift, grad_out):
    outputs, pull = jax.vjp(layer_norm, inputs, gain, shift)
    return pull(grad_out)


def exact_gelu(values):
    return jax.nn.gelu(values, approximate=False)


BLOCK = 128


def head_masks(width):
    lanes = lax.broadcasted_iota(jnp.int32, (1, 128), 1) // width
    return [(lanes == index).astype(jnp.float32) for index in range(128 // width)]


def spread_heads(cells, masks):
    wide = cells.astype(jnp.float32)
    return jnp.concatenate([(wide * mask).astype(jnp.bfloat16) for mask in masks], axis=0)


def attend_kernel(window, width, q_ref, k_ref, v_ref, qid_ref, kid_ref, o_ref):
    start = pl.multiple_of(pl.program_id(0) * BLOCK, BLOCK)
    scale = width ** (-0.5)
    masks = head_masks(width)
    bias = jnp.where(qid_ref[...] == kid_ref[:, pl.ds(start, window)], 0.0, MASK_FILL)
    for group in range(q_ref.shape[1] // 128):
        lanes = slice(group * 128, (group + 1) * 128)
        keys = k_ref[pl.ds(start, window), lanes]
        values = v_ref[pl.ds(start, window), lanes]
        stacked = spread_heads(q_ref[:, lanes], masks)
        scores = mul_trans(stacked, keys) * scale
        outcome = jnp.zeros((BLOCK, 128), jnp.float32)
        for index, mask in enumerate(masks):
            part = scores[index * BLOCK : (index + 1) * BLOCK] + bias
            powers = jnp.exp(part - jnp.max(part, axis=1, keepdims=True))
            probs = powers * (1.0 / jnp.sum(powers, axis=1, keepdims=True))
            outcome += matmul(probs.astype(jnp.bfloat16), values) * mask
        o_ref[:, lanes] = outcome.astype(jnp.bfloat16)


def attend_back_kernel(
    window, width, q_ref, g_ref, k_ref, v_ref, qid_ref, kid_ref, dq_ref, dk_ref, dv_ref
):
    step = pl.program_id(0)
    start = pl.multiple_of(step * BLOCK, BLOCK)
    scale = width ** (-0.5)
    masks = head_masks(width)

    @pl.when(step == 0)
    def _():
        dk_ref[...] = jnp.zeros_like(dk_ref)
        dv_ref[...] = jnp.zeros_like(dv_ref)

    near = pl.ds(start, window)
    bias = jnp.where(kid_ref[near, :] == qid_ref[...], 0.0, MASK_FILL)
    bias = jnp.concatenate([bias, bias], axis=1)
    for group in range(q_ref.shape[1] // 128):
        lanes = slice(group * 128, (group + 1) * 128)
        keys = k_ref[near, lanes]
        values = v_ref[near, lanes]
        query = q_ref[:, lanes]
        grads = g_ref[:, lanes]
        dq = jnp.zeros((BLOCK, 128), jnp.float32)
        dk = jnp.zeros((window, 128), jnp.float32)
        dv = jnp.zeros((window, 128), jnp.float32)
        for pair in range(0, len(masks), 2):
            both = masks[pair : pair + 2]
            queries = spread_heads(query, both)
            outs = spread_heads(grads, both)
            scores = mul_trans(keys, queries) * scale + bias
            powers = jnp.exp(scores - jnp.max(scores, axis=0, keepdims=True))
            probs = powers * (1.0 / jnp.sum(powers, axis=0, keepdims=True))
            prob_grad = mul_trans(values, outs)
            shared = jnp.sum(probs * prob_grad, axis=0, keepdims=True)
            score_grad = (probs * (prob_grad - shared)).astype(jnp.bfloat16)
            dv += matmul(probs.astype(jnp.bfloat16), outs)
            dk += matmul(score_grad, queries)
            part = trans_mul(score_grad, keys)
            dq += part[:BLOCK] * both[0] + part[BLOCK:] * both[1]
        dq_ref[:, lanes] = dq * scale
        dk_ref[near, lanes] += dk * scale
        dv_ref[near, lanes] += dv


def padded(cells, rows, fill=0):
    return jnp.pad(
        cells, [(0, rows - cells.shape[0])] + [(0, 0)] * (cells.ndim - 1), constant_values=fill
    )


def attend_sizes(query, keys, rim):
    steps = -(-query.shape[0] // BLOCK)
    window = BLOCK + 2 * rim if rim else keys.shape[0]
    return steps, window, (steps - 1) * BLOCK + window


def whole_spec(dims):
    return pl.BlockSpec(dims, lambda i: (0, 0))


def step_spec(columns):
    return pl.BlockSpec((BLOCK, columns), lambda i: (i, 0))


def attend(query, keys, values, query_ids, key_ids, heads, rim):
    count, columns = query.shape
    steps, window, span = attend_sizes(query, keys, rim)
    outcome = pl.pallas_call(
        functools.partial(attend_kernel, window, columns // heads),
        grid=(steps,),
        in_specs=[
            step_spec(columns),
            whole_spec((span, columns)),
            whole_spec((span, columns)),
            step_spec(1),
            whole_spec((1, span)),
        ],
        out_specs=step_spec(columns),
        out_shape=jax.ShapeDtypeStruct((steps * BLOCK, columns), jnp.bfloat16),
        compiler_params=pltpu.CompilerParams(vmem_limit_bytes=48 << 20),
        cost_estimate=pl.CostEstimate(
            flops=4 * steps * BLOCK * window * columns,
            bytes_accessed=8 * span * columns,
            transcendentals=steps * BLOCK * window * heads,
        ),
    )(
        padded(query, steps * BLOCK),
        padded(keys, span),
        padded(values, span),
        padded(query_ids, steps * BLOCK, -4)[:, None],
        padded(key_ids, span, -5)[None, :],
    )
    return outcome[:count]


def attend_back(query, keys, values, query_ids, key_ids, heads, rim, out_grad):
    count, columns = query.shape
    steps, window, span = attend_sizes(query, keys, rim)
    dq, dk, dv = pl.pallas_call(
        functools.partial(attend_back_kernel, window, columns // heads),
        grid=(steps,),
        in_specs=[
            step_spec(columns),
            step_spec(columns),
            whole_spec((span, columns)),
            whole_spec((span, columns)),
            pl.BlockSpec((1, BLOCK), lambda i: (0, i)),
            whole_spec((span, 1)),
        ],
        out_specs=[step_spec(columns), whole_spec((span, columns)), whole_spec((span, columns))],
        out_shape=[
            jax.ShapeDtypeStruct((steps * BLOCK, columns), jnp.float32),
            jax.ShapeDtypeStruct((span, columns), jnp.float32),
            jax.ShapeDtypeStruct((span, columns), jnp.float32),
        ],
        compiler_params=pltpu.CompilerParams(vmem_limit_bytes=48 << 20),
        cost_estimate=pl.CostEstimate(
            flops=10 * steps * BLOCK * window * columns,
            bytes_accessed=20 * span * columns,
            transcendentals=steps * BLOCK * window * heads,
        ),
    )(
        padded(query, steps * BLOCK),
        padded(out_grad, steps * BLOCK),
        padded(keys, span),
        padded(values, span),
        padded(query_ids, steps * BLOCK, -4)[None, :],
        padded(key_ids, span, -5)[:, None],
    )
    return dq[:count], dk[: keys.shape[0]], dv[: keys.shape[0]]


def block_forward(inputs, table, heads, rim, query_ids, key_ids, share_keys):
    gains = table["norm_g"].astype(jnp.float32)
    shifts = table["norm_b"].astype(jnp.float32)
    width = inputs.shape[1]
    normed_one = layer_norm(inputs, gains[0], shifts[0]).astype(jnp.bfloat16)
    qkv = matmul(normed_one, table["qkv_w"]).astype(jnp.bfloat16)
    query = qkv[:, :width]
    all_keys, all_values = share_keys((qkv[:, width : 2 * width], qkv[:, 2 * width :]))
    attended = attend(query, all_keys, all_values, query_ids, key_ids, heads, rim)
    mixed = inputs + (matmul(attended, table["out_w"]) + table["out_b"].astype(jnp.float32))
    normed_two = layer_norm(mixed, gains[1], shifts[1]).astype(jnp.bfloat16)
    hidden = matmul(normed_two, table["up_w"]) + table["up_b"].astype(jnp.float32)
    activated = exact_gelu(hidden).astype(jnp.bfloat16)
    result = mixed + (matmul(activated, table["down_w"]) + table["down_b"].astype(jnp.float32))
    saved = (
        inputs,
        normed_one,
        query,
        all_keys,
        all_values,
        attended,
        mixed,
        normed_two,
        hidden,
        activated,
    )
    return (result, saved)


def block_backward(grad_out, table, heads, rim, query_ids, key_ids, saved, return_keys):
    (
        inputs,
        normed_one,
        query,
        all_keys,
        all_values,
        attended,
        mixed,
        normed_two,
        hidden,
        activated,
    ) = saved
    gains = table["norm_g"].astype(jnp.float32)
    shifts = table["norm_b"].astype(jnp.float32)
    grads = {}
    pairs = {}
    down_grad = grad_out.astype(jnp.bfloat16)
    pairs["down_w"] = (activated, down_grad)
    grads["down_b"] = jnp.sum(down_grad.astype(jnp.float32), axis=0)
    act_grad = mul_trans(down_grad, table["down_w"])
    gelu_out, gelu_pull = jax.vjp(exact_gelu, hidden)
    hidden_grad = gelu_pull(act_grad)[0].astype(jnp.bfloat16)
    pairs["up_w"] = (normed_two, hidden_grad)
    grads["up_b"] = jnp.sum(hidden_grad.astype(jnp.float32), axis=0)
    mixed_part, gain_two, shift_two = norm_back(
        mixed, gains[1], shifts[1], mul_trans(hidden_grad, table["up_w"])
    )
    mixed_grad = grad_out + mixed_part
    branch_grad = mixed_grad.astype(jnp.bfloat16)
    pairs["out_w"] = (attended, branch_grad)
    grads["out_b"] = jnp.sum(branch_grad.astype(jnp.float32), axis=0)
    attended_grad = mul_trans(branch_grad, table["out_w"]).astype(jnp.bfloat16)
    query_grad, keys_grad_all, values_grad_all = attend_back(
        query, all_keys, all_values, query_ids, key_ids, heads, rim, attended_grad
    )
    keys_grad, values_grad = return_keys((keys_grad_all, values_grad_all))
    qkv_grad = jnp.concatenate([query_grad, keys_grad, values_grad], axis=1).astype(jnp.bfloat16)
    pairs["qkv_w"] = (normed_one, qkv_grad)
    input_part, gain_one, shift_one = norm_back(
        inputs, gains[0], shifts[0], mul_trans(qkv_grad, table["qkv_w"])
    )
    return (mixed_grad + input_part, grads, (gain_one, shift_one, gain_two, shift_two), pairs)


def core_side():
    return (lax.axis_index("grp") % 2).astype(jnp.int32).reshape(1)


def small_rows(table, names, rows):
    joined = jnp.concatenate([table[name].reshape(-1) for name in names])
    return jnp.pad(joined, (0, rows * 128 - joined.size)).reshape(rows // 2, 256)


def pick_half(pairs, side):
    return jnp.where(side == 0, pairs[:, :128], pairs[:, 128:])


def store_flat(target, product):
    rows, blocks = product.shape[0], product.shape[1] // 128
    for index in range(blocks):
        target[pl.ds(index, rows, stride=blocks), :] = product[:, index * 128 : (index + 1) * 128]


def column_blocks(ref, blocks):
    parts = [ref[:, pl.ds(pl.multiple_of(index * 128, 128), 128)] for index in blocks]
    return parts[0] if len(parts) == 1 else jnp.concatenate(parts, axis=1)


def steps_of(rows, size):
    return [(start, min(size, rows - start)) for start in range(0, rows, size)]


def enc_grad_kernel(sizes, side_ref, *refs):
    small_ref, out_ref, stage_ref, sems = refs[-4:]
    side = side_ref[0]
    offset = 0
    flight = [None, None]
    turn = 0

    def send(source, rows):
        nonlocal turn, offset
        copy = pltpu.make_async_copy(source, out_ref.at[pl.ds(offset, rows)], sems.at[turn % 2])
        copy.start()
        flight[turn % 2] = copy
        turn += 1
        offset += rows

    def settle():
        if flight[turn % 2] is not None:
            flight[turn % 2].wait()

    for index, size in enumerate(sizes):
        x_ref, y_ref = refs[2 * index], refs[2 * index + 1]
        blocks = y_ref.shape[1] // 256
        right = column_blocks(y_ref, [2 * block + side for block in range(blocks)])
        for start, rows in steps_of(x_ref.shape[1], size):
            settle()
            target = stage_ref.at[turn % 2]
            store_flat(target, trans_mul(x_ref[:, start : start + rows], right))
            send(target.at[pl.ds(0, rows * blocks)], rows * blocks)
    settle()
    send(small_ref, small_ref.shape[0])
    settle()
    turn += 1
    settle()


def enc_grad_half(inputs, grads, small, total_rows):
    operands = [part for pair in zip(inputs, grads) for part in pair]
    sizes = [640, 256, 384, 256, 768]
    whole = pl.BlockSpec(memory_space=pltpu.VMEM)
    return pl.pallas_call(
        functools.partial(enc_grad_kernel, sizes),
        in_specs=[pl.BlockSpec(memory_space=pltpu.SMEM)] + [whole] * (len(operands) + 1),
        out_specs=pl.BlockSpec(memory_space=pl.ANY),
        out_shape=jax.ShapeDtypeStruct((total_rows // 2, 128), jnp.float32),
        scratch_shapes=[pltpu.VMEM((2, 3072, 128), jnp.float32), pltpu.SemaphoreType.DMA((2,))],
        compiler_params=pltpu.CompilerParams(vmem_limit_bytes=40 << 20),
        cost_estimate=pl.CostEstimate(
            flops=total_rows * 128 * inputs[0].shape[0],
            bytes_accessed=total_rows * 256,
            transcendentals=0,
        ),
    )(core_side(), *operands, small)


def store_pixels(product_ref, targets):
    groups = product_ref.shape[1] // 4

    def load(row, block):
        return product_ref.at[block][pl.ds(row, groups, stride=4), :]

    def piece(row, block):
        if block < 13:
            return load(row, block)
        if block == 13:
            left, right = load(row, 13)[:, :64], load(row + 1, 0)[:, :64]
        else:
            left, right = load(row + 1, block - 14)[:, 64:], load(row + 1, block - 13)[:, :64]
        return jnp.concatenate([left, right], axis=1)

    for index in range(54):
        block = piece(0, index) if index < 27 else piece(2, index - 27)
        targets[index % 2][pl.ds(index // 2, groups, stride=27), :] = block


def dec_grad_kernel(plan, side_ref, *refs):
    small_mine, small_theirs, mine_ref, theirs_ref, stage_ref, pixel_ref, sems = refs[-7:]
    side = side_ref[0]
    flight = [None, None]
    turn = 0
    for index, (size, offset) in enumerate(plan):
        x_ref, y_ref = refs[2 * index], refs[2 * index + 1]
        pixels = y_ref.shape[1] % 256 != 0
        for start, rows in steps_of(x_ref.shape[1], size):
            product = trans_mul(x_ref[:, start : start + rows], y_ref[...])
            slot = turn % 2
            for copy in flight[slot] or ():
                copy.wait()
            if pixels:
                for block in range(14):
                    part = product[:, block * 128 : (block + 1) * 128]
                    pixel_ref[block, :, : part.shape[1]] = part
                store_pixels(pixel_ref, [stage_ref.at[slot, 0], stage_ref.at[slot, 1]])
            else:
                blocks = y_ref.shape[1] // 128
                for block in range(blocks):
                    stage_ref.at[slot, block % 2][
                        pl.ds(block // 2, rows, stride=blocks // 2), :
                    ] = product[:, block * 128 : (block + 1) * 128]
            amount = rows * y_ref.shape[1] // 256
            flight[slot] = [
                pltpu.make_async_copy(
                    stage_ref.at[slot, parity, pl.ds(0, amount)],
                    target.at[pl.ds(offset, amount)],
                    sems.at[slot, order],
                )
                for order, (parity, target) in enumerate(
                    ((side, mine_ref), (1 - side, theirs_ref))
                )
            ]
            for copy in flight[slot]:
                copy.start()
            offset += amount
            turn += 1
    rows = small_mine.shape[0]
    last = [
        pltpu.make_async_copy(
            source, target.at[pl.ds(target.shape[0] - rows, rows)], sems.at[2, order]
        )
        for order, (source, target) in enumerate(
            ((small_mine, mine_ref), (small_theirs, theirs_ref))
        )
    ]
    for copy in last:
        copy.start()
    for copy in last + flight[0] + flight[1]:
        copy.wait()


def dec_grad_halves(pairs, small_mine, small_theirs, total_rows):
    plan = [(256, 0), (256, 1536), (256, 4608), (256, 5632), (512, 9728), (512, 13824)]
    operands = [part for pair in pairs for part in pair]
    whole = pl.BlockSpec(memory_space=pltpu.VMEM)
    anywhere = pl.BlockSpec(memory_space=pl.ANY)
    shape = jax.ShapeDtypeStruct((total_rows // 2, 128), jnp.float32)
    return pl.pallas_call(
        functools.partial(dec_grad_kernel, plan),
        in_specs=[pl.BlockSpec(memory_space=pltpu.SMEM)] + [whole] * (len(operands) + 2),
        out_specs=[anywhere, anywhere],
        out_shape=[shape, shape],
        scratch_shapes=[
            pltpu.VMEM((2, 2, 3456, 128), jnp.float32),
            pltpu.VMEM((14, 512, 128), jnp.float32),
            pltpu.SemaphoreType.DMA((3, 2)),
        ],
        compiler_params=pltpu.CompilerParams(vmem_limit_bytes=56 << 20),
        cost_estimate=pl.CostEstimate(
            flops=total_rows * 256 * pairs[1][0].shape[0],
            bytes_accessed=total_rows * 512,
            transcendentals=0,
        ),
    )(core_side(), *operands, small_mine, small_theirs)


def adamw_kernel(with_average, side_ref, scalar_ref, mine_ref, theirs_ref, *refs):
    count = 4 if with_average else 3
    ins, outs, grad_ref = refs[:count], refs[count:-1], refs[-1]
    side = side_ref[0]
    rows = mine_ref.shape[0]
    grad_ref[pl.ds(side, rows, stride=2), :] = mine_ref[...]
    grad_ref[pl.ds(1 - side, rows, stride=2), :] = theirs_ref[...]
    weights = ins[0][...]
    clipped = grad_ref[...] * scalar_ref[0]
    first_new = BETA_ONE * ins[1][...] + (1.0 - BETA_ONE) * clipped
    second_new = BETA_TWO * ins[2][...] + (1.0 - BETA_TWO) * clipped * clipped
    first_hat = first_new / scalar_ref[1]
    second_hat = second_new / scalar_ref[2]
    weights_new = weights * (1.0 - LEARN_RATE * WEIGHT_DECAY) - LEARN_RATE * first_hat / (
        jnp.sqrt(second_hat) + ADAM_EPS
    )
    outs[0][...] = weights_new
    outs[1][...] = first_new
    outs[2][...] = second_new
    outs[3][...] = weights_new.astype(jnp.bfloat16)
    if with_average:
        outs[4][...] = EMA_RATE * ins[3][...] + (1.0 - EMA_RATE) * weights_new


def adamw(halves, arrays, factor, steps_done):
    rows = arrays[0].shape[0]
    steps = 1
    for count in (2, 3, 4, 6, 8):
        if rows % (count * 32) == 0:
            steps = count
    block = pl.BlockSpec((rows // steps, 128), lambda i: (i, 0))
    half = pl.BlockSpec((rows // steps // 2, 128), lambda i: (i, 0))
    scalar = pl.BlockSpec(memory_space=pltpu.SMEM)
    scalars = jnp.stack([factor, 1.0 - BETA_ONE**steps_done, 1.0 - BETA_TWO**steps_done])
    full = jax.ShapeDtypeStruct((rows, 128), jnp.float32)
    shapes = [full, full, full, jax.ShapeDtypeStruct((rows, 128), jnp.bfloat16)]
    if len(arrays) == 4:
        shapes.append(full)
    return pl.pallas_call(
        functools.partial(adamw_kernel, len(arrays) == 4),
        grid=(steps,),
        in_specs=[scalar, scalar, half, half] + [block] * len(arrays),
        out_specs=[block] * len(shapes),
        out_shape=shapes,
        scratch_shapes=[pltpu.VMEM((rows // steps, 128), jnp.float32)],
        compiler_params=pltpu.CompilerParams(vmem_limit_bytes=40 << 20),
    )(core_side(), scalars, *halves, *arrays)


def paired(block):
    return jnp.concatenate([block, swap(block, "grp", 1)], axis=0)


def per_device(
    patches,
    segments,
    visible,
    enc_params,
    enc_first,
    enc_second,
    enc_average,
    dec_params,
    dec_first,
    dec_second,
    step_count,
):
    my_index = lax.axis_index("grp")
    slot_dev = segments.shape[0]
    rim = TILE_HI
    counts = jnp.sum((segments >= 0).astype(jnp.float32)) - visible.shape[0]
    total_count = total(jnp.full((8, 128), counts))[0, 0]
    enc_copy, dec_copy = gather_both(
        enc_params.astype(jnp.bfloat16), dec_params.astype(jnp.bfloat16)
    )
    enc_table = unpack(enc_copy, enc_pieces())
    dec_table = unpack(dec_copy, dec_pieces())
    group_vis = group_rows(visible)
    group_seg = double(double(segments, 0, "grp", 2), 1, "grp", 1).reshape(-1)
    group_ids = group_seg[group_vis]
    own_ids = group_ids[: visible.shape[0]]
    key_ids = extended(segments + 3, rim) - 3
    local_slot = group_vis - my_index * slot_dev
    chosen = (
        local_slot[:, None] == jnp.arange(slot_dev, dtype=jnp.int32)[None, :]
    ).astype(jnp.bfloat16)
    seen = jnp.sum(chosen.astype(jnp.float32), axis=0) > 0.5
    enc_input = own_rows(matmul(chosen, patches).astype(jnp.bfloat16))
    enc_start = (
        matmul(enc_input, enc_table["patch_w"])
        + enc_table["patch_b"].astype(jnp.float32)
        + sincos(visible % L, D)
    )

    def enc_share(pair):
        joined = group_rows(jnp.concatenate(pair, axis=1))
        return (joined[:, :D], joined[:, D:])

    def enc_return(pair):
        joined = own_rows(jnp.concatenate(pair, axis=1))
        return (joined[:, :D], joined[:, D:])

    enc_out, enc_saved = block_forward(enc_start, enc_table, H, 0, own_ids, group_ids, enc_share)
    enc_gain = enc_table["norm_g"].astype(jnp.float32)
    enc_shift = enc_table["norm_b"].astype(jnp.float32)
    enc_final = layer_norm(enc_out, enc_gain[2], enc_shift[2]).astype(jnp.bfloat16)
    latent = (
        matmul(enc_final, dec_table["embed_w"]) + dec_table["embed_b"].astype(jnp.float32)
    ).astype(jnp.bfloat16)
    placed = trans_mul(chosen, group_rows(latent))
    positions = (my_index * slot_dev + jnp.arange(slot_dev, dtype=jnp.int32)) % L
    dec_start = jnp.where(
        seen[:, None], placed, dec_table["mask_token"].astype(jnp.float32)[None, :]
    ) + sincos(positions, E)
    counted = jnp.where((segments >= 0) & jnp.logical_not(seen), 1.0, 0.0)

    def dec_share(pair):
        joined = extended(jnp.concatenate(pair, axis=1), rim)
        return (joined[:, :E], joined[:, E:])

    def dec_return(pair):
        joined = jnp.concatenate(pair, axis=1)
        from_upper = passed_along(joined[:rim], "grp", -1)
        from_lower = passed_along(joined[rim + slot_dev :], "grp", 1)
        middle = joined[rim : rim + slot_dev]
        middle = jnp.concatenate(
            [
                middle[:rim] + from_lower,
                middle[rim : slot_dev - rim],
                middle[slot_dev - rim :] + from_upper,
            ],
            axis=0,
        )
        return (middle[:, :E], middle[:, E:])

    dec_out, dec_saved = block_forward(
        dec_start, dec_table, EH, rim, segments, key_ids, dec_share
    )
    dec_gain = dec_table["norm_g"].astype(jnp.float32)
    dec_shift = dec_table["norm_b"].astype(jnp.float32)
    dec_final = layer_norm(dec_out, dec_gain[2], dec_shift[2]).astype(jnp.bfloat16)
    predicted = matmul(dec_final, dec_table["pix_w"]) + dec_table["pix_b"].astype(jnp.float32)
    pixels = patches.astype(jnp.float32)
    centered = pixels - jnp.mean(pixels, axis=1, keepdims=True)
    target = centered * lax.rsqrt(jnp.mean(centered * centered, axis=1, keepdims=True) + NORM_EPS)
    errors = predicted - target
    loss_part = jnp.sum(counted * jnp.mean(errors * errors, axis=1))
    pred_grad = (counted[:, None] * errors * (2.0 / PATCH) / total_count).astype(jnp.bfloat16)
    dec_grads = {}
    side = core_side()[0]
    dec_grads["pix_b"] = jnp.sum(pred_grad.astype(jnp.float32), axis=0)
    dec_out_grad, dec_gain_last, dec_shift_last = norm_back(
        dec_out, dec_gain[2], dec_shift[2], mul_trans(pred_grad, dec_table["pix_w"])
    )
    start_grad, block_grads, dec_small, dec_pairs = block_backward(
        dec_out_grad, dec_table, EH, rim, segments, key_ids, dec_saved, dec_return
    )
    dec_grads.update(block_grads)
    dec_grads["norm_g"] = jnp.stack([dec_small[0], dec_small[2], dec_gain_last])
    dec_grads["norm_b"] = jnp.stack([dec_small[1], dec_small[3], dec_shift_last])
    dec_grads["mask_token"] = jnp.sum(jnp.where(seen[:, None], 0.0, start_grad), axis=0)
    latent_grad = own_rows(matmul(chosen, start_grad.astype(jnp.bfloat16)).astype(jnp.bfloat16))
    dec_grads["embed_b"] = jnp.sum(latent_grad.astype(jnp.float32), axis=0)
    dec_pairs["embed_w"] = (enc_final, latent_grad)
    dec_pairs["pix_w"] = (dec_final, pred_grad)
    dec_vectors = small_rows(
        dec_grads,
        ("embed_b", "mask_token", "out_b", "up_b", "down_b", "pix_b", "norm_g", "norm_b"),
        256,
    )
    halves = dec_grad_halves(
        [dec_pairs[name] for name in ("embed_w", "qkv_w", "out_w", "up_w", "down_w", "pix_w")],
        pick_half(dec_vectors, side),
        pick_half(dec_vectors, 1 - side),
        DR,
    )
    dec_half = halves[0] + swap(halves[1], "grp", 1)
    latent_grad, dec_half = lax.optimization_barrier((latent_grad, dec_half))
    dec_sum = reduce_stages(dec_half)
    enc_out_grad, enc_gain_last, enc_shift_last = norm_back(
        enc_out, enc_gain[2], enc_shift[2], mul_trans(latent_grad, dec_table["embed_w"])
    )
    enc_start_grad, enc_grads, enc_small, enc_pairs = block_backward(
        enc_out_grad, enc_table, H, 0, own_ids, group_ids, enc_saved, enc_return
    )
    enc_grads["norm_g"] = jnp.stack([enc_small[0], enc_small[2], enc_gain_last])
    enc_grads["norm_b"] = jnp.stack([enc_small[1], enc_small[3], enc_shift_last])
    patch_grad = enc_start_grad.astype(jnp.bfloat16)
    enc_pairs["patch_w"] = (enc_input, patch_grad)
    enc_grads["patch_b"] = jnp.sum(patch_grad.astype(jnp.float32), axis=0)
    names = ("patch_w", "qkv_w", "out_w", "up_w", "down_w")
    enc_vectors = small_rows(
        enc_grads, ("patch_b", "out_b", "up_b", "down_b", "norm_g", "norm_b"), 384
    )
    enc_half = enc_grad_half(
        [paired(enc_pairs[name][0]) for name in names],
        [paired(enc_pairs[name][1]) for name in names],
        pick_half(enc_vectors, side) + swap(pick_half(enc_vectors, 1 - side), "grp", 1),
        ER,
    )
    enc_sum = reduce_stages(enc_half)
    squares = sum(jnp.sum(part * part) for part in enc_sum + dec_sum)
    lane = lax.broadcasted_iota(jnp.int32, (8, 128), 1)
    sums = total(jnp.where(lane == 0, squares, jnp.where(lane == 1, loss_part, 0.0)))
    loss_total = sums[0, 1]
    grad_norm = jnp.sqrt(sums[0, 0])
    factor = jnp.minimum(1.0, CLIP_LIMIT / (grad_norm + NORM_EPS))
    steps_done = step_count[0].astype(jnp.float32)
    enc_new, enc_first_new, enc_second_new, enc_copy_new, average_new = adamw(
        spread_pieces(enc_sum), (enc_params, enc_first, enc_second, enc_average), factor, steps_done
    )
    dec_new, dec_first_new, dec_second_new, dec_copy_new = adamw(
        spread_pieces(dec_sum), (dec_params, dec_first, dec_second), factor, steps_done
    )
    return (
        enc_new,
        enc_first_new,
        enc_second_new,
        enc_copy_new,
        dec_new,
        dec_first_new,
        dec_second_new,
        dec_copy_new,
        average_new,
        grad_norm,
        loss_total,
        total_count,
    )


def solution(mesh):
    placed = (
        P(("dp", "grp"), None),
        P(("dp", "grp")),
        P(("dp", "grp")),
        P("dp", None),
        P("dp", None),
        P("dp", None),
        P("dp", None),
        P("dp", None),
        P("dp", None),
        P("dp", None),
        P(),
    )
    return jax.shard_map(
        per_device,
        mesh=mesh,
        in_specs=placed,
        out_specs=(
            P("dp", None),
            P("dp", None),
            P("dp", None),
            P("dp", None),
            P("dp", None),
            P("dp", None),
            P("dp", None),
            P("dp", None),
            P("dp", None),
            P(),
            P(),
            P(),
        ),
        check_vma=False,
    )
```

```python
import functools
import math

import jax
import jax.numpy as jnp
from jax import lax
from jax.experimental import pallas as pl
from jax.experimental.pallas import tpu as pltpu
from jax.sharding import PartitionSpec as P

D = 768
H = 12
F = 3072
E = 512
EH = 16
FE = 2048
PATCH = 1728
L = 1728
TILE_HI = 192
ER = 66048
DR = 34816


NORM_EPS = 1e-06
MASK_FILL = -1e30
CLIP_LIMIT = 0.0002
LEARN_RATE = 0.02
BETA_ONE = 0.5
BETA_TWO = 0.5
ADAM_EPS = 1e-08
WEIGHT_DECAY = 0.05
EMA_RATE = 0.9


def swap(block, axis, bit):
    count = lax.axis_size(axis)
    return lax.ppermute(block, axis, [(i, i ^ bit) for i in range(count)])


def bit_of(axis, bit):
    return (lax.axis_index(axis) // bit) % 2


def double(block, dim, axis, bit):
    mine = bit_of(axis, bit)
    other = swap(block, axis, bit)
    first = jnp.where(mine == 0, block, other)
    second = jnp.where(mine == 0, other, block)
    return jnp.stack([first, second], axis=dim)


def total(values):
    for axis in ("grp", "dp"):
        bit = 1
        while bit < lax.axis_size(axis):
            values = values + swap(values, axis, bit)
            bit *= 2
    return values


def dp_bits():
    bits = [1]
    while bits[-1] * 2 < lax.axis_size("dp"):
        bits.append(bits[-1] * 2)
    return bits


def cut(rows, shares):
    unit = 16 if rows % 16 == 0 else 2
    sizes = [int(round(rows // unit * share)) * unit for share in shares]
    return sizes + [rows - sum(sizes)]


def gather_quarters(shard):
    part = shard.shape[0] // 4
    quarter = lax.dynamic_slice_in_dim(shard, lax.axis_index("grp") * part, part, 0)
    return lax.all_gather(quarter, ("dp", "grp"), axis=0, tiled=True)


def gather_both(enc_shard, dec_shard):
    enc_copy = gather_quarters(enc_shard)
    enc_copy, dec_shard = lax.optimization_barrier((enc_copy, dec_shard))
    return enc_copy, gather_quarters(dec_shard)


def section(cells, dim, start, size):
    return lax.dynamic_slice_in_dim(cells, start, size, dim)


def reduce_bit(cells, dim, axis, bit, start=0, size=None):
    half = (cells.shape[dim] if size is None else size) // 2
    mine = bit_of(axis, bit)
    sent = section(cells, dim, start + (1 - mine) * half, half)
    return section(cells, dim, start + mine * half, half) + swap(sent, axis, bit)


def dec_routes():
    bits = [("dp", bit) for bit in dp_bits()]
    return [bits[:1] + [("grp", 2)] + bits[1:], bits[1:2] + [("grp", 2)] + bits[2:] + bits[:1]]


def reduce_first(half, routes, shares):
    shards = lax.axis_size("dp")
    half_rows = half.shape[0] // shards
    bits = dp_bits()
    names = [("dp", bit) for bit in reversed(bits)]
    cells = half.reshape([2] * len(bits) + [half_rows, 128])
    blocks = []
    start = 0
    for route, rows in zip(routes, cut(half_rows, shares)):
        axis, bit = route[0]
        if axis == "grp":
            block = reduce_bit(cells, len(bits), axis, bit, start, rows)
        else:
            dim = names.index(route[0])
            mine = bit_of(axis, bit)

            def pick(index, dim=dim, start=start, rows=rows):
                corner = [0] * dim + [index] + [0] * (len(bits) - dim - 1) + [start, 0]
                sizes = [2] * dim + [1] + [2] * (len(bits) - dim - 1) + [rows, 128]
                return lax.dynamic_slice(cells, corner, sizes)

            block = pick(mine) + swap(pick(1 - mine), axis, bit)
        blocks.append(block)
        start += rows
    return blocks


def reduce_rest(blocks, routes):
    bits = dp_bits()
    names = [("dp", bit) for bit in reversed(bits)]
    blocks = list(blocks)
    for step in range(1, len(routes[0])):
        for index, route in enumerate(routes):
            axis, bit = route[step]
            dim = len(bits) if axis == "grp" else names.index(route[step])
            blocks[index] = reduce_bit(blocks[index], dim, axis, bit)
    return [block.reshape(-1, 128) for block in blocks]


def dp_routes():
    bits = [("dp", bit) for bit in dp_bits()]
    return [bits, bits[1:] + bits[:1]]


def spread_pieces(pieces):
    wide = [double(piece, 0, "grp", 2).reshape(-1, 128) for piece in pieces]
    mine = jnp.concatenate(wide, axis=0)
    return mine, swap(mine, "grp", 1)


def group_rows(block):
    across = swap(block, "grp", 2)
    near, far = (
        swap(block, "grp", 1),
        swap(across, "grp", 1),
    )
    return jnp.concatenate([block, near, across, far], axis=0)


def own_rows(blocks):
    count = blocks.shape[0] // 4
    parts = [lax.slice_in_dim(blocks, i * count, (i + 1) * count, axis=0) for i in range(4)]
    sent = jnp.concatenate([parts[1], parts[3]], axis=0)
    arrived = swap(sent, "grp", 1)
    kept = parts[0] + arrived[:count]
    other = parts[2] + arrived[count:]
    return kept + swap(other, "grp", 2)


def extended(cells, width):
    count = lax.axis_size("grp")
    ends = count - 1
    head = cells[:width]
    tail = cells[cells.shape[0] - width :]
    return jnp.concatenate(
        [
            lax.ppermute(tail, "grp", [(i, i + 1) for i in range(ends)]),
            cells,
            lax.ppermute(head, "grp", [(i + 1, i) for i in range(ends)]),
        ],
        axis=0,
    )


def passed_along(block, axis, distance):
    devices = range(lax.axis_size(axis))
    route = [(i - distance, i) for i in devices if i - distance in devices]
    return lax.ppermute(block, axis, route)


def enc_pieces():
    return [
        ("patch_w", (PATCH, D)),
        ("qkv_w", (D, 3 * D)),
        ("out_w", (D, D)),
        ("up_w", (D, F)),
        ("down_w", (F, D)),
        ("patch_b", (D,)),
        ("out_b", (D,)),
        ("up_b", (F,)),
        ("down_b", (D,)),
        ("norm_g", (3, D)),
        ("norm_b", (3, D)),
    ]


def dec_pieces():
    return [
        ("embed_w", (D, E)),
        ("qkv_w", (E, 3 * E)),
        ("out_w", (E, E)),
        ("up_w", (E, FE)),
        ("down_w", (FE, E)),
        ("pix_w", (E, PATCH)),
        ("embed_b", (E,)),
        ("mask_token", (E,)),
        ("out_b", (E,)),
        ("up_b", (FE,)),
        ("down_b", (E,)),
        ("pix_b", (PATCH,)),
        ("norm_g", (3, E)),
        ("norm_b", (3, E)),
    ]


def relayout_kernel(plan, *refs):
    source, outs = refs[0], refs[1 : 1 + len(plan)]
    raw_ref, wide_ref, stages, in_sems, out_sems = (
        refs[1 + len(plan)],
        refs[2 + len(plan)],
        refs[3 + len(plan) : -2],
        refs[-2],
        refs[-1],
    )
    steps = [
        (index, offset + start * blocks, start, rows, blocks)
        for index, (offset, depth, blocks, rows) in enumerate(plan)
        for start in range(0, depth, rows)
    ]

    def fetch(turn):
        _, offset, _, rows, blocks = steps[turn]
        return pltpu.make_async_copy(
            source.at[pl.ds(offset, rows * blocks)],
            raw_ref.at[turn % 2, pl.ds(0, rows * blocks)],
            in_sems.at[turn % 2],
        )

    flight = {}
    fetch(0).start()
    for turn, (index, _, start, rows, blocks) in enumerate(steps):
        if turn + 1 < len(steps):
            fetch(turn + 1).start()
        fetch(turn).wait()
        wide_ref[: rows * blocks, :] = raw_ref[turn % 2, : rows * blocks, :].astype(jnp.float32)
        slot = turn % 2
        if slot in flight:
            flight.pop(slot).wait()
        stage = stages[index].at[slot]
        for block in range(blocks):
            stage[:, block * 128 : (block + 1) * 128] = wide_ref[
                pl.ds(block, rows, stride=blocks), :
            ].astype(jnp.bfloat16)
        flight[slot] = pltpu.make_async_copy(
            stage, outs[index].at[pl.ds(start, rows)], out_sems.at[slot]
        )
        flight[slot].start()
    for copy in flight.values():
        copy.wait()


def relayout(rows, plan):
    anywhere = pl.BlockSpec(memory_space=pl.ANY)
    most = max(step * blocks for _, _, blocks, step in plan)
    return pl.pallas_call(
        functools.partial(relayout_kernel, plan),
        in_specs=[anywhere],
        out_specs=[anywhere] * len(plan),
        out_shape=[
            jax.ShapeDtypeStruct((depth, blocks * 128), jnp.bfloat16)
            for _, depth, blocks, _ in plan
        ],
        scratch_shapes=[
            pltpu.VMEM((2, most, 128), jnp.bfloat16),
            pltpu.VMEM((most, 128), jnp.float32),
        ]
        + [pltpu.VMEM((2, step, blocks * 128), jnp.bfloat16) for _, _, blocks, step in plan]
        + [pltpu.SemaphoreType.DMA((2,)), pltpu.SemaphoreType.DMA((2,))],
        compiler_params=pltpu.CompilerParams(vmem_limit_bytes=40 << 20),
        cost_estimate=pl.CostEstimate(
            flops=0, bytes_accessed=rows.size * 4, transcendentals=0
        ),
    )(rows)


ENC_STEPS = {"patch_w": 576, "qkv_w": 192, "out_w": 384, "up_w": 128, "down_w": 512}
DEC_STEPS = {"embed_w": 768, "qkv_w": 256, "out_w": 512, "up_w": 128, "down_w": 512}


def unpack(rows, pieces, steps):
    table = {}
    offset = 0
    plan = []
    vectors = sum(1 for _, dims in pieces if len(dims) == 2 and dims[0] > 3)
    for piece_name, piece_dims in pieces[:vectors]:
        amount = math.prod(piece_dims) // 128
        if piece_name in steps:
            plan.append((offset, piece_dims[0], piece_dims[1] // 128, steps[piece_name]))
        else:
            table[piece_name] = rows[offset : offset + amount].reshape(piece_dims)
        offset += amount
    small = rows[offset:].reshape(-1)
    table.update(zip(steps, relayout(rows, plan)))
    offset = 0
    for piece_name, piece_dims in pieces[vectors:]:
        amount = math.prod(piece_dims)
        table[piece_name] = small[offset : offset + amount].reshape(piece_dims)
        offset += amount
    return table


def matmul(left, right):
    return jnp.dot(left, right, preferred_element_type=jnp.float32)


def mul_trans(left, right):
    return lax.dot_general(
        left, right, (((1,), (1,)), ((), ())), preferred_element_type=jnp.float32
    )


def trans_mul(left, right):
    return lax.dot_general(
        left, right, (((0,), (0,)), ((), ())), preferred_element_type=jnp.float32
    )


def sincos(positions, width):
    half_width = width // 2
    freq_row = jnp.exp(
        jnp.arange(half_width, dtype=jnp.float32) * (-2.0 * math.log(10000.0) / width)
    )
    angles = positions.astype(jnp.float32)[:, None] * freq_row[None, :]
    return jnp.concatenate([jnp.sin(angles), jnp.cos(angles)], axis=1)


def layer_norm(inputs, gain, shift):
    center = inputs - jnp.mean(inputs, axis=-1, keepdims=True)
    return (
        center * lax.rsqrt(jnp.mean(center * center, axis=-1, keepdims=True) + NORM_EPS) * gain
        + shift
    )


def norm_back(inputs, gain, shift, grad_out):
    outputs, pull = jax.vjp(layer_norm, inputs, gain, shift)
    return pull(grad_out)


def exact_gelu(values):
    return jax.nn.gelu(values, approximate=False)


BLOCK = 128


def head_masks(width):
    lanes = lax.broadcasted_iota(jnp.int32, (1, 128), 1) // width
    return [(lanes == index).astype(jnp.float32) for index in range(128 // width)]


def spread_heads(cells, masks):
    wide = cells.astype(jnp.float32)
    return jnp.concatenate([(wide * mask).astype(jnp.bfloat16) for mask in masks], axis=0)


TILE = 32
TALL = 64


def attend_kernel(
    window, width, q_ref, k_ref, v_ref, qid_ref, kid_ref, o_ref, bias_ref, score_ref, prob_ref
):
    start = pl.multiple_of(pl.program_id(0) * BLOCK, BLOCK)
    scale = width ** (-0.5)
    masks = head_masks(width)
    near = pl.ds(start, window)
    bias_ref[...] = jnp.where(qid_ref[...] == kid_ref[:, near], 0.0, MASK_FILL)
    for group in range(q_ref.shape[1] // 128):
        lanes = slice(group * 128, (group + 1) * 128)
        slot = group % 2
        score_ref[slot] = mul_trans(spread_heads(q_ref[:, lanes], masks), k_ref[near, lanes])
        for first in range(0, len(masks) * BLOCK, TILE):
            rows = slice(first, first + TILE)
            row = first % BLOCK
            part = score_ref[slot, rows, :] * scale + bias_ref[row : row + TILE, :]
            powers = jnp.exp(part - jnp.max(part, axis=1, keepdims=True))
            probs = powers * (1.0 / jnp.sum(powers, axis=1, keepdims=True))
            prob_ref[slot, rows, :] = probs.astype(jnp.bfloat16)
        wide = matmul(prob_ref[slot], v_ref[near, lanes])
        o_ref[:, lanes] = pick_heads(wide, masks).astype(jnp.bfloat16)


def pick_heads(wide, masks):
    return sum(wide[i * BLOCK : (i + 1) * BLOCK] * mask for i, mask in enumerate(masks))


def row_sums(cells, merge):
    return merge(cells.reshape(-1, 8, cells.shape[1]), axis=0)


def attend_back_kernel(window, width, *refs):
    q_ref, g_ref, k_ref, v_ref, qid_ref, kid_ref, dq_ref, dk_ref, dv_ref = refs[:9]
    bias_ref, score_ref, grad_ref, prob_ref, back_ref = refs[9:]
    step = pl.program_id(0)
    start = pl.multiple_of(step * BLOCK, BLOCK)
    scale = width ** (-0.5)
    masks = head_masks(width)

    @pl.when(step == 0)
    def _():
        dk_ref[...] = jnp.zeros_like(dk_ref)
        dv_ref[...] = jnp.zeros_like(dv_ref)

    near = pl.ds(start, window)
    bias_ref[...] = jnp.where(kid_ref[near, :] == qid_ref[...], 0.0, MASK_FILL)
    tiles = [slice(first, first + TALL) for first in range(0, window, TALL)]
    for group in range(q_ref.shape[1] // 128):
        lanes = slice(group * 128, (group + 1) * 128)
        slot = group % 2
        keys = k_ref[near, lanes]
        queries = spread_heads(q_ref[:, lanes], masks)
        outs = spread_heads(g_ref[:, lanes], masks)
        score_ref[slot] = mul_trans(keys, queries)
        grad_ref[slot] = mul_trans(v_ref[near, lanes], outs)
        for index in range(len(masks)):
            head = slice(index * BLOCK, (index + 1) * BLOCK)
            top = None
            for tile in tiles:
                part = score_ref[slot, tile, head] * scale + bias_ref[tile, :]
                score_ref[slot, tile, head] = part
                most = row_sums(part, jnp.max)
                top = most if top is None else jnp.maximum(top, most)
            top = jnp.max(top, axis=0, keepdims=True)
            whole = jnp.zeros((8, BLOCK), jnp.float32)
            for tile in tiles:
                powers = jnp.exp(score_ref[slot, tile, head] - top)
                score_ref[slot, tile, head] = powers
                whole += row_sums(powers, jnp.sum)
            inverse = 1.0 / jnp.sum(whole, axis=0, keepdims=True)
            shared = jnp.zeros((8, BLOCK), jnp.float32)
            for tile in tiles:
                probs = score_ref[slot, tile, head] * inverse
                prob_ref[slot, tile, head] = probs.astype(jnp.bfloat16)
                shared += row_sums(probs * grad_ref[slot, tile, head], jnp.sum)
            shared = jnp.sum(shared, axis=0, keepdims=True)
            for tile in tiles:
                probs = score_ref[slot, tile, head] * inverse
                back_ref[slot, tile, head] = (
                    probs * (grad_ref[slot, tile, head] - shared)
                ).astype(jnp.bfloat16)
        back = back_ref[slot]
        dv_ref[near, lanes] += matmul(prob_ref[slot], outs)
        dk_ref[near, lanes] += matmul(back, queries) * scale
        dq_ref[:, lanes] = pick_heads(trans_mul(back, keys), masks) * scale


def padded(cells, rows, fill=0):
    return jnp.pad(
        cells, [(0, rows - cells.shape[0])] + [(0, 0)] * (cells.ndim - 1), constant_values=fill
    )


def attend_sizes(query, keys, rim):
    steps = -(-query.shape[0] // BLOCK)
    window = BLOCK + 2 * rim if rim else keys.shape[0]
    return steps, window, (steps - 1) * BLOCK + window


def whole_spec(dims):
    return pl.BlockSpec(dims, lambda i: (0, 0))


def step_spec(columns):
    return pl.BlockSpec((BLOCK, columns), lambda i: (i, 0))


def attend(query, keys, values, query_ids, key_ids, heads, rim):
    count, columns = query.shape
    steps, window, span = attend_sizes(query, keys, rim)
    stack = 128 * heads // columns * BLOCK
    outcome = pl.pallas_call(
        functools.partial(attend_kernel, window, columns // heads),
        grid=(steps,),
        in_specs=[
            step_spec(columns),
            whole_spec((span, columns)),
            whole_spec((span, columns)),
            step_spec(1),
            whole_spec((1, span)),
        ],
        out_specs=step_spec(columns),
        out_shape=jax.ShapeDtypeStruct((steps * BLOCK, columns), jnp.bfloat16),
        scratch_shapes=[
            pltpu.VMEM((BLOCK, window), jnp.float32),
            pltpu.VMEM((2, stack, window), jnp.float32),
            pltpu.VMEM((2, stack, window), jnp.bfloat16),
        ],
        compiler_params=pltpu.CompilerParams(vmem_limit_bytes=48 << 20),
        cost_estimate=pl.CostEstimate(
            flops=4 * steps * BLOCK * window * columns,
            bytes_accessed=8 * span * columns,
            transcendentals=steps * BLOCK * window * heads,
        ),
    )(
        padded(query, steps * BLOCK),
        padded(keys, span),
        padded(values, span),
        padded(query_ids, steps * BLOCK, -4)[:, None],
        padded(key_ids, span, -5)[None, :],
    )
    return outcome[:count]


def attend_back(query, keys, values, query_ids, key_ids, heads, rim, out_grad):
    count, columns = query.shape
    steps, window, span = attend_sizes(query, keys, rim)
    stack = 128 * heads // columns * BLOCK
    dq, dk, dv = pl.pallas_call(
        functools.partial(attend_back_kernel, window, columns // heads),
        grid=(steps,),
        in_specs=[
            step_spec(columns),
            step_spec(columns),
            whole_spec((span, columns)),
            whole_spec((span, columns)),
            pl.BlockSpec((1, BLOCK), lambda i: (0, i)),
            whole_spec((span, 1)),
        ],
        out_specs=[step_spec(columns), whole_spec((span, columns)), whole_spec((span, columns))],
        out_shape=[
            jax.ShapeDtypeStruct((steps * BLOCK, columns), jnp.float32),
            jax.ShapeDtypeStruct((span, columns), jnp.float32),
            jax.ShapeDtypeStruct((span, columns), jnp.float32),
        ],
        scratch_shapes=[
            pltpu.VMEM((window, BLOCK), jnp.float32),
            pltpu.VMEM((2, window, stack), jnp.float32),
            pltpu.VMEM((2, window, stack), jnp.float32),
            pltpu.VMEM((2, window, stack), jnp.bfloat16),
            pltpu.VMEM((2, window, stack), jnp.bfloat16),
        ],
        compiler_params=pltpu.CompilerParams(vmem_limit_bytes=48 << 20),
        cost_estimate=pl.CostEstimate(
            flops=10 * steps * BLOCK * window * columns,
            bytes_accessed=20 * span * columns,
            transcendentals=steps * BLOCK * window * heads,
        ),
    )(
        padded(query, steps * BLOCK),
        padded(out_grad, steps * BLOCK),
        padded(keys, span),
        padded(values, span),
        padded(query_ids, steps * BLOCK, -4)[None, :],
        padded(key_ids, span, -5)[:, None],
    )
    return dq[:count], dk[: keys.shape[0]], dv[: keys.shape[0]]


def gelu_pair(hidden):
    below = 0.5 * (1.0 + lax.erf(hidden * math.sqrt(0.5)))
    bell = jnp.exp(-0.5 * hidden * hidden) * (1.0 / math.sqrt(2.0 * math.pi))
    return lax.optimization_barrier(
        ((hidden * below).astype(jnp.bfloat16), below + hidden * bell)
    )


def block_forward(inputs, table, heads, rim, query_ids, key_ids, share_keys):
    gains = table["norm_g"].astype(jnp.float32)
    shifts = table["norm_b"].astype(jnp.float32)
    width = inputs.shape[1]
    normed_one = layer_norm(inputs, gains[0], shifts[0]).astype(jnp.bfloat16)
    qkv = matmul(normed_one, table["qkv_w"]).astype(jnp.bfloat16)
    query = qkv[:, :width]
    all_keys, all_values = share_keys((qkv[:, width : 2 * width], qkv[:, 2 * width :]))
    attended = attend(query, all_keys, all_values, query_ids, key_ids, heads, rim)
    mixed = inputs + (matmul(attended, table["out_w"]) + table["out_b"].astype(jnp.float32))
    normed_two = layer_norm(mixed, gains[1], shifts[1]).astype(jnp.bfloat16)
    hidden = matmul(normed_two, table["up_w"]) + table["up_b"].astype(jnp.float32)
    activated, slope = gelu_pair(hidden)
    result = mixed + (matmul(activated, table["down_w"]) + table["down_b"].astype(jnp.float32))
    saved = (
        inputs,
        normed_one,
        query,
        all_keys,
        all_values,
        attended,
        mixed,
        normed_two,
        slope,
        activated,
    )
    return (result, saved)


def block_backward(
    grad_out, table, heads, rim, query_ids, key_ids, saved, return_keys, pause
):
    (
        inputs,
        normed_one,
        query,
        all_keys,
        all_values,
        attended,
        mixed,
        normed_two,
        slope,
        activated,
    ) = saved
    gains = table["norm_g"].astype(jnp.float32)
    shifts = table["norm_b"].astype(jnp.float32)
    pairs = {}
    down_grad = grad_out.astype(jnp.bfloat16)
    pairs["down_w"] = (activated, down_grad)
    act_grad = mul_trans(down_grad, table["down_w"])
    hidden_grad = (act_grad * slope).astype(jnp.bfloat16)
    pairs["up_w"] = (normed_two, hidden_grad)
    hidden_grad = pause(hidden_grad)
    mixed_part, gain_two, shift_two = norm_back(
        mixed, gains[1], shifts[1], mul_trans(hidden_grad, table["up_w"])
    )
    mixed_grad = grad_out + mixed_part
    branch_grad = mixed_grad.astype(jnp.bfloat16)
    pairs["out_w"] = (attended, branch_grad)
    attended_grad = mul_trans(branch_grad, table["out_w"]).astype(jnp.bfloat16)
    query_grad, keys_grad_all, values_grad_all = attend_back(
        query, all_keys, all_values, query_ids, key_ids, heads, rim, attended_grad
    )
    keys_grad, values_grad = return_keys((keys_grad_all, values_grad_all))
    qkv_grad = jnp.concatenate([query_grad, keys_grad, values_grad], axis=1).astype(jnp.bfloat16)
    pairs["qkv_w"] = (normed_one, qkv_grad)
    input_part, gain_one, shift_one = norm_back(
        inputs, gains[0], shifts[0], mul_trans(qkv_grad, table["qkv_w"])
    )
    return (mixed_grad + input_part, (gain_one, shift_one, gain_two, shift_two), pairs)


def core_side():
    return (lax.axis_index("grp") % 2).astype(jnp.int32).reshape(1)


def store_vector(target, first, lane, vector):
    width = vector.shape[1]
    done = 0
    while done < width:
        size = min(128 - lane, width - done)
        target[first : first + 1, lane : lane + size] = vector[:, done : done + size]
        done += size
        lane += size
        first, lane = first + lane // 128, lane % 128
    return first, lane


def column_sums(ref):
    return jnp.sum(ref[...].astype(jnp.float32), axis=0, keepdims=True)


def store_flat(target, product):
    rows, blocks = product.shape[0], product.shape[1] // 128
    for index in range(blocks):
        target[pl.ds(index, rows, stride=blocks), :] = product[:, index * 128 : (index + 1) * 128]


def column_blocks(ref, blocks):
    parts = [ref[:, pl.ds(pl.multiple_of(index * 128, 128), 128)] for index in blocks]
    return parts[0] if len(parts) == 1 else jnp.concatenate(parts, axis=1)


def steps_of(rows, size):
    return [(start, min(size, rows - start)) for start in range(0, rows, size)]


def enc_grad_kernel(sizes, places, place_ref, x_ref, *refs):
    norm_ref, out_ref, stage_ref, product_ref, small_ref, quarter_ref, sems = refs[-7:]
    side, far = place_ref[0], place_ref[1]
    offset = 0
    flight = [None, None]
    turn = 0

    def settle():
        if flight[turn % 2] is not None:
            flight[turn % 2].wait()

    for index, size in enumerate(sizes):
        y_ref = refs[index]
        blocks = y_ref.shape[1] // 256
        first, depth = places[index]
        if blocks % 2:
            columns = [2 * block + side for block in range(blocks)]
        else:
            columns = [4 * block + 2 * far + side for block in range(blocks // 2)]
        right = column_blocks(y_ref, columns)
        for start, rows in steps_of(depth, size):
            settle()
            target = stage_ref.at[turn % 2]
            product = trans_mul(x_ref[:, first + start : first + start + rows], right)
            if blocks % 2 == 0:
                store_flat(target, product)
            else:
                for block in range(blocks):
                    product_ref[block, :rows] = product[:, block * 128 : (block + 1) * 128]
                    odd = (far + block) % 2
                    target[
                        pl.ds((odd * blocks + block - far) // 2, rows // 2, stride=blocks), :
                    ] = product_ref.at[block][pl.ds(odd, rows // 2, stride=2), :]
            amount = rows * blocks // 2
            copy = pltpu.make_async_copy(
                target.at[pl.ds(0, amount)], out_ref.at[pl.ds(offset, amount)], sems.at[turn % 2]
            )
            copy.start()
            flight[turn % 2] = copy
            turn += 1
            offset += amount
    small_ref[...] = jnp.zeros_like(small_ref)
    spot = 0, 0
    for index in (0, 2, 3, 4):
        spot = store_vector(small_ref, *spot, column_sums(refs[index]))
    rows = norm_ref.shape[0] // 4
    norms = sum(norm_ref[index * rows : (index + 1) * rows] for index in range(4))
    for index in range(rows):
        spot = store_vector(small_ref, *spot, norms[index : index + 1])
    rows = quarter_ref.shape[0]
    quarter_ref[...] = small_ref[pl.ds(side + 2 * far, rows, stride=4), :]
    last = pltpu.make_async_copy(quarter_ref, out_ref.at[pl.ds(offset, rows)], sems.at[2])
    last.start()
    for copy in [last] + flight:
        copy.wait()


def member_place():
    place = lax.axis_index("grp").astype(jnp.int32)
    return jnp.stack([place % 2, place // 2])


def enc_grad_quarter(inputs, places, grads, norms, total_rows):
    sizes = [640, 256, 384, 256, 768]
    whole = pl.BlockSpec(memory_space=pltpu.VMEM)
    return pl.pallas_call(
        functools.partial(enc_grad_kernel, sizes, places),
        in_specs=[pl.BlockSpec(memory_space=pltpu.SMEM)] + [whole] * (len(grads) + 2),
        out_specs=pl.BlockSpec(memory_space=pl.ANY),
        out_shape=jax.ShapeDtypeStruct((total_rows // 4, 128), jnp.float32),
        scratch_shapes=[
            pltpu.VMEM((2, 1536, 128), jnp.float32),
            pltpu.VMEM((9, 768, 128), jnp.float32),
            pltpu.VMEM((384, 128), jnp.float32),
            pltpu.VMEM((96, 128), jnp.float32),
            pltpu.SemaphoreType.DMA((3,)),
        ],
        compiler_params=pltpu.CompilerParams(vmem_limit_bytes=48 << 20),
        cost_estimate=pl.CostEstimate(
            flops=total_rows * 128 * inputs.shape[0],
            bytes_accessed=total_rows * 128,
            transcendentals=0,
        ),
    )(member_place(), inputs, *grads, norms)


def store_pixels(product_ref, targets):
    groups = product_ref.shape[1] // 4

    def load(row, block):
        return product_ref.at[block][pl.ds(row, groups, stride=4), :]

    def piece(row, block):
        if block < 13:
            return load(row, block)
        if block == 13:
            left, right = load(row, 13)[:, :64], load(row + 1, 0)[:, :64]
        else:
            left, right = load(row + 1, block - 14)[:, 64:], load(row + 1, block - 13)[:, :64]
        return jnp.concatenate([left, right], axis=1)

    for index in range(54):
        block = piece(0, index) if index < 27 else piece(2, index - 27)
        targets[index % 2][pl.ds(index // 2, groups, stride=27), :] = block


def dec_grad_kernel(plan, side_ref, *refs):
    norm_ref, mine_ref, theirs_ref, stage_ref, pixel_ref, small_ref, halves_ref, sems = refs[-8:]
    side = side_ref[0]
    flight = [None, None]
    turn = 0
    for index, (size, offset) in enumerate(plan):
        x_ref, y_ref = refs[2 * index], refs[2 * index + 1]
        pixels = y_ref.shape[1] % 256 != 0
        for start, rows in steps_of(x_ref.shape[1], size):
            product = trans_mul(x_ref[:, start : start + rows], y_ref[...])
            slot = turn % 2
            for copy in flight[slot] or ():
                copy.wait()
            if pixels:
                for block in range(14):
                    part = product[:, block * 128 : (block + 1) * 128]
                    pixel_ref[block, :, : part.shape[1]] = part
                store_pixels(pixel_ref, [stage_ref.at[slot, 0], stage_ref.at[slot, 1]])
            else:
                blocks = y_ref.shape[1] // 128
                for block in range(blocks):
                    stage_ref.at[slot, block % 2][
                        pl.ds(block // 2, rows, stride=blocks // 2), :
                    ] = product[:, block * 128 : (block + 1) * 128]
            amount = rows * y_ref.shape[1] // 256
            flight[slot] = [
                pltpu.make_async_copy(
                    stage_ref.at[slot, parity, pl.ds(0, amount)],
                    target.at[pl.ds(offset, amount)],
                    sems.at[slot, order],
                )
                for order, (parity, target) in enumerate(
                    ((side, mine_ref), (1 - side, theirs_ref))
                )
            ]
            for copy in flight[slot]:
                copy.start()
            offset += amount
            turn += 1
    small_ref[...] = jnp.zeros_like(small_ref)
    spot = store_vector(small_ref, 0, 0, column_sums(refs[1]))
    spot = store_vector(small_ref, *spot, norm_ref[0:1])
    for index in (2, 3, 4, 5):
        spot = store_vector(small_ref, *spot, column_sums(refs[2 * index + 1]))
    for index in range(1, norm_ref.shape[0]):
        spot = store_vector(small_ref, *spot, norm_ref[index : index + 1])
    rows = halves_ref.shape[1]
    for parity in range(2):
        halves_ref[parity] = small_ref[pl.ds(parity, rows, stride=2), :]
    last = [
        pltpu.make_async_copy(
            halves_ref.at[parity], target.at[pl.ds(target.shape[0] - rows, rows)], sems.at[2, order]
        )
        for order, (parity, target) in enumerate(((side, mine_ref), (1 - side, theirs_ref)))
    ]
    for copy in last:
        copy.start()
    for copy in last + flight[0] + flight[1]:
        copy.wait()


def dec_grad_halves(pairs, norms, total_rows):
    plan = [(256, 0), (256, 1536), (256, 4608), (256, 5632), (512, 9728), (512, 13824)]
    operands = [part for pair in pairs for part in pair]
    whole = pl.BlockSpec(memory_space=pltpu.VMEM)
    anywhere = pl.BlockSpec(memory_space=pl.ANY)
    shape = jax.ShapeDtypeStruct((total_rows // 2, 128), jnp.float32)
    return pl.pallas_call(
        functools.partial(dec_grad_kernel, plan),
        in_specs=[pl.BlockSpec(memory_space=pltpu.SMEM)] + [whole] * (len(operands) + 1),
        out_specs=[anywhere, anywhere],
        out_shape=[shape, shape],
        scratch_shapes=[
            pltpu.VMEM((2, 2, 3456, 128), jnp.float32),
            pltpu.VMEM((14, 512, 128), jnp.float32),
            pltpu.VMEM((256, 128), jnp.float32),
            pltpu.VMEM((2, 128, 128), jnp.float32),
            pltpu.SemaphoreType.DMA((3, 2)),
        ],
        compiler_params=pltpu.CompilerParams(vmem_limit_bytes=56 << 20),
        cost_estimate=pl.CostEstimate(
            flops=total_rows * 256 * pairs[1][0].shape[0],
            bytes_accessed=total_rows * 512,
            transcendentals=0,
        ),
    )(core_side(), *operands, norms)


def adamw_kernel(parts, with_average, place_ref, scalar_ref, *refs):
    count = 4 if with_average else 3
    ins, outs, grad_ref = refs[parts : parts + count], refs[parts + count : -1], refs[-1]
    for index in range(parts):
        rows = refs[index].shape[0]
        grad_ref[pl.ds(place_ref[index], rows, stride=parts), :] = refs[index][...]
    weights = ins[0][...]
    clipped = grad_ref[...] * scalar_ref[0]
    first_new = BETA_ONE * ins[1][...] + (1.0 - BETA_ONE) * clipped
    second_new = BETA_TWO * ins[2][...] + (1.0 - BETA_TWO) * clipped * clipped
    first_hat = first_new / scalar_ref[1]
    second_hat = second_new / scalar_ref[2]
    weights_new = weights * (1.0 - LEARN_RATE * WEIGHT_DECAY) - LEARN_RATE * first_hat / (
        jnp.sqrt(second_hat) + ADAM_EPS
    )
    outs[0][...] = weights_new
    outs[1][...] = first_new
    outs[2][...] = second_new
    outs[3][...] = weights_new.astype(jnp.bfloat16)
    if with_average:
        outs[4][...] = EMA_RATE * ins[3][...] + (1.0 - EMA_RATE) * weights_new


def adamw(parts, arrays, factor, steps_done):
    count = len(parts)
    place = lax.axis_index("grp")
    places = jnp.stack([(place ^ index) % count for index in range(count)])
    rows = arrays[0].shape[0]
    steps = 1
    for split in (2, 3, 4, 6, 8):
        if rows % (split * 8 * count) == 0:
            steps = split
    block = pl.BlockSpec((rows // steps, 128), lambda i: (i, 0))
    share = pl.BlockSpec((rows // steps // count, 128), lambda i: (i, 0))
    scalar = pl.BlockSpec(memory_space=pltpu.SMEM)
    scalars = jnp.stack([factor, 1.0 - BETA_ONE**steps_done, 1.0 - BETA_TWO**steps_done])
    full = jax.ShapeDtypeStruct((rows, 128), jnp.float32)
    shapes = [full, full, full, jax.ShapeDtypeStruct((rows, 128), jnp.bfloat16)]
    if len(arrays) == 4:
        shapes.append(full)
    return pl.pallas_call(
        functools.partial(adamw_kernel, count, len(arrays) == 4),
        grid=(steps,),
        in_specs=[scalar, scalar] + [share] * count + [block] * len(arrays),
        out_specs=[block] * len(shapes),
        out_shape=shapes,
        scratch_shapes=[pltpu.VMEM((rows // steps, 128), jnp.float32)],
        compiler_params=pltpu.CompilerParams(vmem_limit_bytes=40 << 20),
    )(places.astype(jnp.int32), scalars, *parts, *arrays)


def per_device(
    patches,
    segments,
    visible,
    enc_params,
    enc_first,
    enc_second,
    enc_average,
    dec_params,
    dec_first,
    dec_second,
    step_count,
):
    my_index = lax.axis_index("grp")
    slot_dev = segments.shape[0]
    rim = TILE_HI
    counts = jnp.sum((segments >= 0).astype(jnp.float32)) - visible.shape[0]
    total_count = total(jnp.full((8, 128), counts))[0, 0]
    enc_copy = gather_quarters(enc_params.astype(jnp.bfloat16))
    group_vis = group_rows(visible)
    group_seg = double(double(segments, 0, "grp", 2), 1, "grp", 1).reshape(-1)
    group_ids = group_seg[group_vis]
    key_ids = extended(segments + 3, rim) - 3
    local_slot = group_vis - my_index * slot_dev
    chosen = (
        local_slot[:, None] == jnp.arange(slot_dev, dtype=jnp.int32)[None, :]
    ).astype(jnp.bfloat16)
    seen = jnp.sum(chosen.astype(jnp.float32), axis=0) > 0.5
    enc_input = own_rows(matmul(chosen, patches).astype(jnp.bfloat16))
    enc_waves = sincos(visible % L, D)
    positions = (my_index * slot_dev + jnp.arange(slot_dev, dtype=jnp.int32)) % L
    dec_waves = sincos(positions, E)
    pixels = patches.astype(jnp.float32)
    pixel_mean = jnp.mean(pixels, axis=1, keepdims=True)
    centered = pixels - pixel_mean
    pixel_rate = lax.rsqrt(jnp.mean(centered * centered, axis=1, keepdims=True) + NORM_EPS)
    (
        enc_copy,
        enc_input,
        enc_waves,
        dec_waves,
        pixel_mean,
        pixel_rate,
        seen,
        group_ids,
        key_ids,
        chosen,
        total_count,
    ) = lax.optimization_barrier(
        (
            enc_copy,
            enc_input,
            enc_waves,
            dec_waves,
            pixel_mean,
            pixel_rate,
            seen,
            group_ids,
            key_ids,
            chosen,
            total_count,
        )
    )
    own_ids = group_ids[: visible.shape[0]]
    enc_copy, dec_shard = lax.optimization_barrier((enc_copy, dec_params))
    dec_copy = gather_quarters(dec_shard.astype(jnp.bfloat16))
    enc_table = unpack(enc_copy, enc_pieces(), ENC_STEPS)
    dec_table = unpack(dec_copy, dec_pieces(), DEC_STEPS)
    enc_start = (
        matmul(enc_input, enc_table["patch_w"])
        + enc_table["patch_b"].astype(jnp.float32)
        + enc_waves
    )

    def enc_share(pair):
        joined = group_rows(jnp.concatenate(pair, axis=1))
        return (joined[:, :D], joined[:, D:])

    enc_out, enc_saved = block_forward(enc_start, enc_table, H, 0, own_ids, group_ids, enc_share)
    enc_gain = enc_table["norm_g"].astype(jnp.float32)
    enc_shift = enc_table["norm_b"].astype(jnp.float32)
    enc_final = layer_norm(enc_out, enc_gain[2], enc_shift[2]).astype(jnp.bfloat16)
    latent = (
        matmul(enc_final, dec_table["embed_w"]) + dec_table["embed_b"].astype(jnp.float32)
    ).astype(jnp.bfloat16)
    group_latent = group_rows(latent)
    enc_inputs = jnp.concatenate(
        [enc_saved[1], enc_saved[5], enc_saved[7], enc_saved[9], enc_input], axis=1
    )
    group_latent, enc_inputs = lax.optimization_barrier((group_latent, enc_inputs))
    group_inputs = group_rows(enc_inputs)
    placed = trans_mul(chosen, group_latent)
    dec_start = jnp.where(
        seen[:, None], placed, dec_table["mask_token"].astype(jnp.float32)[None, :]
    ) + dec_waves
    counted = jnp.where((segments >= 0) & jnp.logical_not(seen), 1.0, 0.0)

    def dec_share(pair):
        joined = extended(jnp.concatenate(pair, axis=1), rim)
        return (joined[:, :E], joined[:, E:])

    def dec_return(pair):
        joined = jnp.concatenate(pair, axis=1)
        from_upper = passed_along(joined[:rim], "grp", -1)
        from_lower = passed_along(joined[rim + slot_dev :], "grp", 1)
        middle = joined[rim : rim + slot_dev]
        middle = jnp.concatenate(
            [
                middle[:rim] + from_lower,
                middle[rim : slot_dev - rim],
                middle[slot_dev - rim :] + from_upper,
            ],
            axis=0,
        )
        return (middle[:, :E], middle[:, E:])

    dec_out, dec_saved = block_forward(
        dec_start, dec_table, EH, rim, segments, key_ids, dec_share
    )
    dec_gain = dec_table["norm_g"].astype(jnp.float32)
    dec_shift = dec_table["norm_b"].astype(jnp.float32)
    dec_final = layer_norm(dec_out, dec_gain[2], dec_shift[2]).astype(jnp.bfloat16)
    predicted = matmul(dec_final, dec_table["pix_w"]) + dec_table["pix_b"].astype(jnp.float32)
    target = (patches.astype(jnp.float32) - pixel_mean) * pixel_rate
    errors = predicted - target
    loss_part = jnp.sum(counted * jnp.mean(errors * errors, axis=1))
    errors, group_inputs = lax.optimization_barrier((errors, group_inputs))
    pred_grad = (counted[:, None] * errors * (2.0 / PATCH) / total_count).astype(jnp.bfloat16)
    dec_out_grad, dec_gain_last, dec_shift_last = norm_back(
        dec_out, dec_gain[2], dec_shift[2], mul_trans(pred_grad, dec_table["pix_w"])
    )
    start_grad, dec_small, dec_pairs = block_backward(
        dec_out_grad, dec_table, EH, rim, segments, key_ids, dec_saved, dec_return, lambda grad: grad
    )
    mask_grad = jnp.sum(jnp.where(seen[:, None], 0.0, start_grad), axis=0)
    latent_grad = own_rows(matmul(chosen, start_grad.astype(jnp.bfloat16)).astype(jnp.bfloat16))
    dec_pairs["embed_w"] = (enc_final, latent_grad)
    dec_pairs["pix_w"] = (dec_final, pred_grad)
    mine, theirs = dec_grad_halves(
        [dec_pairs[name] for name in ("embed_w", "qkv_w", "out_w", "up_w", "down_w", "pix_w")],
        jnp.stack(
            [
                mask_grad,
                dec_small[0],
                dec_small[2],
                dec_gain_last,
                dec_small[1],
                dec_small[3],
                dec_shift_last,
            ]
        ),
        DR,
    )
    arrived = swap(theirs, "grp", 1)
    latent_grad, mine = lax.optimization_barrier((latent_grad, mine))
    dec_blocks = None

    def enc_pause(grad):
        nonlocal dec_blocks
        grad, dec_half = lax.optimization_barrier((grad, mine + arrived))
        dec_blocks = reduce_first(dec_half, dec_routes(), (0.5,))
        return grad

    enc_out_grad, enc_gain_last, enc_shift_last = norm_back(
        enc_out, enc_gain[2], enc_shift[2], mul_trans(latent_grad, dec_table["embed_w"])
    )
    def enc_return(pair):
        nonlocal dec_blocks
        joined = own_rows(jnp.concatenate(pair, axis=1))
        joined, dec_blocks = lax.optimization_barrier((joined, dec_blocks))
        return (joined[:, :D], joined[:, D:])

    enc_start_grad, enc_small, enc_pairs = block_backward(
        enc_out_grad, enc_table, H, 0, own_ids, group_ids, enc_saved, enc_return, enc_pause
    )
    enc_norms = jnp.stack(
        [
            enc_small[0],
            enc_small[2],
            enc_gain_last,
            enc_small[1],
            enc_small[3],
            enc_shift_last,
            jnp.zeros_like(enc_shift_last),
            jnp.zeros_like(enc_shift_last),
        ]
    )
    enc_pairs["patch_w"] = (enc_input, enc_start_grad.astype(jnp.bfloat16))
    names = ("patch_w", "qkv_w", "out_w", "up_w", "down_w")
    places = [(3 * D + F, PATCH), (0, D), (D, D), (2 * D, D), (3 * D, F)]
    enc_quarter = enc_grad_quarter(
        group_inputs,
        places,
        [group_rows(enc_pairs[name][1]) for name in names],
        group_rows(enc_norms),
        ER,
    )
    enc_blocks = reduce_first(enc_quarter, dp_routes(), (0.5,))
    enc_sum = reduce_rest(enc_blocks, dp_routes())
    dec_sum = reduce_rest(dec_blocks, dec_routes())
    squares = sum(jnp.sum(part * part) for part in enc_sum + dec_sum)
    lane = lax.broadcasted_iota(jnp.int32, (8, 128), 1)
    enc_own = jnp.concatenate(enc_sum, axis=0)
    enc_across = swap(enc_own, "grp", 2)
    sums = total(jnp.where(lane == 0, squares, jnp.where(lane == 1, loss_part, 0.0)))
    enc_across, sums = lax.optimization_barrier((enc_across, sums))
    enc_quarters = (
        enc_own,
        swap(enc_own, "grp", 1),
        enc_across,
        swap(enc_across, "grp", 1),
    )
    loss_total = sums[0, 1]
    grad_norm = jnp.sqrt(sums[0, 0])
    factor = jnp.minimum(1.0, CLIP_LIMIT / (grad_norm + NORM_EPS))
    steps_done = step_count[0].astype(jnp.float32)
    enc_new, enc_first_new, enc_second_new, enc_copy_new, average_new = adamw(
        enc_quarters, (enc_params, enc_first, enc_second, enc_average), factor, steps_done
    )
    dec_new, dec_first_new, dec_second_new, dec_copy_new = adamw(
        spread_pieces(dec_sum), (dec_params, dec_first, dec_second), factor, steps_done
    )
    return (
        enc_new,
        enc_first_new,
        enc_second_new,
        enc_copy_new,
        dec_new,
        dec_first_new,
        dec_second_new,
        dec_copy_new,
        average_new,
        grad_norm,
        loss_total,
        total_count,
    )


def solution(mesh):
    placed = (
        P(("dp", "grp"), None),
        P(("dp", "grp")),
        P(("dp", "grp")),
        P("dp", None),
        P("dp", None),
        P("dp", None),
        P("dp", None),
        P("dp", None),
        P("dp", None),
        P("dp", None),
        P(),
    )
    return jax.shard_map(
        per_device,
        mesh=mesh,
        in_specs=placed,
        out_specs=(
            P("dp", None),
            P("dp", None),
            P("dp", None),
            P("dp", None),
            P("dp", None),
            P("dp", None),
            P("dp", None),
            P("dp", None),
            P("dp", None),
            P(),
            P(),
            P(),
        ),
        check_vma=False,
    )
```

```python
import functools
import math

import jax
import jax.numpy as jnp
from jax import lax
from jax.experimental import pallas as pl
from jax.experimental.pallas import tpu as pltpu
from jax.sharding import PartitionSpec as P

D = 768
H = 12
F = 3072
E = 512
EH = 16
FE = 2048
PATCH = 1728
L = 1728
TILE_HI = 192
ER = 66048
DR = 34816


NORM_EPS = 1e-06
MASK_FILL = -1e30
CLIP_LIMIT = 0.0002
LEARN_RATE = 0.02
BETA_ONE = 0.5
BETA_TWO = 0.5
ADAM_EPS = 1e-08
WEIGHT_DECAY = 0.05
EMA_RATE = 0.9


def swap(block, axis, bit):
    count = lax.axis_size(axis)
    return lax.ppermute(block, axis, [(i, i ^ bit) for i in range(count)])


def bit_of(axis, bit):
    return (lax.axis_index(axis) // bit) % 2


def double(block, dim, axis, bit):
    mine = bit_of(axis, bit)
    other = swap(block, axis, bit)
    first = jnp.where(mine == 0, block, other)
    second = jnp.where(mine == 0, other, block)
    return jnp.stack([first, second], axis=dim)


def total(values):
    for axis in ("grp", "dp"):
        bit = 1
        while bit < lax.axis_size(axis):
            values = values + swap(values, axis, bit)
            bit *= 2
    return values


def dp_bits():
    bits = [1]
    while bits[-1] * 2 < lax.axis_size("dp"):
        bits.append(bits[-1] * 2)
    return bits


def cut(rows, shares):
    unit = 16 if rows % 16 == 0 else 2
    sizes = [int(round(rows // unit * share)) * unit for share in shares]
    return sizes + [rows - sum(sizes)]


def gather_quarters(shard):
    part = shard.shape[0] // 4
    quarter = lax.dynamic_slice_in_dim(shard, lax.axis_index("grp") * part, part, 0)
    return lax.all_gather(quarter, ("dp", "grp"), axis=0, tiled=True)


def section(cells, dim, start, size):
    return lax.dynamic_slice_in_dim(cells, start, size, dim)


def reduce_bit(cells, dim, axis, bit, start=0, size=None):
    half = (cells.shape[dim] if size is None else size) // 2
    mine = bit_of(axis, bit)
    sent = section(cells, dim, start + (1 - mine) * half, half)
    return section(cells, dim, start + mine * half, half) + swap(sent, axis, bit)


def dec_routes():
    bits = [("dp", bit) for bit in dp_bits()]
    return [bits[:1] + [("grp", 2)] + bits[1:], bits[1:2] + [("grp", 2)] + bits[2:] + bits[:1]]


def reduce_first(half, routes, shares):
    shards = lax.axis_size("dp")
    half_rows = half.shape[0] // shards
    bits = dp_bits()
    names = [("dp", bit) for bit in reversed(bits)]
    cells = half.reshape([2] * len(bits) + [half_rows, 128])
    blocks = []
    start = 0
    for route, rows in zip(routes, cut(half_rows, shares)):
        axis, bit = route[0]
        if axis == "grp":
            block = reduce_bit(cells, len(bits), axis, bit, start, rows)
        else:
            dim = names.index(route[0])
            mine = bit_of(axis, bit)

            def pick(index, dim=dim, start=start, rows=rows):
                corner = [0] * dim + [index] + [0] * (len(bits) - dim - 1) + [start, 0]
                sizes = [2] * dim + [1] + [2] * (len(bits) - dim - 1) + [rows, 128]
                return lax.dynamic_slice(cells, corner, sizes)

            block = pick(mine) + swap(pick(1 - mine), axis, bit)
        blocks.append(block)
        start += rows
    return blocks


def reduce_rest(blocks, routes, first=1, last=None):
    bits = dp_bits()
    names = [("dp", bit) for bit in reversed(bits)]
    blocks = list(blocks)
    for step in range(first, len(routes[0]) if last is None else last):
        for index, route in enumerate(routes):
            axis, bit = route[step]
            dim = len(bits) if axis == "grp" else names.index(route[step])
            blocks[index] = reduce_bit(blocks[index], dim, axis, bit)
    if last is not None:
        return blocks
    return [block.reshape(-1, 128) for block in blocks]


def dp_routes():
    bits = [("dp", bit) for bit in dp_bits()]
    return [bits, bits[1:] + bits[:1]]


def spread_pieces(pieces):
    wide = [double(piece, 0, "grp", 2).reshape(-1, 128) for piece in pieces]
    mine = jnp.concatenate(wide, axis=0)
    return mine, swap(mine, "grp", 1)


def group_rows(block):
    across = swap(block, "grp", 2)
    near, far = (
        swap(block, "grp", 1),
        swap(across, "grp", 1),
    )
    return jnp.concatenate([block, near, across, far], axis=0)


def own_rows(blocks):
    count = blocks.shape[0] // 4
    parts = [lax.slice_in_dim(blocks, i * count, (i + 1) * count, axis=0) for i in range(4)]
    sent = jnp.concatenate([parts[1], parts[3]], axis=0)
    arrived = swap(sent, "grp", 1)
    kept = parts[0] + arrived[:count]
    other = parts[2] + arrived[count:]
    return kept + swap(other, "grp", 2)


def extended(cells, width):
    count = lax.axis_size("grp")
    ends = count - 1
    head = cells[:width]
    tail = cells[cells.shape[0] - width :]
    return jnp.concatenate(
        [
            lax.ppermute(tail, "grp", [(i, i + 1) for i in range(ends)]),
            cells,
            lax.ppermute(head, "grp", [(i + 1, i) for i in range(ends)]),
        ],
        axis=0,
    )


def passed_along(block, axis, distance):
    devices = range(lax.axis_size(axis))
    route = [(i - distance, i) for i in devices if i - distance in devices]
    return lax.ppermute(block, axis, route)


def enc_pieces():
    return [
        ("patch_w", (PATCH, D)),
        ("qkv_w", (D, 3 * D)),
        ("out_w", (D, D)),
        ("up_w", (D, F)),
        ("down_w", (F, D)),
        ("patch_b", (D,)),
        ("out_b", (D,)),
        ("up_b", (F,)),
        ("down_b", (D,)),
        ("norm_g", (3, D)),
        ("norm_b", (3, D)),
    ]


def dec_pieces():
    return [
        ("embed_w", (D, E)),
        ("qkv_w", (E, 3 * E)),
        ("out_w", (E, E)),
        ("up_w", (E, FE)),
        ("down_w", (FE, E)),
        ("pix_w", (E, PATCH)),
        ("embed_b", (E,)),
        ("mask_token", (E,)),
        ("out_b", (E,)),
        ("up_b", (FE,)),
        ("down_b", (E,)),
        ("pix_b", (PATCH,)),
        ("norm_g", (3, E)),
        ("norm_b", (3, E)),
    ]


def relayout_kernel(plan, *refs):
    source, outs = refs[0], refs[1 : 1 + len(plan)]
    raw_ref, wide_ref, stages, in_sems, out_sems = (
        refs[1 + len(plan)],
        refs[2 + len(plan)],
        refs[3 + len(plan) : -2],
        refs[-2],
        refs[-1],
    )
    steps = [
        (index, offset + start * blocks, start, rows, blocks)
        for index, (offset, depth, blocks, rows) in enumerate(plan)
        for start in range(0, depth, rows)
    ]

    def fetch(turn):
        _, offset, _, rows, blocks = steps[turn]
        return pltpu.make_async_copy(
            source.at[pl.ds(offset, rows * blocks)],
            raw_ref.at[turn % 2, pl.ds(0, rows * blocks)],
            in_sems.at[turn % 2],
        )

    flight = {}
    fetch(0).start()
    for turn, (index, _, start, rows, blocks) in enumerate(steps):
        if turn + 1 < len(steps):
            fetch(turn + 1).start()
        fetch(turn).wait()
        wide_ref[: rows * blocks, :] = raw_ref[turn % 2, : rows * blocks, :].astype(jnp.float32)
        slot = turn % 2
        if slot in flight:
            flight.pop(slot).wait()
        stage = stages[index].at[slot]
        for block in range(blocks):
            stage[:, block * 128 : (block + 1) * 128] = wide_ref[
                pl.ds(block, rows, stride=blocks), :
            ].astype(jnp.bfloat16)
        flight[slot] = pltpu.make_async_copy(
            stage, outs[index].at[pl.ds(start, rows)], out_sems.at[slot]
        )
        flight[slot].start()
    for copy in flight.values():
        copy.wait()


def relayout(rows, plan):
    anywhere = pl.BlockSpec(memory_space=pl.ANY)
    most = max(step * blocks for _, _, blocks, step in plan)
    return pl.pallas_call(
        functools.partial(relayout_kernel, plan),
        in_specs=[anywhere],
        out_specs=[anywhere] * len(plan),
        out_shape=[
            jax.ShapeDtypeStruct((depth, blocks * 128), jnp.bfloat16)
            for _, depth, blocks, _ in plan
        ],
        scratch_shapes=[
            pltpu.VMEM((2, most, 128), jnp.bfloat16),
            pltpu.VMEM((most, 128), jnp.float32),
        ]
        + [pltpu.VMEM((2, step, blocks * 128), jnp.bfloat16) for _, _, blocks, step in plan]
        + [pltpu.SemaphoreType.DMA((2,)), pltpu.SemaphoreType.DMA((2,))],
        compiler_params=pltpu.CompilerParams(vmem_limit_bytes=40 << 20),
        cost_estimate=pl.CostEstimate(
            flops=0, bytes_accessed=rows.size * 4, transcendentals=0
        ),
    )(rows)


ENC_STEPS = {"patch_w": 576, "qkv_w": 192, "out_w": 384, "up_w": 128, "down_w": 512}
DEC_STEPS = {"embed_w": 768, "qkv_w": 256, "out_w": 512, "up_w": 128, "down_w": 512}


def unpack(rows, pieces, steps):
    table = {}
    offset = 0
    plan = []
    vectors = sum(1 for _, dims in pieces if len(dims) == 2 and dims[0] > 3)
    for piece_name, piece_dims in pieces[:vectors]:
        amount = math.prod(piece_dims) // 128
        if piece_name in steps:
            plan.append((offset, piece_dims[0], piece_dims[1] // 128, steps[piece_name]))
        else:
            table[piece_name] = rows[offset : offset + amount].reshape(piece_dims)
        offset += amount
    small = rows[offset:].reshape(-1)
    table.update(zip(steps, relayout(rows, plan)))
    offset = 0
    for piece_name, piece_dims in pieces[vectors:]:
        amount = math.prod(piece_dims)
        table[piece_name] = small[offset : offset + amount].reshape(piece_dims)
        offset += amount
    return table


def matmul(left, right):
    return jnp.dot(left, right, preferred_element_type=jnp.float32)


def mul_trans(left, right):
    return lax.dot_general(
        left, right, (((1,), (1,)), ((), ())), preferred_element_type=jnp.float32
    )


def trans_mul(left, right):
    return lax.dot_general(
        left, right, (((0,), (0,)), ((), ())), preferred_element_type=jnp.float32
    )


def sincos(positions, width):
    half_width = width // 2
    freq_row = jnp.exp(
        jnp.arange(half_width, dtype=jnp.float32) * (-2.0 * math.log(10000.0) / width)
    )
    angles = positions.astype(jnp.float32)[:, None] * freq_row[None, :]
    return jnp.concatenate([jnp.sin(angles), jnp.cos(angles)], axis=1)


def layer_norm(inputs, gain, shift):
    center = inputs - jnp.mean(inputs, axis=-1, keepdims=True)
    return (
        center * lax.rsqrt(jnp.mean(center * center, axis=-1, keepdims=True) + NORM_EPS) * gain
        + shift
    )


def norm_back(inputs, gain, shift, grad_out):
    outputs, pull = jax.vjp(layer_norm, inputs, gain, shift)
    return pull(grad_out)


def exact_gelu(values):
    return jax.nn.gelu(values, approximate=False)


BLOCK = 128


def head_masks(width):
    lanes = lax.broadcasted_iota(jnp.int32, (1, 128), 1) // width
    return [(lanes == index).astype(jnp.float32) for index in range(128 // width)]


def spread_heads(cells, masks):
    wide = cells.astype(jnp.float32)
    return jnp.concatenate([(wide * mask).astype(jnp.bfloat16) for mask in masks], axis=0)


TILE = 32
TALL = 64


def attend_kernel(
    window,
    stride,
    width,
    q_ref,
    k_ref,
    v_ref,
    qid_ref,
    kid_ref,
    o_ref,
    bias_ref,
    score_ref,
    prob_ref,
):
    start = pl.multiple_of(pl.program_id(0) * stride, BLOCK)
    scale = width ** (-0.5)
    masks = head_masks(width)
    near = pl.ds(start, window)
    bias_ref[...] = jnp.where(qid_ref[...] == kid_ref[:, near], 0.0, MASK_FILL)
    for group in range(q_ref.shape[1] // 128):
        lanes = slice(group * 128, (group + 1) * 128)
        slot = group % 2
        score_ref[slot] = mul_trans(spread_heads(q_ref[:, lanes], masks), k_ref[near, lanes])
        for first in range(0, len(masks) * BLOCK, TILE):
            rows = slice(first, first + TILE)
            row = first % BLOCK
            part = score_ref[slot, rows, :] * scale + bias_ref[row : row + TILE, :]
            powers = jnp.exp(part - jnp.max(part, axis=1, keepdims=True))
            probs = powers * (1.0 / jnp.sum(powers, axis=1, keepdims=True))
            prob_ref[slot, rows, :] = probs.astype(jnp.bfloat16)
        wide = matmul(prob_ref[slot], v_ref[near, lanes])
        o_ref[:, lanes] = pick_heads(wide, masks).astype(jnp.bfloat16)


def pick_heads(wide, masks):
    return sum(wide[i * BLOCK : (i + 1) * BLOCK] * mask for i, mask in enumerate(masks))


def row_sums(cells, merge):
    return merge(cells.reshape(-1, 8, cells.shape[1]), axis=0)


def attend_back_kernel(window, stride, width, pick, *refs):
    q_ref, g_ref, k_ref, v_ref, qid_ref, kid_ref = refs[:6]
    dq_ref, dk_ref, dv_ref, bias_ref, score_ref, grad_ref, prob_ref, back_ref = refs[-8:]
    before = refs[6:-8]
    step = pl.program_id(0)
    start = pl.multiple_of(pick(step) * stride, BLOCK)
    scale = width ** (-0.5)
    masks = head_masks(width)

    @pl.when(step == 0)
    def _():
        dk_ref[...] = before[0][...] if before else jnp.zeros_like(dk_ref)
        dv_ref[...] = before[1][...] if before else jnp.zeros_like(dv_ref)

    near = pl.ds(start, window)
    bias_ref[...] = jnp.where(kid_ref[near, :] == qid_ref[...], 0.0, MASK_FILL)
    tiles = [slice(first, first + TALL) for first in range(0, window, TALL)]
    for group in range(q_ref.shape[1] // 128):
        lanes = slice(group * 128, (group + 1) * 128)
        slot = group % 2
        keys = k_ref[near, lanes]
        queries = spread_heads(q_ref[:, lanes], masks)
        outs = spread_heads(g_ref[:, lanes], masks)
        score_ref[slot] = mul_trans(keys, queries)
        grad_ref[slot] = mul_trans(v_ref[near, lanes], outs)
        for index in range(len(masks)):
            head = slice(index * BLOCK, (index + 1) * BLOCK)
            top = None
            for tile in tiles:
                part = score_ref[slot, tile, head] * scale + bias_ref[tile, :]
                score_ref[slot, tile, head] = part
                most = row_sums(part, jnp.max)
                top = most if top is None else jnp.maximum(top, most)
            top = jnp.max(top, axis=0, keepdims=True)
            whole = jnp.zeros((8, BLOCK), jnp.float32)
            for tile in tiles:
                powers = jnp.exp(score_ref[slot, tile, head] - top)
                score_ref[slot, tile, head] = powers
                whole += row_sums(powers, jnp.sum)
            inverse = 1.0 / jnp.sum(whole, axis=0, keepdims=True)
            shared = jnp.zeros((8, BLOCK), jnp.float32)
            for tile in tiles:
                probs = score_ref[slot, tile, head] * inverse
                prob_ref[slot, tile, head] = probs.astype(jnp.bfloat16)
                shared += row_sums(probs * grad_ref[slot, tile, head], jnp.sum)
            shared = jnp.sum(shared, axis=0, keepdims=True)
            for tile in tiles:
                probs = score_ref[slot, tile, head] * inverse
                back_ref[slot, tile, head] = (
                    probs * (grad_ref[slot, tile, head] - shared)
                ).astype(jnp.bfloat16)
        back = back_ref[slot]
        dv_ref[near, lanes] += matmul(prob_ref[slot], outs)
        dk_ref[near, lanes] += matmul(back, queries) * scale
        dq_ref[:, lanes] = pick_heads(trans_mul(back, keys), masks) * scale


def padded(cells, rows, fill=0):
    return jnp.pad(
        cells, [(0, rows - cells.shape[0])] + [(0, 0)] * (cells.ndim - 1), constant_values=fill
    )


def attend_sizes(query, keys, rim):
    steps = -(-query.shape[0] // BLOCK)
    if rim:
        return steps, BLOCK + 2 * rim, steps * BLOCK + 2 * rim, BLOCK
    return steps, keys.shape[0], keys.shape[0], 0


def whole_spec(dims):
    return pl.BlockSpec(dims, lambda i: (0, 0))


def step_spec(columns):
    return pl.BlockSpec((BLOCK, columns), lambda i: (i, 0))


def attend(query, keys, values, query_ids, key_ids, heads, rim):
    count, columns = query.shape
    steps, window, span, stride = attend_sizes(query, keys, rim)
    stack = 128 * heads // columns * BLOCK
    outcome = pl.pallas_call(
        functools.partial(attend_kernel, window, stride, columns // heads),
        grid=(steps,),
        in_specs=[
            step_spec(columns),
            whole_spec((span, columns)),
            whole_spec((span, columns)),
            step_spec(1),
            whole_spec((1, span)),
        ],
        out_specs=step_spec(columns),
        out_shape=jax.ShapeDtypeStruct((steps * BLOCK, columns), jnp.bfloat16),
        scratch_shapes=[
            pltpu.VMEM((BLOCK, window), jnp.float32),
            pltpu.VMEM((2, stack, window), jnp.float32),
            pltpu.VMEM((2, stack, window), jnp.bfloat16),
        ],
        compiler_params=pltpu.CompilerParams(vmem_limit_bytes=48 << 20),
        cost_estimate=pl.CostEstimate(
            flops=4 * steps * BLOCK * window * columns,
            bytes_accessed=8 * span * columns,
            transcendentals=steps * BLOCK * window * heads,
        ),
    )(
        padded(query, steps * BLOCK),
        padded(keys, span),
        padded(values, span),
        padded(query_ids, steps * BLOCK, -4)[:, None],
        padded(key_ids, span, -5)[None, :],
    )
    return outcome[:count]


def same_step(step):
    return step


def attend_back(
    query, keys, values, query_ids, key_ids, heads, rim, out_grad, steps=None, pick=same_step, before=()
):
    count, columns = query.shape
    all_steps, window, span, stride = attend_sizes(query, keys, rim)
    steps = all_steps if steps is None else steps
    stack = 128 * heads // columns * BLOCK
    block = pl.BlockSpec((BLOCK, columns), lambda i: (pick(i), 0))
    return pl.pallas_call(
        functools.partial(attend_back_kernel, window, stride, columns // heads, pick),
        grid=(steps,),
        in_specs=[
            block,
            block,
            whole_spec((span, columns)),
            whole_spec((span, columns)),
            pl.BlockSpec((1, BLOCK), lambda i: (0, pick(i))),
            whole_spec((span, 1)),
        ]
        + [whole_spec((span, columns))] * len(before),
        out_specs=[block, whole_spec((span, columns)), whole_spec((span, columns))],
        out_shape=[
            jax.ShapeDtypeStruct((all_steps * BLOCK, columns), jnp.float32),
            jax.ShapeDtypeStruct((span, columns), jnp.float32),
            jax.ShapeDtypeStruct((span, columns), jnp.float32),
        ],
        scratch_shapes=[
            pltpu.VMEM((window, BLOCK), jnp.float32),
            pltpu.VMEM((2, window, stack), jnp.float32),
            pltpu.VMEM((2, window, stack), jnp.float32),
            pltpu.VMEM((2, window, stack), jnp.bfloat16),
            pltpu.VMEM((2, window, stack), jnp.bfloat16),
        ],
        compiler_params=pltpu.CompilerParams(vmem_limit_bytes=48 << 20),
        cost_estimate=pl.CostEstimate(
            flops=80 * steps * BLOCK * window * columns,
            bytes_accessed=20 * span * columns,
            transcendentals=steps * BLOCK * window * heads,
        ),
    )(
        padded(query, all_steps * BLOCK),
        padded(out_grad, all_steps * BLOCK),
        padded(keys, span),
        padded(values, span),
        padded(query_ids, all_steps * BLOCK, -4)[None, :],
        padded(key_ids, span, -5)[:, None],
        *before,
    )


def attend_back_slots(query, keys, values, query_ids, key_ids, heads, rim, out_grad):
    count = query.shape[0]
    steps, window, _, _ = attend_sizes(query, keys, rim)
    low = -(-rim // BLOCK)
    high = next(i for i in range(low, steps) if i * BLOCK + window > rim + count)
    args = (query, keys, values, query_ids, key_ids, heads, rim, out_grad)
    edges = attend_back(
        *args, steps=low + steps - high, pick=lambda i: i + (i // low) * (high - low)
    )
    ends = slice(rim + count, 2 * rim + count)
    from_upper = passed_along(
        jnp.concatenate([edges[1][:rim], edges[2][:rim]], axis=1), "grp", -1
    )
    from_lower = passed_along(
        jnp.concatenate([edges[1][ends], edges[2][ends]], axis=1), "grp", 1
    )
    inner = attend_back(
        *args, steps=high - low, pick=lambda i: i + low, before=(edges[1], edges[2])
    )
    query_grad = jnp.concatenate(
        [
            edges[0][: low * BLOCK],
            inner[0][low * BLOCK : high * BLOCK],
            edges[0][high * BLOCK : count],
        ],
        axis=0,
    )
    middle = jnp.concatenate([inner[1], inner[2]], axis=1)[rim : rim + count]
    middle = jnp.concatenate(
        [
            middle[:rim] + from_lower,
            middle[rim : count - rim],
            middle[count - rim :] + from_upper,
        ],
        axis=0,
    )
    return jnp.concatenate([query_grad, middle], axis=1)


def gelu_pair(hidden):
    below = 0.5 * (1.0 + lax.erf(hidden * math.sqrt(0.5)))
    bell = jnp.exp(-0.5 * hidden * hidden) * (1.0 / math.sqrt(2.0 * math.pi))
    return lax.optimization_barrier(
        ((hidden * below).astype(jnp.bfloat16), below + hidden * bell)
    )


def block_forward(inputs, table, heads, rim, query_ids, key_ids, share_keys):
    gains = table["norm_g"].astype(jnp.float32)
    shifts = table["norm_b"].astype(jnp.float32)
    width = inputs.shape[1]
    normed_one = layer_norm(inputs, gains[0], shifts[0]).astype(jnp.bfloat16)
    qkv = matmul(normed_one, table["qkv_w"]).astype(jnp.bfloat16)
    query = qkv[:, :width]
    all_keys, all_values = share_keys((qkv[:, width : 2 * width], qkv[:, 2 * width :]))
    attended = attend(query, all_keys, all_values, query_ids, key_ids, heads, rim)
    mixed = inputs + (matmul(attended, table["out_w"]) + table["out_b"].astype(jnp.float32))
    normed_two = layer_norm(mixed, gains[1], shifts[1]).astype(jnp.bfloat16)
    hidden = matmul(normed_two, table["up_w"]) + table["up_b"].astype(jnp.float32)
    activated, slope = gelu_pair(hidden)
    result = mixed + (matmul(activated, table["down_w"]) + table["down_b"].astype(jnp.float32))
    saved = (
        inputs,
        normed_one,
        query,
        all_keys,
        all_values,
        attended,
        mixed,
        normed_two,
        slope,
        activated,
    )
    return (result, saved)


def block_backward(
    grad_out, table, heads, rim, query_ids, key_ids, saved
):
    (
        inputs,
        normed_one,
        query,
        all_keys,
        all_values,
        attended,
        mixed,
        normed_two,
        slope,
        activated,
    ) = saved
    gains = table["norm_g"].astype(jnp.float32)
    shifts = table["norm_b"].astype(jnp.float32)
    pairs = {}
    down_grad = grad_out.astype(jnp.bfloat16)
    pairs["down_w"] = (activated, down_grad)
    act_grad = mul_trans(down_grad, table["down_w"])
    hidden_grad = (act_grad * slope).astype(jnp.bfloat16)
    pairs["up_w"] = (normed_two, hidden_grad)
    mixed_part, gain_two, shift_two = norm_back(
        mixed, gains[1], shifts[1], mul_trans(hidden_grad, table["up_w"])
    )
    mixed_grad = grad_out + mixed_part
    branch_grad = mixed_grad.astype(jnp.bfloat16)
    pairs["out_w"] = (attended, branch_grad)
    attended_grad = mul_trans(branch_grad, table["out_w"]).astype(jnp.bfloat16)
    qkv_grad = attend_back_slots(
        query, all_keys, all_values, query_ids, key_ids, heads, rim, attended_grad
    ).astype(jnp.bfloat16)
    pairs["qkv_w"] = (normed_one, qkv_grad)
    input_part, gain_one, shift_one = norm_back(
        inputs, gains[0], shifts[0], mul_trans(qkv_grad, table["qkv_w"])
    )
    return (mixed_grad + input_part, (gain_one, shift_one, gain_two, shift_two), pairs)


def enc_forward(inputs, table, own, ids):
    gains = table["norm_g"].astype(jnp.float32)
    shifts = table["norm_b"].astype(jnp.float32)
    normed_one = layer_norm(inputs, gains[0], shifts[0]).astype(jnp.bfloat16)
    qkv = matmul(normed_one, table["qkv_w"]).astype(jnp.bfloat16)
    attended = attend(
        qkv[:own, :D], qkv[:, D : 2 * D], qkv[:, 2 * D :], ids[:own], ids, H, 0
    )
    mixed = inputs[:own] + (matmul(attended, table["out_w"]) + table["out_b"].astype(jnp.float32))
    normed_two = layer_norm(mixed, gains[1], shifts[1]).astype(jnp.bfloat16)
    hidden = matmul(normed_two, table["up_w"]) + table["up_b"].astype(jnp.float32)
    activated, slope = gelu_pair(hidden)
    result = mixed + (matmul(activated, table["down_w"]) + table["down_b"].astype(jnp.float32))
    return result, (normed_one, qkv, attended, mixed, normed_two, slope, activated)


def enc_backward(grad_out, table, inputs, ids, saved, pause, settle):
    normed_one, qkv, attended, mixed, normed_two, slope, activated = saved
    gains = table["norm_g"].astype(jnp.float32)
    shifts = table["norm_b"].astype(jnp.float32)
    down_grad = grad_out.astype(jnp.bfloat16)
    hidden_grad = (mul_trans(down_grad, table["down_w"]) * slope).astype(jnp.bfloat16)
    hidden_grad = pause(hidden_grad)
    mixed_part, gain_two, shift_two = norm_back(
        mixed, gains[1], shifts[1], mul_trans(hidden_grad, table["up_w"])
    )
    mixed_grad = group_rows(grad_out + mixed_part)
    branch_grad = mixed_grad.astype(jnp.bfloat16)
    attended_grad = mul_trans(branch_grad, table["out_w"]).astype(jnp.bfloat16)
    parts = attend_back(
        qkv[:, :D], qkv[:, D : 2 * D], qkv[:, 2 * D :], ids, ids, H, 0, attended_grad
    )
    qkv_grad = jnp.concatenate(parts, axis=1).astype(jnp.bfloat16)
    input_part, gain_one, shift_one = norm_back(
        inputs, gains[0], shifts[0], mul_trans(qkv_grad, table["qkv_w"])
    )
    patch_grad = settle((mixed_grad + input_part).astype(jnp.bfloat16))
    return (
        (patch_grad, qkv_grad, branch_grad, jnp.concatenate([hidden_grad, down_grad], axis=1)),
        (gain_one, shift_one, gain_two, shift_two),
    )


def core_side():
    return (lax.axis_index("grp") % 2).astype(jnp.int32).reshape(1)


def store_vector(target, first, lane, vector):
    width = vector.shape[1]
    done = 0
    while done < width:
        size = min(128 - lane, width - done)
        target[first : first + 1, lane : lane + size] = vector[:, done : done + size]
        done += size
        lane += size
        first, lane = first + lane // 128, lane % 128
    return first, lane


def column_sums(ref, first=0, width=None):
    width = ref.shape[1] if width is None else width
    cells = ref[:, first : first + width].astype(jnp.float32)
    return jnp.sum(cells, axis=0, keepdims=True)


def store_flat(target, product):
    rows, blocks = product.shape[0], product.shape[1] // 128
    for index in range(blocks):
        target[pl.ds(index, rows, stride=blocks), :] = product[:, index * 128 : (index + 1) * 128]


def column_blocks(ref, blocks):
    parts = [ref[:, pl.ds(pl.multiple_of(index * 128, 128), 128)] for index in blocks]
    return parts[0] if len(parts) == 1 else jnp.concatenate(parts, axis=1)


def steps_of(rows, size):
    return [(start, min(size, rows - start)) for start in range(0, rows, size)]


def enc_grad_kernel(plan, place_ref, *refs):
    norm_ref, own_norm_ref, out_ref, stage_ref, product_ref, small_ref, quarter_ref, sems = refs[
        -8:
    ]
    side, far = place_ref[0], place_ref[1]
    offset = 0
    flight = [None, None]
    turn = 0
    for size, left, first, depth, right, column, blocks in plan:
        x_ref, y_ref = refs[left], refs[right]
        if blocks % 2:
            columns = [2 * block + side for block in range(blocks)]
        else:
            columns = [4 * block + 2 * far + side for block in range(blocks // 2)]
        factor = column_blocks(y_ref, [column // 128 + block for block in columns])
        for start, rows in steps_of(depth, size):
            if flight[turn % 2] is not None:
                flight[turn % 2].wait()
            target = stage_ref.at[turn % 2]
            product = trans_mul(x_ref[:, first + start : first + start + rows], factor)
            if blocks % 2 == 0:
                store_flat(target, product)
            else:
                for block in range(blocks):
                    product_ref[block, :rows] = product[:, block * 128 : (block + 1) * 128]
                    odd = (far + block) % 2
                    target[
                        pl.ds((odd * blocks + block - far) // 2, rows // 2, stride=blocks), :
                    ] = product_ref.at[block][pl.ds(odd, rows // 2, stride=2), :]
            amount = rows * blocks // 2
            copy = pltpu.make_async_copy(
                target.at[pl.ds(0, amount)], out_ref.at[pl.ds(offset, amount)], sems.at[turn % 2]
            )
            copy.start()
            flight[turn % 2] = copy
            turn += 1
            offset += amount
    small_ref[...] = jnp.zeros_like(small_ref)
    spot = 0, 0
    for _, _, _, _, right, column, blocks in plan[:1] + plan[2:]:
        spot = store_vector(
            small_ref, *spot, column_sums(refs[right], column, blocks * 256)
        )
    rows = norm_ref.shape[0] // 4
    norms = sum(norm_ref[index * rows : (index + 1) * rows] for index in range(4))
    for vector in (
        own_norm_ref[0:1],
        norms[0:1],
        norms[1:2],
        own_norm_ref[1:2],
        norms[2:3],
        norms[3:4],
    ):
        spot = store_vector(small_ref, *spot, vector)
    rows = quarter_ref.shape[0]
    quarter_ref[...] = small_ref[pl.ds(side + 2 * far, rows, stride=4), :]
    last = pltpu.make_async_copy(quarter_ref, out_ref.at[pl.ds(offset, rows)], sems.at[2])
    last.start()
    for copy in [last] + flight:
        copy.wait()


def member_place():
    place = lax.axis_index("grp").astype(jnp.int32)
    return jnp.stack([place % 2, place // 2])


def enc_grad_quarter(inputs, grads, norms, own_norms, total_rows):
    count = len(inputs)
    plan = [
        (640, 0, 0, PATCH, count, 0, D // 256),
        (256, 1, 0, D, count + 1, 0, 3 * D // 256),
        (384, 2, 0, D, count + 2, 0, D // 256),
        (256, 2, D, D, count + 3, 0, F // 256),
        (768, 2, 2 * D, F, count + 3, F, D // 256),
    ]
    whole = pl.BlockSpec(memory_space=pltpu.VMEM)
    return pl.pallas_call(
        functools.partial(enc_grad_kernel, plan),
        in_specs=[pl.BlockSpec(memory_space=pltpu.SMEM)] + [whole] * (count + len(grads) + 2),
        out_specs=pl.BlockSpec(memory_space=pl.ANY),
        out_shape=jax.ShapeDtypeStruct((total_rows // 4, 128), jnp.float32),
        scratch_shapes=[
            pltpu.VMEM((2, 1536, 128), jnp.float32),
            pltpu.VMEM((9, 768, 128), jnp.float32),
            pltpu.VMEM((384, 128), jnp.float32),
            pltpu.VMEM((96, 128), jnp.float32),
            pltpu.SemaphoreType.DMA((3,)),
        ],
        compiler_params=pltpu.CompilerParams(vmem_limit_bytes=48 << 20),
        cost_estimate=pl.CostEstimate(
            flops=total_rows * 128 * inputs[0].shape[0],
            bytes_accessed=total_rows * 128,
            transcendentals=0,
        ),
    )(member_place(), *inputs, *grads, norms, own_norms)


def store_pixels(product_ref, targets):
    groups = product_ref.shape[1] // 4

    def load(row, block):
        return product_ref.at[block][pl.ds(row, groups, stride=4), :]

    def piece(row, block):
        if block < 13:
            return load(row, block)
        if block == 13:
            left, right = load(row, 13)[:, :64], load(row + 1, 0)[:, :64]
        else:
            left, right = load(row + 1, block - 14)[:, 64:], load(row + 1, block - 13)[:, :64]
        return jnp.concatenate([left, right], axis=1)

    for index in range(54):
        block = piece(0, index) if index < 27 else piece(2, index - 27)
        targets[index % 2][pl.ds(index // 2, groups, stride=27), :] = block


def dec_grad_kernel(plan, side_ref, *refs):
    norm_ref, mine_ref, theirs_ref, stage_ref, pixel_ref, small_ref, halves_ref, sems = refs[-8:]
    side = side_ref[0]
    flight = [None, None]
    turn = 0
    for index, (size, offset) in enumerate(plan):
        x_ref, y_ref = refs[2 * index], refs[2 * index + 1]
        pixels = y_ref.shape[1] % 256 != 0
        for start, rows in steps_of(x_ref.shape[1], size):
            product = trans_mul(x_ref[:, start : start + rows], y_ref[...])
            slot = turn % 2
            for copy in flight[slot] or ():
                copy.wait()
            if pixels:
                for block in range(14):
                    part = product[:, block * 128 : (block + 1) * 128]
                    pixel_ref[block, :, : part.shape[1]] = part
                store_pixels(pixel_ref, [stage_ref.at[slot, 0], stage_ref.at[slot, 1]])
            else:
                blocks = y_ref.shape[1] // 128
                for block in range(blocks):
                    stage_ref.at[slot, block % 2][
                        pl.ds(block // 2, rows, stride=blocks // 2), :
                    ] = product[:, block * 128 : (block + 1) * 128]
            amount = rows * y_ref.shape[1] // 256
            flight[slot] = [
                pltpu.make_async_copy(
                    stage_ref.at[slot, parity, pl.ds(0, amount)],
                    target.at[pl.ds(offset, amount)],
                    sems.at[slot, order],
                )
                for order, (parity, target) in enumerate(
                    ((side, mine_ref), (1 - side, theirs_ref))
                )
            ]
            for copy in flight[slot]:
                copy.start()
            offset += amount
            turn += 1
    small_ref[...] = jnp.zeros_like(small_ref)
    spot = store_vector(small_ref, 0, 0, column_sums(refs[1]))
    spot = store_vector(small_ref, *spot, norm_ref[0:1])
    for index in (2, 3, 4, 5):
        spot = store_vector(small_ref, *spot, column_sums(refs[2 * index + 1]))
    for index in range(1, norm_ref.shape[0]):
        spot = store_vector(small_ref, *spot, norm_ref[index : index + 1])
    rows = halves_ref.shape[1]
    for parity in range(2):
        halves_ref[parity] = small_ref[pl.ds(parity, rows, stride=2), :]
    last = [
        pltpu.make_async_copy(
            halves_ref.at[parity], target.at[pl.ds(target.shape[0] - rows, rows)], sems.at[2, order]
        )
        for order, (parity, target) in enumerate(((side, mine_ref), (1 - side, theirs_ref)))
    ]
    for copy in last:
        copy.start()
    for copy in last + flight[0] + flight[1]:
        copy.wait()


def dec_grad_halves(pairs, norms, total_rows):
    plan = [(256, 0), (256, 1536), (256, 4608), (256, 5632), (512, 9728), (512, 13824)]
    operands = [part for pair in pairs for part in pair]
    whole = pl.BlockSpec(memory_space=pltpu.VMEM)
    anywhere = pl.BlockSpec(memory_space=pl.ANY)
    shape = jax.ShapeDtypeStruct((total_rows // 2, 128), jnp.float32)
    return pl.pallas_call(
        functools.partial(dec_grad_kernel, plan),
        in_specs=[pl.BlockSpec(memory_space=pltpu.SMEM)] + [whole] * (len(operands) + 1),
        out_specs=[anywhere, anywhere],
        out_shape=[shape, shape],
        scratch_shapes=[
            pltpu.VMEM((2, 2, 3456, 128), jnp.float32),
            pltpu.VMEM((14, 512, 128), jnp.float32),
            pltpu.VMEM((256, 128), jnp.float32),
            pltpu.VMEM((2, 128, 128), jnp.float32),
            pltpu.SemaphoreType.DMA((3, 2)),
        ],
        compiler_params=pltpu.CompilerParams(vmem_limit_bytes=56 << 20),
        cost_estimate=pl.CostEstimate(
            flops=total_rows * 256 * pairs[1][0].shape[0],
            bytes_accessed=total_rows * 512,
            transcendentals=0,
        ),
    )(core_side(), *operands, norms)


def adamw_kernel(parts, with_average, place_ref, scalar_ref, *refs):
    count = 4 if with_average else 3
    ins, outs, grad_ref = refs[parts : parts + count], refs[parts + count : -1], refs[-1]
    for index in range(parts):
        rows = refs[index].shape[0]
        grad_ref[pl.ds(place_ref[index], rows, stride=parts), :] = refs[index][...]
    weights = ins[0][...]
    clipped = grad_ref[...] * scalar_ref[0]
    first_new = BETA_ONE * ins[1][...] + (1.0 - BETA_ONE) * clipped
    second_new = BETA_TWO * ins[2][...] + (1.0 - BETA_TWO) * clipped * clipped
    first_hat = first_new / scalar_ref[1]
    second_hat = second_new / scalar_ref[2]
    weights_new = weights * (1.0 - LEARN_RATE * WEIGHT_DECAY) - LEARN_RATE * first_hat / (
        jnp.sqrt(second_hat) + ADAM_EPS
    )
    outs[0][...] = weights_new
    outs[1][...] = first_new
    outs[2][...] = second_new
    outs[3][...] = weights_new.astype(jnp.bfloat16)
    if with_average:
        outs[4][...] = EMA_RATE * ins[3][...] + (1.0 - EMA_RATE) * weights_new


def adamw(parts, arrays, factor, steps_done):
    count = len(parts)
    place = lax.axis_index("grp")
    places = jnp.stack([(place ^ index) % count for index in range(count)])
    rows = arrays[0].shape[0]
    steps = 1
    for split in (2, 3, 4, 6, 8):
        if rows % (split * 8 * count) == 0:
            steps = split
    block = pl.BlockSpec((rows // steps, 128), lambda i: (i, 0))
    share = pl.BlockSpec((rows // steps // count, 128), lambda i: (i, 0))
    scalar = pl.BlockSpec(memory_space=pltpu.SMEM)
    scalars = jnp.stack([factor, 1.0 - BETA_ONE**steps_done, 1.0 - BETA_TWO**steps_done])
    full = jax.ShapeDtypeStruct((rows, 128), jnp.float32)
    shapes = [full, full, full, jax.ShapeDtypeStruct((rows, 128), jnp.bfloat16)]
    if len(arrays) == 4:
        shapes.append(full)
    return pl.pallas_call(
        functools.partial(adamw_kernel, count, len(arrays) == 4),
        grid=(steps,),
        in_specs=[scalar, scalar] + [share] * count + [block] * len(arrays),
        out_specs=[block] * len(shapes),
        out_shape=shapes,
        scratch_shapes=[pltpu.VMEM((rows // steps, 128), jnp.float32)],
        compiler_params=pltpu.CompilerParams(vmem_limit_bytes=40 << 20),
    )(places.astype(jnp.int32), scalars, *parts, *arrays)


def per_device(
    patches,
    segments,
    visible,
    enc_params,
    enc_first,
    enc_second,
    enc_average,
    dec_params,
    dec_first,
    dec_second,
    step_count,
):
    my_index = lax.axis_index("grp")
    slot_dev = segments.shape[0]
    rim = TILE_HI
    counts = jnp.sum((segments >= 0).astype(jnp.float32)) - visible.shape[0]
    total_count = total(jnp.full((8, 128), counts))[0, 0]
    enc_copy = gather_quarters(enc_params.astype(jnp.bfloat16))
    group_vis = group_rows(visible)
    group_seg = double(double(segments, 0, "grp", 2), 1, "grp", 1).reshape(-1)
    group_ids = group_seg[group_vis]
    key_ids = extended(segments + 3, rim) - 3
    local_slot = group_vis - my_index * slot_dev
    chosen = (
        local_slot[:, None] == jnp.arange(slot_dev, dtype=jnp.int32)[None, :]
    ).astype(jnp.bfloat16)
    seen = jnp.sum(chosen.astype(jnp.float32), axis=0) > 0.5
    enc_input = group_rows(own_rows(matmul(chosen, patches).astype(jnp.bfloat16)))
    enc_waves = sincos(group_vis % L, D)
    positions = (my_index * slot_dev + jnp.arange(slot_dev, dtype=jnp.int32)) % L
    dec_waves = sincos(positions, E)
    pixels = patches.astype(jnp.float32)
    pixel_mean = jnp.mean(pixels, axis=1, keepdims=True)
    centered = pixels - pixel_mean
    pixel_rate = lax.rsqrt(jnp.mean(centered * centered, axis=1, keepdims=True) + NORM_EPS)
    (
        enc_copy,
        enc_input,
        enc_waves,
        dec_waves,
        pixel_mean,
        pixel_rate,
        seen,
        group_ids,
        key_ids,
        chosen,
        total_count,
    ) = lax.optimization_barrier(
        (
            enc_copy,
            enc_input,
            enc_waves,
            dec_waves,
            pixel_mean,
            pixel_rate,
            seen,
            group_ids,
            key_ids,
            chosen,
            total_count,
        )
    )
    enc_copy, dec_shard = lax.optimization_barrier((enc_copy, dec_params))
    dec_copy = gather_quarters(dec_shard.astype(jnp.bfloat16))
    enc_table = unpack(enc_copy, enc_pieces(), ENC_STEPS)
    dec_table = unpack(dec_copy, dec_pieces(), DEC_STEPS)
    enc_start = (
        matmul(enc_input, enc_table["patch_w"])
        + enc_table["patch_b"].astype(jnp.float32)
        + enc_waves
    )

    own = visible.shape[0]
    enc_out, enc_saved = enc_forward(enc_start, enc_table, own, group_ids)
    enc_gain = enc_table["norm_g"].astype(jnp.float32)
    enc_shift = enc_table["norm_b"].astype(jnp.float32)
    enc_final = layer_norm(enc_out, enc_gain[2], enc_shift[2]).astype(jnp.bfloat16)
    latent = (
        matmul(enc_final, dec_table["embed_w"]) + dec_table["embed_b"].astype(jnp.float32)
    ).astype(jnp.bfloat16)
    group_latent = group_rows(latent)
    enc_inputs = jnp.concatenate([enc_saved[2], enc_saved[4], enc_saved[6]], axis=1)
    group_latent, enc_inputs = lax.optimization_barrier((group_latent, enc_inputs))
    group_inputs = group_rows(enc_inputs)
    placed = trans_mul(chosen, group_latent)
    dec_start = jnp.where(
        seen[:, None], placed, dec_table["mask_token"].astype(jnp.float32)[None, :]
    ) + dec_waves
    counted = jnp.where((segments >= 0) & jnp.logical_not(seen), 1.0, 0.0)

    def dec_share(pair):
        joined = extended(jnp.concatenate(pair, axis=1), rim)
        return (joined[:, :E], joined[:, E:])

    dec_out, dec_saved = block_forward(
        dec_start, dec_table, EH, rim, segments, key_ids, dec_share
    )
    dec_gain = dec_table["norm_g"].astype(jnp.float32)
    dec_shift = dec_table["norm_b"].astype(jnp.float32)
    dec_final = layer_norm(dec_out, dec_gain[2], dec_shift[2]).astype(jnp.bfloat16)
    predicted = matmul(dec_final, dec_table["pix_w"]) + dec_table["pix_b"].astype(jnp.float32)
    target = (patches.astype(jnp.float32) - pixel_mean) * pixel_rate
    errors = predicted - target
    loss_part = jnp.sum(counted * jnp.mean(errors * errors, axis=1))
    errors, group_inputs = lax.optimization_barrier((errors, group_inputs))
    pred_grad = (counted[:, None] * errors * (2.0 / PATCH) / total_count).astype(jnp.bfloat16)
    dec_out_grad, dec_gain_last, dec_shift_last = norm_back(
        dec_out, dec_gain[2], dec_shift[2], mul_trans(pred_grad, dec_table["pix_w"])
    )
    start_grad, dec_small, dec_pairs = block_backward(
        dec_out_grad, dec_table, EH, rim, segments, key_ids, dec_saved
    )
    mask_grad = jnp.sum(jnp.where(seen[:, None], 0.0, start_grad), axis=0)
    latent_grad = own_rows(matmul(chosen, start_grad.astype(jnp.bfloat16)).astype(jnp.bfloat16))
    dec_pairs["embed_w"] = (enc_final, latent_grad)
    dec_pairs["pix_w"] = (dec_final, pred_grad)
    mine, theirs = dec_grad_halves(
        [dec_pairs[name] for name in ("embed_w", "qkv_w", "out_w", "up_w", "down_w", "pix_w")],
        jnp.stack(
            [
                mask_grad,
                dec_small[0],
                dec_small[2],
                dec_gain_last,
                dec_small[1],
                dec_small[3],
                dec_shift_last,
            ]
        ),
        DR,
    )
    arrived = swap(theirs, "grp", 1)
    latent_grad, mine = lax.optimization_barrier((latent_grad, mine))
    dec_blocks = None

    def enc_pause(grad):
        nonlocal dec_blocks
        grad, dec_half = lax.optimization_barrier((grad, mine + arrived))
        dec_blocks = reduce_first(dec_half, dec_routes(), (0.5,))
        return grad

    def enc_settle(grad):
        nonlocal dec_blocks
        grad, dec_blocks = lax.optimization_barrier((grad, dec_blocks))
        return grad

    enc_out_grad, enc_gain_last, enc_shift_last = norm_back(
        enc_out, enc_gain[2], enc_shift[2], mul_trans(latent_grad, dec_table["embed_w"])
    )
    enc_grads, enc_small = enc_backward(
        enc_out_grad, enc_table, enc_start, group_ids, enc_saved, enc_pause, enc_settle
    )
    enc_norms = jnp.stack([enc_small[2], enc_gain_last, enc_small[3], enc_shift_last])
    branch_grad, far_grad, enc_norms = lax.optimization_barrier(
        (enc_grads[2], enc_grads[3], enc_norms)
    )
    enc_quarter = enc_grad_quarter(
        [enc_input, enc_saved[0], group_inputs],
        [*enc_grads[:2], branch_grad, group_rows(far_grad)],
        group_rows(enc_norms),
        jnp.stack([enc_small[0], enc_small[1]]),
        ER,
    )
    enc_blocks = reduce_first(enc_quarter, dp_routes(), (0.5,))
    dec_blocks = reduce_rest(dec_blocks, dec_routes(), 1, 2)
    enc_sum = reduce_rest(enc_blocks, dp_routes())
    enc_sum, dec_blocks = lax.optimization_barrier((enc_sum, dec_blocks))
    enc_own = jnp.concatenate(enc_sum, axis=0)
    enc_across = swap(enc_own, "grp", 2)
    dec_sum = reduce_rest(dec_blocks, dec_routes(), 2)
    squares = sum(jnp.sum(part * part) for part in enc_sum + dec_sum)
    lane = lax.broadcasted_iota(jnp.int32, (8, 128), 1)
    sums = total(jnp.where(lane == 0, squares, jnp.where(lane == 1, loss_part, 0.0)))
    dec_wide = [double(piece, 0, "grp", 2).reshape(-1, 128) for piece in dec_sum]
    enc_quarters = (
        enc_own,
        swap(enc_own, "grp", 1),
        enc_across,
        swap(enc_across, "grp", 1),
    )
    dec_mine = jnp.concatenate(dec_wide, axis=0)
    dec_halves = dec_mine, swap(dec_mine, "grp", 1)
    loss_total = sums[0, 1]
    grad_norm = jnp.sqrt(sums[0, 0])
    factor = jnp.minimum(1.0, CLIP_LIMIT / (grad_norm + NORM_EPS))
    steps_done = step_count[0].astype(jnp.float32)
    enc_new, enc_first_new, enc_second_new, enc_copy_new, average_new = adamw(
        enc_quarters, (enc_params, enc_first, enc_second, enc_average), factor, steps_done
    )
    dec_new, dec_first_new, dec_second_new, dec_copy_new = adamw(
        dec_halves, (dec_params, dec_first, dec_second), factor, steps_done
    )
    return (
        enc_new,
        enc_first_new,
        enc_second_new,
        enc_copy_new,
        dec_new,
        dec_first_new,
        dec_second_new,
        dec_copy_new,
        average_new,
        grad_norm,
        loss_total,
        total_count,
    )


def solution(mesh):
    placed = (
        P(("dp", "grp"), None),
        P(("dp", "grp")),
        P(("dp", "grp")),
        P("dp", None),
        P("dp", None),
        P("dp", None),
        P("dp", None),
        P("dp", None),
        P("dp", None),
        P("dp", None),
        P(),
    )
    return jax.shard_map(
        per_device,
        mesh=mesh,
        in_specs=placed,
        out_specs=(
            P("dp", None),
            P("dp", None),
            P("dp", None),
            P("dp", None),
            P("dp", None),
            P("dp", None),
            P("dp", None),
            P("dp", None),
            P("dp", None),
            P(),
            P(),
            P(),
        ),
        check_vma=False,
    )
```

```python
import functools
import math

import jax
import jax.numpy as jnp
from jax import lax
from jax.experimental import pallas as pl
from jax.experimental.pallas import tpu as pltpu
from jax.sharding import PartitionSpec as P

D = 768
H = 12
F = 3072
E = 512
EH = 16
FE = 2048
PATCH = 1728
L = 1728
TILE_HI = 192
ER = 66048
DR = 34816


NORM_EPS = 1e-06
MASK_FILL = -1e30
CLIP_LIMIT = 0.0002
LEARN_RATE = 0.02
BETA_ONE = 0.5
BETA_TWO = 0.5
ADAM_EPS = 1e-08
WEIGHT_DECAY = 0.05
EMA_RATE = 0.9


def swap(block, axis, bit):
    count = lax.axis_size(axis)
    return lax.ppermute(block, axis, [(i, i ^ bit) for i in range(count)])


def bit_of(axis, bit):
    return (lax.axis_index(axis) // bit) % 2


def double(block, dim, axis, bit):
    mine = bit_of(axis, bit)
    other = swap(block, axis, bit)
    first = jnp.where(mine == 0, block, other)
    second = jnp.where(mine == 0, other, block)
    return jnp.stack([first, second], axis=dim)


def total(values):
    for axis in ("grp", "dp"):
        bit = 1
        while bit < lax.axis_size(axis):
            values = values + swap(values, axis, bit)
            bit *= 2
    return values


def dp_bits():
    bits = [1]
    while bits[-1] * 2 < lax.axis_size("dp"):
        bits.append(bits[-1] * 2)
    return bits


def cut(rows, shares):
    unit = 16 if rows % 16 == 0 else 2
    sizes = [int(round(rows // unit * share)) * unit for share in shares]
    return sizes + [rows - sum(sizes)]


def gather_quarters(shard):
    part = shard.shape[0] // 4
    quarter = lax.dynamic_slice_in_dim(shard, lax.axis_index("grp") * part, part, 0)
    return lax.all_gather(quarter, ("dp", "grp"), axis=0, tiled=True)


def section(cells, dim, start, size):
    return lax.dynamic_slice_in_dim(cells, start, size, dim)


def reduce_bit(cells, dim, axis, bit, start=0, size=None):
    half = (cells.shape[dim] if size is None else size) // 2
    mine = bit_of(axis, bit)
    sent = section(cells, dim, start + (1 - mine) * half, half)
    return section(cells, dim, start + mine * half, half) + swap(sent, axis, bit)


def dec_routes():
    bits = [("dp", bit) for bit in dp_bits()]
    return [bits[:1] + [("grp", 2)] + bits[1:], bits[1:2] + [("grp", 2)] + bits[2:] + bits[:1]]


def reduce_first(half, routes, shares):
    shards = lax.axis_size("dp")
    half_rows = half.shape[0] // shards
    bits = dp_bits()
    names = [("dp", bit) for bit in reversed(bits)]
    cells = half.reshape([2] * len(bits) + [half_rows, 128])
    blocks = []
    start = 0
    for route, rows in zip(routes, cut(half_rows, shares)):
        axis, bit = route[0]
        if axis == "grp":
            block = reduce_bit(cells, len(bits), axis, bit, start, rows)
        else:
            dim = names.index(route[0])
            mine = bit_of(axis, bit)

            def pick(index, dim=dim, start=start, rows=rows):
                corner = [0] * dim + [index] + [0] * (len(bits) - dim - 1) + [start, 0]
                sizes = [2] * dim + [1] + [2] * (len(bits) - dim - 1) + [rows, 128]
                return lax.dynamic_slice(cells, corner, sizes)

            block = pick(mine) + swap(pick(1 - mine), axis, bit)
        blocks.append(block)
        start += rows
    return blocks


def reduce_rest(blocks, routes, first=1, last=None):
    bits = dp_bits()
    names = [("dp", bit) for bit in reversed(bits)]
    blocks = list(blocks)
    for step in range(first, len(routes[0]) if last is None else last):
        for index, route in enumerate(routes):
            axis, bit = route[step]
            dim = len(bits) if axis == "grp" else names.index(route[step])
            blocks[index] = reduce_bit(blocks[index], dim, axis, bit)
    if last is not None:
        return blocks
    return [block.reshape(-1, 128) for block in blocks]


def dp_routes():
    bits = [("dp", bit) for bit in dp_bits()]
    return [bits, bits[1:] + bits[:1]]


def spread_pieces(pieces):
    wide = [double(piece, 0, "grp", 2).reshape(-1, 128) for piece in pieces]
    mine = jnp.concatenate(wide, axis=0)
    return mine, swap(mine, "grp", 1)


def group_rows(block):
    across = swap(block, "grp", 2)
    near, far = (
        swap(block, "grp", 1),
        swap(across, "grp", 1),
    )
    return jnp.concatenate([block, near, across, far], axis=0)


def own_rows(blocks):
    count = blocks.shape[0] // 4
    parts = [lax.slice_in_dim(blocks, i * count, (i + 1) * count, axis=0) for i in range(4)]
    sent = jnp.concatenate([parts[1], parts[3]], axis=0)
    arrived = swap(sent, "grp", 1)
    kept = parts[0] + arrived[:count]
    other = parts[2] + arrived[count:]
    return kept + swap(other, "grp", 2)


def extended(cells, width):
    count = lax.axis_size("grp")
    ends = count - 1
    head = cells[:width]
    tail = cells[cells.shape[0] - width :]
    return jnp.concatenate(
        [
            lax.ppermute(tail, "grp", [(i, i + 1) for i in range(ends)]),
            cells,
            lax.ppermute(head, "grp", [(i + 1, i) for i in range(ends)]),
        ],
        axis=0,
    )


def passed_along(block, axis, distance):
    devices = range(lax.axis_size(axis))
    route = [(i - distance, i) for i in devices if i - distance in devices]
    return lax.ppermute(block, axis, route)


def enc_pieces():
    return [
        ("patch_w", (PATCH, D)),
        ("qkv_w", (D, 3 * D)),
        ("out_w", (D, D)),
        ("up_w", (D, F)),
        ("down_w", (F, D)),
        ("patch_b", (D,)),
        ("out_b", (D,)),
        ("up_b", (F,)),
        ("down_b", (D,)),
        ("norm_g", (3, D)),
        ("norm_b", (3, D)),
    ]


def dec_pieces():
    return [
        ("embed_w", (D, E)),
        ("qkv_w", (E, 3 * E)),
        ("out_w", (E, E)),
        ("up_w", (E, FE)),
        ("down_w", (FE, E)),
        ("pix_w", (E, PATCH)),
        ("embed_b", (E,)),
        ("mask_token", (E,)),
        ("out_b", (E,)),
        ("up_b", (FE,)),
        ("down_b", (E,)),
        ("pix_b", (PATCH,)),
        ("norm_g", (3, E)),
        ("norm_b", (3, E)),
    ]


def relayout_kernel(plan, *refs):
    source, outs = refs[0], refs[1 : 1 + len(plan)]
    raw_ref, wide_ref, stages, in_sems, out_sems = (
        refs[1 + len(plan)],
        refs[2 + len(plan)],
        refs[3 + len(plan) : -2],
        refs[-2],
        refs[-1],
    )
    steps = [
        (index, offset + start * blocks, start, rows, blocks)
        for index, (offset, depth, blocks, rows) in enumerate(plan)
        for start in range(0, depth, rows)
    ]

    def fetch(turn):
        _, offset, _, rows, blocks = steps[turn]
        return pltpu.make_async_copy(
            source.at[pl.ds(offset, rows * blocks)],
            raw_ref.at[turn % 2, pl.ds(0, rows * blocks)],
            in_sems.at[turn % 2],
        )

    flight = {}
    fetch(0).start()
    for turn, (index, _, start, rows, blocks) in enumerate(steps):
        if turn + 1 < len(steps):
            fetch(turn + 1).start()
        fetch(turn).wait()
        wide_ref[: rows * blocks, :] = raw_ref[turn % 2, : rows * blocks, :].astype(jnp.float32)
        slot = turn % 2
        if slot in flight:
            flight.pop(slot).wait()
        stage = stages[index].at[slot]
        for block in range(blocks):
            stage[:, block * 128 : (block + 1) * 128] = wide_ref[
                pl.ds(block, rows, stride=blocks), :
            ].astype(jnp.bfloat16)
        flight[slot] = pltpu.make_async_copy(
            stage, outs[index].at[pl.ds(start, rows)], out_sems.at[slot]
        )
        flight[slot].start()
    for copy in flight.values():
        copy.wait()


def relayout(rows, plan):
    anywhere = pl.BlockSpec(memory_space=pl.ANY)
    most = max(step * blocks for _, _, blocks, step in plan)
    return pl.pallas_call(
        functools.partial(relayout_kernel, plan),
        in_specs=[anywhere],
        out_specs=[anywhere] * len(plan),
        out_shape=[
            jax.ShapeDtypeStruct((depth, blocks * 128), jnp.bfloat16)
            for _, depth, blocks, _ in plan
        ],
        scratch_shapes=[
            pltpu.VMEM((2, most, 128), jnp.bfloat16),
            pltpu.VMEM((most, 128), jnp.float32),
        ]
        + [pltpu.VMEM((2, step, blocks * 128), jnp.bfloat16) for _, _, blocks, step in plan]
        + [pltpu.SemaphoreType.DMA((2,)), pltpu.SemaphoreType.DMA((2,))],
        compiler_params=pltpu.CompilerParams(vmem_limit_bytes=40 << 20),
        cost_estimate=pl.CostEstimate(
            flops=0, bytes_accessed=rows.size * 4, transcendentals=0
        ),
    )(rows)


ENC_STEPS = {"patch_w": 576, "qkv_w": 192, "out_w": 384, "up_w": 128, "down_w": 512}
DEC_STEPS = {"embed_w": 768, "qkv_w": 256, "out_w": 512, "up_w": 128, "down_w": 512}


def unpack(rows, pieces, steps):
    table = {}
    offset = 0
    plan = []
    vectors = sum(1 for _, dims in pieces if len(dims) == 2 and dims[0] > 3)
    for piece_name, piece_dims in pieces[:vectors]:
        amount = math.prod(piece_dims) // 128
        if piece_name in steps:
            plan.append((offset, piece_dims[0], piece_dims[1] // 128, steps[piece_name]))
        else:
            table[piece_name] = rows[offset : offset + amount].reshape(piece_dims)
        offset += amount
    small = rows[offset:].reshape(-1)
    table.update(zip(steps, relayout(rows, plan)))
    offset = 0
    for piece_name, piece_dims in pieces[vectors:]:
        amount = math.prod(piece_dims)
        table[piece_name] = small[offset : offset + amount].reshape(piece_dims)
        offset += amount
    return table


def matmul(left, right):
    return jnp.dot(left, right, preferred_element_type=jnp.float32)


def mul_trans(left, right):
    return lax.dot_general(
        left, right, (((1,), (1,)), ((), ())), preferred_element_type=jnp.float32
    )


def trans_mul(left, right):
    return lax.dot_general(
        left, right, (((0,), (0,)), ((), ())), preferred_element_type=jnp.float32
    )


def sincos(positions, width):
    half_width = width // 2
    freq_row = jnp.exp(
        jnp.arange(half_width, dtype=jnp.float32) * (-2.0 * math.log(10000.0) / width)
    )
    angles = positions.astype(jnp.float32)[:, None] * freq_row[None, :]
    return jnp.concatenate([jnp.sin(angles), jnp.cos(angles)], axis=1)


def layer_norm(inputs, gain, shift):
    center = inputs - jnp.mean(inputs, axis=-1, keepdims=True)
    return (
        center * lax.rsqrt(jnp.mean(center * center, axis=-1, keepdims=True) + NORM_EPS) * gain
        + shift
    )


def norm_back(inputs, gain, shift, grad_out):
    outputs, pull = jax.vjp(layer_norm, inputs, gain, shift)
    return pull(grad_out)


def exact_gelu(values):
    return jax.nn.gelu(values, approximate=False)


BLOCK = 128


def head_masks(width):
    lanes = lax.broadcasted_iota(jnp.int32, (1, 128), 1) // width
    return [(lanes == index).astype(jnp.float32) for index in range(128 // width)]


def spread_heads(cells, masks):
    wide = cells.astype(jnp.float32)
    return jnp.concatenate([(wide * mask).astype(jnp.bfloat16) for mask in masks], axis=0)


TILE = 32
TALL = 64


def attend_kernel(
    window,
    stride,
    width,
    q_ref,
    k_ref,
    v_ref,
    qid_ref,
    kid_ref,
    o_ref,
    bias_ref,
    score_ref,
    prob_ref,
):
    start = pl.multiple_of(pl.program_id(0) * stride, BLOCK)
    scale = width ** (-0.5)
    masks = head_masks(width)
    near = pl.ds(start, window)
    bias_ref[...] = jnp.where(qid_ref[...] == kid_ref[:, near], 0.0, MASK_FILL)
    for group in range(q_ref.shape[1] // 128):
        lanes = slice(group * 128, (group + 1) * 128)
        slot = group % 2
        score_ref[slot] = mul_trans(spread_heads(q_ref[:, lanes], masks), k_ref[near, lanes])
        for first in range(0, len(masks) * BLOCK, TILE):
            rows = slice(first, first + TILE)
            row = first % BLOCK
            part = score_ref[slot, rows, :] * scale + bias_ref[row : row + TILE, :]
            powers = jnp.exp(part - jnp.max(part, axis=1, keepdims=True))
            probs = powers * (1.0 / jnp.sum(powers, axis=1, keepdims=True))
            prob_ref[slot, rows, :] = probs.astype(jnp.bfloat16)
        wide = matmul(prob_ref[slot], v_ref[near, lanes])
        o_ref[:, lanes] = pick_heads(wide, masks).astype(jnp.bfloat16)


def pick_heads(wide, masks):
    return sum(wide[i * BLOCK : (i + 1) * BLOCK] * mask for i, mask in enumerate(masks))


def row_sums(cells, merge):
    return merge(cells.reshape(-1, 8, cells.shape[1]), axis=0)


def attend_back_kernel(window, stride, width, pick, *refs):
    q_ref, g_ref, k_ref, v_ref, qid_ref, kid_ref = refs[:6]
    dq_ref, both_ref, bias_ref, score_ref, grad_ref, prob_ref, back_ref = refs[-7:]
    before = refs[6:-7]
    columns = q_ref.shape[1]
    step = pl.program_id(0)
    start = pl.multiple_of(pick(step) * stride, BLOCK)
    scale = width ** (-0.5)
    masks = head_masks(width)

    @pl.when(step == 0)
    def _():
        both_ref[...] = before[0][...] if before else jnp.zeros_like(both_ref)

    near = pl.ds(start, window)
    bias_ref[...] = jnp.where(kid_ref[near, :] == qid_ref[...], 0.0, MASK_FILL)
    tiles = [slice(first, first + TALL) for first in range(0, window, TALL)]
    for group in range(q_ref.shape[1] // 128):
        lanes = slice(group * 128, (group + 1) * 128)
        slot = group % 2
        keys = k_ref[near, lanes]
        queries = spread_heads(q_ref[:, lanes], masks)
        outs = spread_heads(g_ref[:, lanes], masks)
        score_ref[slot] = mul_trans(keys, queries)
        grad_ref[slot] = mul_trans(v_ref[near, lanes], outs)
        for index in range(len(masks)):
            head = slice(index * BLOCK, (index + 1) * BLOCK)
            top = None
            for tile in tiles:
                part = score_ref[slot, tile, head] * scale + bias_ref[tile, :]
                score_ref[slot, tile, head] = part
                most = row_sums(part, jnp.max)
                top = most if top is None else jnp.maximum(top, most)
            top = jnp.max(top, axis=0, keepdims=True)
            whole = jnp.zeros((8, BLOCK), jnp.float32)
            for tile in tiles:
                powers = jnp.exp(score_ref[slot, tile, head] - top)
                score_ref[slot, tile, head] = powers
                whole += row_sums(powers, jnp.sum)
            inverse = 1.0 / jnp.sum(whole, axis=0, keepdims=True)
            shared = jnp.zeros((8, BLOCK), jnp.float32)
            for tile in tiles:
                probs = score_ref[slot, tile, head] * inverse
                prob_ref[slot, tile, head] = probs.astype(jnp.bfloat16)
                shared += row_sums(probs * grad_ref[slot, tile, head], jnp.sum)
            shared = jnp.sum(shared, axis=0, keepdims=True)
            for tile in tiles:
                probs = score_ref[slot, tile, head] * inverse
                back_ref[slot, tile, head] = (
                    probs * (grad_ref[slot, tile, head] - shared)
                ).astype(jnp.bfloat16)
        back = back_ref[slot]
        far_lanes = slice(columns + group * 128, columns + (group + 1) * 128)
        both_ref[near, far_lanes] += matmul(prob_ref[slot], outs)
        both_ref[near, lanes] += matmul(back, queries) * scale
        dq_ref[:, lanes] = pick_heads(trans_mul(back, keys), masks) * scale


def padded(cells, rows, fill=0):
    return jnp.pad(
        cells, [(0, rows - cells.shape[0])] + [(0, 0)] * (cells.ndim - 1), constant_values=fill
    )


def attend_sizes(query, keys, rim):
    steps = -(-query.shape[0] // BLOCK)
    if rim:
        return steps, BLOCK + 2 * rim, steps * BLOCK + 2 * rim, BLOCK
    return steps, keys.shape[0], keys.shape[0], 0


def whole_spec(dims):
    return pl.BlockSpec(dims, lambda i: (0, 0))


def step_spec(columns):
    return pl.BlockSpec((BLOCK, columns), lambda i: (i, 0))


def attend(query, keys, values, query_ids, key_ids, heads, rim):
    count, columns = query.shape
    steps, window, span, stride = attend_sizes(query, keys, rim)
    stack = 128 * heads // columns * BLOCK
    outcome = pl.pallas_call(
        functools.partial(attend_kernel, window, stride, columns // heads),
        grid=(steps,),
        in_specs=[
            step_spec(columns),
            whole_spec((span, columns)),
            whole_spec((span, columns)),
            step_spec(1),
            whole_spec((1, span)),
        ],
        out_specs=step_spec(columns),
        out_shape=jax.ShapeDtypeStruct((steps * BLOCK, columns), jnp.bfloat16),
        scratch_shapes=[
            pltpu.VMEM((BLOCK, window), jnp.float32),
            pltpu.VMEM((2, stack, window), jnp.float32),
            pltpu.VMEM((2, stack, window), jnp.bfloat16),
        ],
        compiler_params=pltpu.CompilerParams(vmem_limit_bytes=48 << 20),
        cost_estimate=pl.CostEstimate(
            flops=4 * steps * BLOCK * window * columns,
            bytes_accessed=8 * span * columns,
            transcendentals=steps * BLOCK * window * heads,
        ),
    )(
        padded(query, steps * BLOCK),
        padded(keys, span),
        padded(values, span),
        padded(query_ids, steps * BLOCK, -4)[:, None],
        padded(key_ids, span, -5)[None, :],
    )
    return outcome[:count]


def same_step(step):
    return step


def attend_back(
    query, keys, values, query_ids, key_ids, heads, rim, out_grad, steps=None, pick=same_step, before=()
):
    count, columns = query.shape
    all_steps, window, span, stride = attend_sizes(query, keys, rim)
    steps = all_steps if steps is None else steps
    stack = 128 * heads // columns * BLOCK
    block = pl.BlockSpec((BLOCK, columns), lambda i: (pick(i), 0))
    return pl.pallas_call(
        functools.partial(attend_back_kernel, window, stride, columns // heads, pick),
        grid=(steps,),
        in_specs=[
            block,
            block,
            whole_spec((span, columns)),
            whole_spec((span, columns)),
            pl.BlockSpec((1, BLOCK), lambda i: (0, pick(i))),
            whole_spec((span, 1)),
        ]
        + ([whole_spec((span, 2 * columns)), pl.BlockSpec(memory_space=pl.ANY)] if before else []),
        out_specs=[block, whole_spec((span, 2 * columns))],
        out_shape=[
            jax.ShapeDtypeStruct((all_steps * BLOCK, columns), jnp.float32),
            jax.ShapeDtypeStruct((span, 2 * columns), jnp.float32),
        ],
        input_output_aliases={7: 0} if before else {},
        scratch_shapes=[
            pltpu.VMEM((window, BLOCK), jnp.float32),
            pltpu.VMEM((2, window, stack), jnp.float32),
            pltpu.VMEM((2, window, stack), jnp.float32),
            pltpu.VMEM((2, window, stack), jnp.bfloat16),
            pltpu.VMEM((2, window, stack), jnp.bfloat16),
        ],
        compiler_params=pltpu.CompilerParams(vmem_limit_bytes=48 << 20),
        cost_estimate=pl.CostEstimate(
            flops=80 * steps * BLOCK * window * columns,
            bytes_accessed=20 * span * columns,
            transcendentals=steps * BLOCK * window * heads,
        ),
    )(
        padded(query, all_steps * BLOCK),
        padded(out_grad, all_steps * BLOCK),
        padded(keys, span),
        padded(values, span),
        padded(query_ids, all_steps * BLOCK, -4)[None, :],
        padded(key_ids, span, -5)[:, None],
        *before,
    )


def attend_back_slots(query, keys, values, query_ids, key_ids, heads, rim, out_grad):
    count = query.shape[0]
    steps, window, _, _ = attend_sizes(query, keys, rim)
    low = -(-rim // BLOCK)
    high = next(i for i in range(low, steps) if i * BLOCK + window > rim + count)
    args = (query, keys, values, query_ids, key_ids, heads, rim, out_grad)
    edges = attend_back(
        *args, steps=low + steps - high, pick=lambda i: i + (i // low) * (high - low)
    )
    from_upper = passed_along(edges[1][:rim], "grp", -1)
    from_lower = passed_along(edges[1][rim + count : 2 * rim + count], "grp", 1)
    inner = attend_back(
        *args, steps=high - low, pick=lambda i: i + low, before=(edges[1], edges[0])
    )
    rims = jnp.pad(from_lower, ((0, count - rim), (0, 0))) + jnp.pad(
        from_upper, ((count - rim, 0), (0, 0))
    )
    middle = (inner[1][rim : rim + count] + rims).astype(jnp.bfloat16)
    query_grad = inner[0][:count].astype(jnp.bfloat16)
    return jnp.concatenate([query_grad, middle], axis=1)


def gelu_pair(hidden):
    below = 0.5 * (1.0 + lax.erf(hidden * math.sqrt(0.5)))
    bell = jnp.exp(-0.5 * hidden * hidden) * (1.0 / math.sqrt(2.0 * math.pi))
    return lax.optimization_barrier(
        ((hidden * below).astype(jnp.bfloat16), below + hidden * bell)
    )


def block_forward(inputs, table, heads, rim, query_ids, key_ids, share_keys):
    gains = table["norm_g"].astype(jnp.float32)
    shifts = table["norm_b"].astype(jnp.float32)
    width = inputs.shape[1]
    normed_one = layer_norm(inputs, gains[0], shifts[0]).astype(jnp.bfloat16)
    qkv = matmul(normed_one, table["qkv_w"]).astype(jnp.bfloat16)
    query = qkv[:, :width]
    all_keys, all_values = share_keys((qkv[:, width : 2 * width], qkv[:, 2 * width :]))
    attended = attend(query, all_keys, all_values, query_ids, key_ids, heads, rim)
    mixed = inputs + (matmul(attended, table["out_w"]) + table["out_b"].astype(jnp.float32))
    normed_two = layer_norm(mixed, gains[1], shifts[1]).astype(jnp.bfloat16)
    hidden = matmul(normed_two, table["up_w"]) + table["up_b"].astype(jnp.float32)
    activated, slope = gelu_pair(hidden)
    result = mixed + (matmul(activated, table["down_w"]) + table["down_b"].astype(jnp.float32))
    saved = (
        inputs,
        normed_one,
        query,
        all_keys,
        all_values,
        attended,
        mixed,
        normed_two,
        slope,
        activated,
    )
    return (result, saved)


def block_backward(
    grad_out, table, heads, rim, query_ids, key_ids, saved
):
    (
        inputs,
        normed_one,
        query,
        all_keys,
        all_values,
        attended,
        mixed,
        normed_two,
        slope,
        activated,
    ) = saved
    gains = table["norm_g"].astype(jnp.float32)
    shifts = table["norm_b"].astype(jnp.float32)
    pairs = {}
    down_grad = grad_out.astype(jnp.bfloat16)
    pairs["down_w"] = (activated, down_grad)
    act_grad = mul_trans(down_grad, table["down_w"])
    hidden_grad = (act_grad * slope).astype(jnp.bfloat16)
    pairs["up_w"] = (normed_two, hidden_grad)
    mixed_part, gain_two, shift_two = norm_back(
        mixed, gains[1], shifts[1], mul_trans(hidden_grad, table["up_w"])
    )
    mixed_grad = grad_out + mixed_part
    branch_grad = mixed_grad.astype(jnp.bfloat16)
    pairs["out_w"] = (attended, branch_grad)
    attended_grad = mul_trans(branch_grad, table["out_w"]).astype(jnp.bfloat16)
    qkv_grad = attend_back_slots(
        query, all_keys, all_values, query_ids, key_ids, heads, rim, attended_grad
    )
    pairs["qkv_w"] = (normed_one, qkv_grad)
    input_part, gain_one, shift_one = norm_back(
        inputs, gains[0], shifts[0], mul_trans(qkv_grad, table["qkv_w"])
    )
    return (mixed_grad + input_part, (gain_one, shift_one, gain_two, shift_two), pairs)


def enc_forward(inputs, table, own, ids):
    gains = table["norm_g"].astype(jnp.float32)
    shifts = table["norm_b"].astype(jnp.float32)
    normed_one = layer_norm(inputs, gains[0], shifts[0]).astype(jnp.bfloat16)
    qkv = matmul(normed_one, table["qkv_w"]).astype(jnp.bfloat16)
    attended = attend(
        qkv[:own, :D], qkv[:, D : 2 * D], qkv[:, 2 * D :], ids[:own], ids, H, 0
    )
    mixed = inputs[:own] + (matmul(attended, table["out_w"]) + table["out_b"].astype(jnp.float32))
    normed_two = layer_norm(mixed, gains[1], shifts[1]).astype(jnp.bfloat16)
    hidden = matmul(normed_two, table["up_w"]) + table["up_b"].astype(jnp.float32)
    activated, slope = gelu_pair(hidden)
    result = mixed + (matmul(activated, table["down_w"]) + table["down_b"].astype(jnp.float32))
    return result, (normed_one, qkv, attended, mixed, normed_two, slope, activated)


def enc_backward(grad_out, table, inputs, ids, saved, pause):
    normed_one, qkv, attended, mixed, normed_two, slope, activated = saved
    gains = table["norm_g"].astype(jnp.float32)
    shifts = table["norm_b"].astype(jnp.float32)
    down_grad = grad_out.astype(jnp.bfloat16)
    hidden_grad = (mul_trans(down_grad, table["down_w"]) * slope).astype(jnp.bfloat16)
    hidden_grad = pause(hidden_grad)
    mixed_part, gain_two, shift_two = norm_back(
        mixed, gains[1], shifts[1], mul_trans(hidden_grad, table["up_w"])
    )
    mixed_grad = group_rows(grad_out + mixed_part)
    branch_grad = mixed_grad.astype(jnp.bfloat16)
    attended_grad = mul_trans(branch_grad, table["out_w"]).astype(jnp.bfloat16)
    parts = attend_back(
        qkv[:, :D], qkv[:, D : 2 * D], qkv[:, 2 * D :], ids, ids, H, 0, attended_grad
    )
    qkv_grad = jnp.concatenate(parts, axis=1).astype(jnp.bfloat16)
    input_part, gain_one, shift_one = norm_back(
        inputs, gains[0], shifts[0], mul_trans(qkv_grad, table["qkv_w"])
    )
    patch_grad = (mixed_grad + input_part).astype(jnp.bfloat16)
    return (
        (patch_grad, qkv_grad, branch_grad, jnp.concatenate([hidden_grad, down_grad], axis=1)),
        (gain_one, shift_one, gain_two, shift_two),
    )


def core_side():
    return (lax.axis_index("grp") % 2).astype(jnp.int32).reshape(1)


def store_vector(target, first, lane, vector):
    width = vector.shape[1]
    done = 0
    while done < width:
        size = min(128 - lane, width - done)
        target[first : first + 1, lane : lane + size] = vector[:, done : done + size]
        done += size
        lane += size
        first, lane = first + lane // 128, lane % 128
    return first, lane


def column_sums(ref, first=0, width=None):
    width = ref.shape[1] if width is None else width
    cells = ref[:, first : first + width].astype(jnp.float32)
    return jnp.sum(cells, axis=0, keepdims=True)


def store_flat(target, product):
    rows, blocks = product.shape[0], product.shape[1] // 128
    for index in range(blocks):
        target[pl.ds(index, rows, stride=blocks), :] = product[:, index * 128 : (index + 1) * 128]


def column_blocks(ref, blocks):
    parts = [ref[:, pl.ds(pl.multiple_of(index * 128, 128), 128)] for index in blocks]
    return parts[0] if len(parts) == 1 else jnp.concatenate(parts, axis=1)


def steps_of(rows, size):
    return [(start, min(size, rows - start)) for start in range(0, rows, size)]


def enc_grad_kernel(plan, place_ref, *refs):
    norm_ref, own_norm_ref, out_ref, stage_ref, product_ref, small_ref, quarter_ref, sems = refs[
        -8:
    ]
    side, far = place_ref[0], place_ref[1]
    offset = 0
    flight = [None, None]
    turn = 0
    for size, left, first, depth, right, column, blocks in plan:
        x_ref, y_ref = refs[left], refs[right]
        if blocks % 2:
            columns = [2 * block + side for block in range(blocks)]
        else:
            columns = [4 * block + 2 * far + side for block in range(blocks // 2)]
        factor = column_blocks(y_ref, [column // 128 + block for block in columns])
        for start, rows in steps_of(depth, size):
            if flight[turn % 2] is not None:
                flight[turn % 2].wait()
            target = stage_ref.at[turn % 2]
            product = trans_mul(x_ref[:, first + start : first + start + rows], factor)
            if blocks % 2 == 0:
                store_flat(target, product)
            else:
                for block in range(blocks):
                    product_ref[block, :rows] = product[:, block * 128 : (block + 1) * 128]
                    odd = (far + block) % 2
                    target[
                        pl.ds((odd * blocks + block - far) // 2, rows // 2, stride=blocks), :
                    ] = product_ref.at[block][pl.ds(odd, rows // 2, stride=2), :]
            amount = rows * blocks // 2
            copy = pltpu.make_async_copy(
                target.at[pl.ds(0, amount)], out_ref.at[pl.ds(offset, amount)], sems.at[turn % 2]
            )
            copy.start()
            flight[turn % 2] = copy
            turn += 1
            offset += amount
    small_ref[...] = jnp.zeros_like(small_ref)
    spot = 0, 0
    for _, _, _, _, right, column, blocks in plan[:1] + plan[2:]:
        spot = store_vector(
            small_ref, *spot, column_sums(refs[right], column, blocks * 256)
        )
    rows = norm_ref.shape[0] // 4
    norms = sum(norm_ref[index * rows : (index + 1) * rows] for index in range(4))
    for vector in (
        own_norm_ref[0:1],
        norms[0:1],
        norms[1:2],
        own_norm_ref[1:2],
        norms[2:3],
        norms[3:4],
    ):
        spot = store_vector(small_ref, *spot, vector)
    rows = quarter_ref.shape[0]
    quarter_ref[...] = small_ref[pl.ds(side + 2 * far, rows, stride=4), :]
    last = pltpu.make_async_copy(quarter_ref, out_ref.at[pl.ds(offset, rows)], sems.at[2])
    last.start()
    for copy in [last] + flight:
        copy.wait()


def member_place():
    place = lax.axis_index("grp").astype(jnp.int32)
    return jnp.stack([place % 2, place // 2])


def enc_grad_quarter(inputs, grads, norms, own_norms, total_rows):
    count = len(inputs)
    plan = [
        (640, 0, 0, PATCH, count, 0, D // 256),
        (256, 1, 0, D, count + 1, 0, 3 * D // 256),
        (384, 2, 0, D, count + 2, 0, D // 256),
        (256, 2, D, D, count + 3, 0, F // 256),
        (768, 2, 2 * D, F, count + 3, F, D // 256),
    ]
    whole = pl.BlockSpec(memory_space=pltpu.VMEM)
    return pl.pallas_call(
        functools.partial(enc_grad_kernel, plan),
        in_specs=[pl.BlockSpec(memory_space=pltpu.SMEM)] + [whole] * (count + len(grads) + 2),
        out_specs=pl.BlockSpec(memory_space=pl.ANY),
        out_shape=jax.ShapeDtypeStruct((total_rows // 4, 128), jnp.float32),
        scratch_shapes=[
            pltpu.VMEM((2, 1536, 128), jnp.float32),
            pltpu.VMEM((9, 768, 128), jnp.float32),
            pltpu.VMEM((384, 128), jnp.float32),
            pltpu.VMEM((96, 128), jnp.float32),
            pltpu.SemaphoreType.DMA((3,)),
        ],
        compiler_params=pltpu.CompilerParams(vmem_limit_bytes=48 << 20),
        cost_estimate=pl.CostEstimate(
            flops=total_rows * 128 * inputs[0].shape[0],
            bytes_accessed=total_rows * 128,
            transcendentals=0,
        ),
    )(member_place(), *inputs, *grads, norms, own_norms)


def store_pixels(product_ref, targets):
    groups = product_ref.shape[1] // 4

    def load(row, block):
        return product_ref.at[block][pl.ds(row, groups, stride=4), :]

    def piece(row, block):
        if block < 13:
            return load(row, block)
        if block == 13:
            left, right = load(row, 13)[:, :64], load(row + 1, 0)[:, :64]
        else:
            left, right = load(row + 1, block - 14)[:, 64:], load(row + 1, block - 13)[:, :64]
        return jnp.concatenate([left, right], axis=1)

    for index in range(54):
        block = piece(0, index) if index < 27 else piece(2, index - 27)
        targets[index % 2][pl.ds(index // 2, groups, stride=27), :] = block


def dec_grad_kernel(plan, side_ref, *refs):
    norm_ref, mine_ref, theirs_ref, stage_ref, pixel_ref, small_ref, halves_ref, sems = refs[-8:]
    side = side_ref[0]
    flight = [None, None]
    turn = 0
    for index, (size, offset) in enumerate(plan):
        x_ref, y_ref = refs[2 * index], refs[2 * index + 1]
        pixels = y_ref.shape[1] % 256 != 0
        for start, rows in steps_of(x_ref.shape[1], size):
            product = trans_mul(x_ref[:, start : start + rows], y_ref[...])
            slot = turn % 2
            for copy in flight[slot] or ():
                copy.wait()
            if pixels:
                for block in range(14):
                    part = product[:, block * 128 : (block + 1) * 128]
                    pixel_ref[block, :, : part.shape[1]] = part
                store_pixels(pixel_ref, [stage_ref.at[slot, 0], stage_ref.at[slot, 1]])
            else:
                blocks = y_ref.shape[1] // 128
                for block in range(blocks):
                    stage_ref.at[slot, block % 2][
                        pl.ds(block // 2, rows, stride=blocks // 2), :
                    ] = product[:, block * 128 : (block + 1) * 128]
            amount = rows * y_ref.shape[1] // 256
            flight[slot] = [
                pltpu.make_async_copy(
                    stage_ref.at[slot, parity, pl.ds(0, amount)],
                    target.at[pl.ds(offset, amount)],
                    sems.at[slot, order],
                )
                for order, (parity, target) in enumerate(
                    ((side, mine_ref), (1 - side, theirs_ref))
                )
            ]
            for copy in flight[slot]:
                copy.start()
            offset += amount
            turn += 1
    small_ref[...] = jnp.zeros_like(small_ref)
    spot = store_vector(small_ref, 0, 0, column_sums(refs[1]))
    spot = store_vector(small_ref, *spot, norm_ref[0:1])
    for index in (2, 3, 4, 5):
        spot = store_vector(small_ref, *spot, column_sums(refs[2 * index + 1]))
    for index in range(1, norm_ref.shape[0]):
        spot = store_vector(small_ref, *spot, norm_ref[index : index + 1])
    rows = halves_ref.shape[1]
    for parity in range(2):
        halves_ref[parity] = small_ref[pl.ds(parity, rows, stride=2), :]
    last = [
        pltpu.make_async_copy(
            halves_ref.at[parity], target.at[pl.ds(target.shape[0] - rows, rows)], sems.at[2, order]
        )
        for order, (parity, target) in enumerate(((side, mine_ref), (1 - side, theirs_ref)))
    ]
    for copy in last:
        copy.start()
    for copy in last + flight[0] + flight[1]:
        copy.wait()


def dec_grad_halves(pairs, norms, total_rows):
    plan = [(256, 0), (256, 1536), (256, 4608), (256, 5632), (512, 9728), (512, 13824)]
    operands = [part for pair in pairs for part in pair]
    whole = pl.BlockSpec(memory_space=pltpu.VMEM)
    anywhere = pl.BlockSpec(memory_space=pl.ANY)
    shape = jax.ShapeDtypeStruct((total_rows // 2, 128), jnp.float32)
    return pl.pallas_call(
        functools.partial(dec_grad_kernel, plan),
        in_specs=[pl.BlockSpec(memory_space=pltpu.SMEM)] + [whole] * (len(operands) + 1),
        out_specs=[anywhere, anywhere],
        out_shape=[shape, shape],
        scratch_shapes=[
            pltpu.VMEM((2, 2, 3456, 128), jnp.float32),
            pltpu.VMEM((14, 512, 128), jnp.float32),
            pltpu.VMEM((256, 128), jnp.float32),
            pltpu.VMEM((2, 128, 128), jnp.float32),
            pltpu.SemaphoreType.DMA((3, 2)),
        ],
        compiler_params=pltpu.CompilerParams(vmem_limit_bytes=56 << 20),
        cost_estimate=pl.CostEstimate(
            flops=total_rows * 256 * pairs[1][0].shape[0],
            bytes_accessed=total_rows * 512,
            transcendentals=0,
        ),
    )(core_side(), *operands, norms)


def adamw_kernel(parts, with_average, place_ref, scalar_ref, *refs):
    count = 4 if with_average else 3
    ins, outs, grad_ref = refs[parts : parts + count], refs[parts + count : -1], refs[-1]
    for index in range(parts):
        rows = refs[index].shape[0]
        grad_ref[pl.ds(place_ref[index], rows, stride=parts), :] = refs[index][...]
    weights = ins[0][...]
    clipped = grad_ref[...] * scalar_ref[0]
    first_new = BETA_ONE * ins[1][...] + (1.0 - BETA_ONE) * clipped
    second_new = BETA_TWO * ins[2][...] + (1.0 - BETA_TWO) * clipped * clipped
    first_hat = first_new / scalar_ref[1]
    second_hat = second_new / scalar_ref[2]
    weights_new = weights * (1.0 - LEARN_RATE * WEIGHT_DECAY) - LEARN_RATE * first_hat / (
        jnp.sqrt(second_hat) + ADAM_EPS
    )
    outs[0][...] = weights_new
    outs[1][...] = first_new
    outs[2][...] = second_new
    outs[3][...] = weights_new.astype(jnp.bfloat16)
    if with_average:
        outs[4][...] = EMA_RATE * ins[3][...] + (1.0 - EMA_RATE) * weights_new


def adamw(parts, arrays, factor, steps_done):
    count = len(parts)
    place = lax.axis_index("grp")
    places = jnp.stack([(place ^ index) % count for index in range(count)])
    rows = arrays[0].shape[0]
    steps = 1
    for split in (2, 3, 4, 6, 8):
        if rows % (split * 8 * count) == 0:
            steps = split
    block = pl.BlockSpec((rows // steps, 128), lambda i: (i, 0))
    share = pl.BlockSpec((rows // steps // count, 128), lambda i: (i, 0))
    scalar = pl.BlockSpec(memory_space=pltpu.SMEM)
    scalars = jnp.stack([factor, 1.0 - BETA_ONE**steps_done, 1.0 - BETA_TWO**steps_done])
    full = jax.ShapeDtypeStruct((rows, 128), jnp.float32)
    shapes = [full, full, full, jax.ShapeDtypeStruct((rows, 128), jnp.bfloat16)]
    if len(arrays) == 4:
        shapes.append(full)
    return pl.pallas_call(
        functools.partial(adamw_kernel, count, len(arrays) == 4),
        grid=(steps,),
        in_specs=[scalar, scalar] + [share] * count + [block] * len(arrays),
        out_specs=[block] * len(shapes),
        out_shape=shapes,
        scratch_shapes=[pltpu.VMEM((rows // steps, 128), jnp.float32)],
        compiler_params=pltpu.CompilerParams(vmem_limit_bytes=40 << 20),
    )(places.astype(jnp.int32), scalars, *parts, *arrays)


def per_device(
    patches,
    segments,
    visible,
    enc_params,
    enc_first,
    enc_second,
    enc_average,
    dec_params,
    dec_first,
    dec_second,
    step_count,
):
    my_index = lax.axis_index("grp")
    slot_dev = segments.shape[0]
    rim = TILE_HI
    counts = jnp.sum((segments >= 0).astype(jnp.float32)) - visible.shape[0]
    total_count = total(jnp.full((8, 128), counts))[0, 0]
    enc_copy = gather_quarters(enc_params.astype(jnp.bfloat16))
    group_vis = group_rows(visible)
    group_seg = double(double(segments, 0, "grp", 2), 1, "grp", 1).reshape(-1)
    group_ids = group_seg[group_vis]
    key_ids = extended(segments + 3, rim) - 3
    local_slot = group_vis - my_index * slot_dev
    chosen = (
        local_slot[:, None] == jnp.arange(slot_dev, dtype=jnp.int32)[None, :]
    ).astype(jnp.bfloat16)
    seen = jnp.sum(chosen.astype(jnp.float32), axis=0) > 0.5
    enc_input = group_rows(own_rows(matmul(chosen, patches).astype(jnp.bfloat16)))
    enc_waves = sincos(group_vis % L, D)
    positions = (my_index * slot_dev + jnp.arange(slot_dev, dtype=jnp.int32)) % L
    dec_waves = sincos(positions, E)
    pixels = patches.astype(jnp.float32)
    pixel_mean = jnp.mean(pixels, axis=1, keepdims=True)
    centered = pixels - pixel_mean
    pixel_rate = lax.rsqrt(jnp.mean(centered * centered, axis=1, keepdims=True) + NORM_EPS)
    (
        enc_copy,
        enc_input,
        enc_waves,
        dec_waves,
        pixel_mean,
        pixel_rate,
        seen,
        group_ids,
        key_ids,
        chosen,
        total_count,
    ) = lax.optimization_barrier(
        (
            enc_copy,
            enc_input,
            enc_waves,
            dec_waves,
            pixel_mean,
            pixel_rate,
            seen,
            group_ids,
            key_ids,
            chosen,
            total_count,
        )
    )
    enc_copy, dec_shard = lax.optimization_barrier((enc_copy, dec_params))
    dec_copy = gather_quarters(dec_shard.astype(jnp.bfloat16))
    enc_table = unpack(enc_copy, enc_pieces(), ENC_STEPS)
    dec_table = unpack(dec_copy, dec_pieces(), DEC_STEPS)
    enc_start = (
        matmul(enc_input, enc_table["patch_w"])
        + enc_table["patch_b"].astype(jnp.float32)
        + enc_waves
    )

    own = visible.shape[0]
    enc_out, enc_saved = enc_forward(enc_start, enc_table, own, group_ids)
    enc_gain = enc_table["norm_g"].astype(jnp.float32)
    enc_shift = enc_table["norm_b"].astype(jnp.float32)
    enc_final = layer_norm(enc_out, enc_gain[2], enc_shift[2]).astype(jnp.bfloat16)
    latent = (
        matmul(enc_final, dec_table["embed_w"]) + dec_table["embed_b"].astype(jnp.float32)
    ).astype(jnp.bfloat16)
    group_latent = group_rows(latent)
    enc_inputs = jnp.concatenate([enc_saved[2], enc_saved[4], enc_saved[6]], axis=1)
    group_latent, enc_inputs = lax.optimization_barrier((group_latent, enc_inputs))
    group_inputs = group_rows(enc_inputs)
    placed = trans_mul(chosen, group_latent)
    dec_start = jnp.where(
        seen[:, None], placed, dec_table["mask_token"].astype(jnp.float32)[None, :]
    ) + dec_waves
    counted = jnp.where((segments >= 0) & jnp.logical_not(seen), 1.0, 0.0)

    def dec_share(pair):
        joined = extended(jnp.concatenate(pair, axis=1), rim)
        return (joined[:, :E], joined[:, E:])

    dec_out, dec_saved = block_forward(
        dec_start, dec_table, EH, rim, segments, key_ids, dec_share
    )
    dec_gain = dec_table["norm_g"].astype(jnp.float32)
    dec_shift = dec_table["norm_b"].astype(jnp.float32)
    dec_final = layer_norm(dec_out, dec_gain[2], dec_shift[2]).astype(jnp.bfloat16)
    predicted = matmul(dec_final, dec_table["pix_w"]) + dec_table["pix_b"].astype(jnp.float32)
    target = (patches.astype(jnp.float32) - pixel_mean) * pixel_rate
    errors = predicted - target
    loss_part = jnp.sum(counted * jnp.mean(errors * errors, axis=1))
    errors, group_inputs = lax.optimization_barrier((errors, group_inputs))
    pred_grad = (counted[:, None] * errors * (2.0 / PATCH) / total_count).astype(jnp.bfloat16)
    dec_out_grad, dec_gain_last, dec_shift_last = norm_back(
        dec_out, dec_gain[2], dec_shift[2], mul_trans(pred_grad, dec_table["pix_w"])
    )
    start_grad, dec_small, dec_pairs = block_backward(
        dec_out_grad, dec_table, EH, rim, segments, key_ids, dec_saved
    )
    mask_grad = jnp.sum(jnp.where(seen[:, None], 0.0, start_grad), axis=0)
    latent_grad = own_rows(matmul(chosen, start_grad.astype(jnp.bfloat16)).astype(jnp.bfloat16))
    dec_pairs["embed_w"] = (enc_final, latent_grad)
    dec_pairs["pix_w"] = (dec_final, pred_grad)
    mine, theirs = dec_grad_halves(
        [dec_pairs[name] for name in ("embed_w", "qkv_w", "out_w", "up_w", "down_w", "pix_w")],
        jnp.stack(
            [
                mask_grad,
                dec_small[0],
                dec_small[2],
                dec_gain_last,
                dec_small[1],
                dec_small[3],
                dec_shift_last,
            ]
        ),
        DR,
    )
    arrived = swap(theirs, "grp", 1)
    latent_grad, mine = lax.optimization_barrier((latent_grad, mine))
    dec_blocks = None

    def enc_pause(grad):
        nonlocal dec_blocks
        grad, dec_half = lax.optimization_barrier((grad, mine + arrived))
        dec_blocks = reduce_first(dec_half, dec_routes(), (0.5,))
        return grad

    enc_out_grad, enc_gain_last, enc_shift_last = norm_back(
        enc_out, enc_gain[2], enc_shift[2], mul_trans(latent_grad, dec_table["embed_w"])
    )
    enc_grads, enc_small = enc_backward(
        enc_out_grad, enc_table, enc_start, group_ids, enc_saved, enc_pause
    )
    enc_norms = jnp.stack([enc_small[2], enc_gain_last, enc_small[3], enc_shift_last])
    branch_grad, far_grad, enc_norms = lax.optimization_barrier(
        (enc_grads[2], enc_grads[3], enc_norms)
    )
    enc_quarter = enc_grad_quarter(
        [enc_input, enc_saved[0], group_inputs],
        [*enc_grads[:2], branch_grad, group_rows(far_grad)],
        group_rows(enc_norms),
        jnp.stack([enc_small[0], enc_small[1]]),
        ER,
    )
    enc_quarter, dec_blocks = lax.optimization_barrier((enc_quarter, dec_blocks))
    enc_blocks = reduce_first(enc_quarter, dp_routes(), (0.5,))
    dec_blocks = reduce_rest(dec_blocks, dec_routes(), 1, 2)
    enc_sum = reduce_rest(enc_blocks, dp_routes())
    enc_sum, dec_blocks = lax.optimization_barrier((enc_sum, dec_blocks))
    enc_own = jnp.concatenate(enc_sum, axis=0)
    enc_across = swap(enc_own, "grp", 2)
    dec_sum = reduce_rest(dec_blocks, dec_routes(), 2)
    squares = sum(jnp.sum(part * part) for part in enc_sum + dec_sum)
    lane = lax.broadcasted_iota(jnp.int32, (8, 128), 1)
    sums = total(jnp.where(lane == 0, squares, jnp.where(lane == 1, loss_part, 0.0)))
    dec_wide = [double(piece, 0, "grp", 2).reshape(-1, 128) for piece in dec_sum]
    enc_quarters = (
        enc_own,
        swap(enc_own, "grp", 1),
        enc_across,
        swap(enc_across, "grp", 1),
    )
    dec_mine = jnp.concatenate(dec_wide, axis=0)
    dec_halves = dec_mine, swap(dec_mine, "grp", 1)
    loss_total = sums[0, 1]
    grad_norm = jnp.sqrt(sums[0, 0])
    factor = jnp.minimum(1.0, CLIP_LIMIT / (grad_norm + NORM_EPS))
    steps_done = step_count[0].astype(jnp.float32)
    enc_new, enc_first_new, enc_second_new, enc_copy_new, average_new = adamw(
        enc_quarters, (enc_params, enc_first, enc_second, enc_average), factor, steps_done
    )
    dec_new, dec_first_new, dec_second_new, dec_copy_new = adamw(
        dec_halves, (dec_params, dec_first, dec_second), factor, steps_done
    )
    return (
        enc_new,
        enc_first_new,
        enc_second_new,
        enc_copy_new,
        dec_new,
        dec_first_new,
        dec_second_new,
        dec_copy_new,
        average_new,
        grad_norm,
        loss_total,
        total_count,
    )


def solution(mesh):
    placed = (
        P(("dp", "grp"), None),
        P(("dp", "grp")),
        P(("dp", "grp")),
        P("dp", None),
        P("dp", None),
        P("dp", None),
        P("dp", None),
        P("dp", None),
        P("dp", None),
        P("dp", None),
        P(),
    )
    return jax.shard_map(
        per_device,
        mesh=mesh,
        in_specs=placed,
        out_specs=(
            P("dp", None),
            P("dp", None),
            P("dp", None),
            P("dp", None),
            P("dp", None),
            P("dp", None),
            P("dp", None),
            P("dp", None),
            P("dp", None),
            P(),
            P(),
            P(),
        ),
        check_vma=False,
    )
```

```python
import functools
import math

import jax
import jax.numpy as jnp
from jax import lax
from jax.experimental import pallas as pl
from jax.experimental.pallas import tpu as pltpu
from jax.sharding import PartitionSpec as P

D = 768
H = 12
F = 3072
E = 512
EH = 16
FE = 2048
PATCH = 1728
L = 1728
TILE_HI = 192
ER = 66048
DR = 34816


NORM_EPS = 1e-06
MASK_FILL = -1e30
CLIP_LIMIT = 0.0002
LEARN_RATE = 0.02
BETA_ONE = 0.5
BETA_TWO = 0.5
ADAM_EPS = 1e-08
WEIGHT_DECAY = 0.05
EMA_RATE = 0.9


def swap(block, axis, bit):
    count = lax.axis_size(axis)
    return lax.ppermute(block, axis, [(i, i ^ bit) for i in range(count)])


def bit_of(axis, bit):
    return (lax.axis_index(axis) // bit) % 2


def double(block, dim, axis, bit):
    mine = bit_of(axis, bit)
    other = swap(block, axis, bit)
    first = jnp.where(mine == 0, block, other)
    second = jnp.where(mine == 0, other, block)
    return jnp.stack([first, second], axis=dim)


def total(values):
    for axis in ("grp", "dp"):
        bit = 1
        while bit < lax.axis_size(axis):
            values = values + swap(values, axis, bit)
            bit *= 2
    return values


def dp_bits():
    bits = [1]
    while bits[-1] * 2 < lax.axis_size("dp"):
        bits.append(bits[-1] * 2)
    return bits


def cut(rows, shares):
    unit = 16 if rows % 16 == 0 else 2
    sizes = [int(round(rows // unit * share)) * unit for share in shares]
    return sizes + [rows - sum(sizes)]


def gather_quarters(shard):
    part = shard.shape[0] // 4
    quarter = lax.dynamic_slice_in_dim(shard, lax.axis_index("grp") * part, part, 0)
    return lax.all_gather(quarter, ("dp", "grp"), axis=0, tiled=True)


def section(cells, dim, start, size):
    return lax.dynamic_slice_in_dim(cells, start, size, dim)


def reduce_bit(cells, dim, axis, bit, start=0, size=None):
    half = (cells.shape[dim] if size is None else size) // 2
    mine = bit_of(axis, bit)
    sent = section(cells, dim, start + (1 - mine) * half, half)
    return section(cells, dim, start + mine * half, half) + swap(sent, axis, bit)


def dec_routes():
    bits = [("dp", bit) for bit in dp_bits()]
    return [bits[:1] + [("grp", 2)] + bits[1:], bits[1:2] + [("grp", 2)] + bits[2:] + bits[:1]]


def reduce_first(half, routes, shares):
    shards = lax.axis_size("dp")
    half_rows = half.shape[0] // shards
    bits = dp_bits()
    names = [("dp", bit) for bit in reversed(bits)]
    cells = half.reshape([2] * len(bits) + [half_rows, 128])
    blocks = []
    start = 0
    for route, rows in zip(routes, cut(half_rows, shares)):
        axis, bit = route[0]
        if axis == "grp":
            block = reduce_bit(cells, len(bits), axis, bit, start, rows)
        else:
            dim = names.index(route[0])
            mine = bit_of(axis, bit)

            def pick(index, dim=dim, start=start, rows=rows):
                corner = [0] * dim + [index] + [0] * (len(bits) - dim - 1) + [start, 0]
                sizes = [2] * dim + [1] + [2] * (len(bits) - dim - 1) + [rows, 128]
                return lax.dynamic_slice(cells, corner, sizes)

            block = pick(mine) + swap(pick(1 - mine), axis, bit)
        blocks.append(block)
        start += rows
    return blocks


def reduce_rest(blocks, routes, first=1, last=None):
    bits = dp_bits()
    names = [("dp", bit) for bit in reversed(bits)]
    blocks = list(blocks)
    for step in range(first, len(routes[0]) if last is None else last):
        for index, route in enumerate(routes):
            axis, bit = route[step]
            dim = len(bits) if axis == "grp" else names.index(route[step])
            blocks[index] = reduce_bit(blocks[index], dim, axis, bit)
    if last is not None:
        return blocks
    return [block.reshape(-1, 128) for block in blocks]


def dp_routes():
    bits = [("dp", bit) for bit in dp_bits()]
    return [bits, bits[1:] + bits[:1]]


def spread_pieces(pieces):
    wide = [double(piece, 0, "grp", 2).reshape(-1, 128) for piece in pieces]
    mine = jnp.concatenate(wide, axis=0)
    return mine, swap(mine, "grp", 1)


def group_rows(block):
    across = swap(block, "grp", 2)
    near, far = (
        swap(block, "grp", 1),
        swap(across, "grp", 1),
    )
    return jnp.concatenate([block, near, across, far], axis=0)


def own_rows(blocks):
    count = blocks.shape[0] // 4
    parts = [lax.slice_in_dim(blocks, i * count, (i + 1) * count, axis=0) for i in range(4)]
    sent = jnp.concatenate([parts[1], parts[3]], axis=0)
    arrived = swap(sent, "grp", 1)
    kept = parts[0] + arrived[:count]
    other = parts[2] + arrived[count:]
    return kept + swap(other, "grp", 2)


def extended(cells, width):
    count = lax.axis_size("grp")
    ends = count - 1
    head = cells[:width]
    tail = cells[cells.shape[0] - width :]
    return jnp.concatenate(
        [
            lax.ppermute(tail, "grp", [(i, i + 1) for i in range(ends)]),
            cells,
            lax.ppermute(head, "grp", [(i + 1, i) for i in range(ends)]),
        ],
        axis=0,
    )


def passed_along(block, axis, distance):
    devices = range(lax.axis_size(axis))
    route = [(i - distance, i) for i in devices if i - distance in devices]
    return lax.ppermute(block, axis, route)


def enc_pieces():
    return [
        ("patch_w", (PATCH, D)),
        ("qkv_w", (D, 3 * D)),
        ("out_w", (D, D)),
        ("up_w", (D, F)),
        ("down_w", (F, D)),
        ("patch_b", (D,)),
        ("out_b", (D,)),
        ("up_b", (F,)),
        ("down_b", (D,)),
        ("norm_g", (3, D)),
        ("norm_b", (3, D)),
    ]


def dec_pieces():
    return [
        ("embed_w", (D, E)),
        ("qkv_w", (E, 3 * E)),
        ("out_w", (E, E)),
        ("up_w", (E, FE)),
        ("down_w", (FE, E)),
        ("pix_w", (E, PATCH)),
        ("embed_b", (E,)),
        ("mask_token", (E,)),
        ("out_b", (E,)),
        ("up_b", (FE,)),
        ("down_b", (E,)),
        ("pix_b", (PATCH,)),
        ("norm_g", (3, E)),
        ("norm_b", (3, E)),
    ]


def relayout_kernel(plan, *refs):
    source, outs = refs[0], refs[1 : 1 + len(plan)]
    raw_ref, wide_ref, stages, in_sems, out_sems = (
        refs[1 + len(plan)],
        refs[2 + len(plan)],
        refs[3 + len(plan) : -2],
        refs[-2],
        refs[-1],
    )
    steps = [
        (index, offset + start * blocks, start, rows, blocks)
        for index, (offset, depth, blocks, rows) in enumerate(plan)
        for start in range(0, depth, rows)
    ]

    def fetch(turn):
        _, offset, _, rows, blocks = steps[turn]
        return pltpu.make_async_copy(
            source.at[pl.ds(offset, rows * blocks)],
            raw_ref.at[turn % 2, pl.ds(0, rows * blocks)],
            in_sems.at[turn % 2],
        )

    flight = {}
    fetch(0).start()
    for turn, (index, _, start, rows, blocks) in enumerate(steps):
        if turn + 1 < len(steps):
            fetch(turn + 1).start()
        fetch(turn).wait()
        wide_ref[: rows * blocks, :] = raw_ref[turn % 2, : rows * blocks, :].astype(jnp.float32)
        slot = turn % 2
        if slot in flight:
            flight.pop(slot).wait()
        stage = stages[index].at[slot]
        for block in range(blocks):
            stage[:, block * 128 : (block + 1) * 128] = wide_ref[
                pl.ds(block, rows, stride=blocks), :
            ].astype(jnp.bfloat16)
        flight[slot] = pltpu.make_async_copy(
            stage, outs[index].at[pl.ds(start, rows)], out_sems.at[slot]
        )
        flight[slot].start()
    for copy in flight.values():
        copy.wait()


def relayout(rows, plan):
    anywhere = pl.BlockSpec(memory_space=pl.ANY)
    most = max(step * blocks for _, _, blocks, step in plan)
    return pl.pallas_call(
        functools.partial(relayout_kernel, plan),
        in_specs=[anywhere],
        out_specs=[anywhere] * len(plan),
        out_shape=[
            jax.ShapeDtypeStruct((depth, blocks * 128), jnp.bfloat16)
            for _, depth, blocks, _ in plan
        ],
        scratch_shapes=[
            pltpu.VMEM((2, most, 128), jnp.bfloat16),
            pltpu.VMEM((most, 128), jnp.float32),
        ]
        + [pltpu.VMEM((2, step, blocks * 128), jnp.bfloat16) for _, _, blocks, step in plan]
        + [pltpu.SemaphoreType.DMA((2,)), pltpu.SemaphoreType.DMA((2,))],
        compiler_params=pltpu.CompilerParams(vmem_limit_bytes=40 << 20),
        cost_estimate=pl.CostEstimate(
            flops=0, bytes_accessed=rows.size * 4, transcendentals=0
        ),
    )(rows)


ENC_STEPS = {"patch_w": 576, "qkv_w": 192, "out_w": 384, "up_w": 128, "down_w": 512}
DEC_STEPS = {"embed_w": 768, "qkv_w": 256, "out_w": 512, "up_w": 128, "down_w": 512}


def unpack(rows, pieces, steps):
    table = {}
    offset = 0
    plan = []
    vectors = sum(1 for _, dims in pieces if len(dims) == 2 and dims[0] > 3)
    for piece_name, piece_dims in pieces[:vectors]:
        amount = math.prod(piece_dims) // 128
        if piece_name in steps:
            plan.append((offset, piece_dims[0], piece_dims[1] // 128, steps[piece_name]))
        else:
            table[piece_name] = rows[offset : offset + amount].reshape(piece_dims)
        offset += amount
    small = rows[offset:].reshape(-1)
    table.update(zip(steps, relayout(rows, plan)))
    offset = 0
    for piece_name, piece_dims in pieces[vectors:]:
        amount = math.prod(piece_dims)
        table[piece_name] = small[offset : offset + amount].reshape(piece_dims)
        offset += amount
    return table


def matmul(left, right):
    return jnp.dot(left, right, preferred_element_type=jnp.float32)


def mul_trans(left, right):
    return lax.dot_general(
        left, right, (((1,), (1,)), ((), ())), preferred_element_type=jnp.float32
    )


def trans_mul(left, right):
    return lax.dot_general(
        left, right, (((0,), (0,)), ((), ())), preferred_element_type=jnp.float32
    )


def sincos(positions, width):
    half_width = width // 2
    freq_row = jnp.exp(
        jnp.arange(half_width, dtype=jnp.float32) * (-2.0 * math.log(10000.0) / width)
    )
    angles = positions.astype(jnp.float32)[:, None] * freq_row[None, :]
    return jnp.concatenate([jnp.sin(angles), jnp.cos(angles)], axis=1)


def layer_norm(inputs, gain, shift):
    center = inputs - jnp.mean(inputs, axis=-1, keepdims=True)
    return (
        center * lax.rsqrt(jnp.mean(center * center, axis=-1, keepdims=True) + NORM_EPS) * gain
        + shift
    )


def norm_back(inputs, gain, shift, grad_out):
    outputs, pull = jax.vjp(layer_norm, inputs, gain, shift)
    return pull(grad_out)


def exact_gelu(values):
    return jax.nn.gelu(values, approximate=False)


BLOCK = 128


def head_masks(width):
    lanes = lax.broadcasted_iota(jnp.int32, (1, 128), 1) // width
    return [(lanes == index).astype(jnp.float32) for index in range(128 // width)]


def spread_heads(cells, masks):
    wide = cells.astype(jnp.float32)
    return jnp.concatenate([(wide * mask).astype(jnp.bfloat16) for mask in masks], axis=0)


TILE = 32
TALL = 64


def attend_kernel(
    window,
    stride,
    width,
    q_ref,
    k_ref,
    v_ref,
    qid_ref,
    kid_ref,
    o_ref,
    bias_ref,
    score_ref,
    prob_ref,
):
    start = pl.multiple_of(pl.program_id(0) * stride, BLOCK)
    scale = width ** (-0.5)
    masks = head_masks(width)
    near = pl.ds(start, window)
    bias_ref[...] = jnp.where(qid_ref[...] == kid_ref[:, near], 0.0, MASK_FILL)
    for group in range(q_ref.shape[1] // 128):
        lanes = slice(group * 128, (group + 1) * 128)
        slot = group % 2
        score_ref[slot] = mul_trans(spread_heads(q_ref[:, lanes], masks), k_ref[near, lanes])
        for first in range(0, len(masks) * BLOCK, TILE):
            rows = slice(first, first + TILE)
            row = first % BLOCK
            part = score_ref[slot, rows, :] * scale + bias_ref[row : row + TILE, :]
            powers = jnp.exp(part - jnp.max(part, axis=1, keepdims=True))
            probs = powers * (1.0 / jnp.sum(powers, axis=1, keepdims=True))
            prob_ref[slot, rows, :] = probs.astype(jnp.bfloat16)
        wide = matmul(prob_ref[slot], v_ref[near, lanes])
        o_ref[:, lanes] = pick_heads(wide, masks).astype(jnp.bfloat16)


def pick_heads(wide, masks):
    return sum(wide[i * BLOCK : (i + 1) * BLOCK] * mask for i, mask in enumerate(masks))


def row_sums(cells, merge):
    return merge(cells.reshape(-1, 8, cells.shape[1]), axis=0)


def attend_back_kernel(window, stride, width, pick, *refs):
    q_ref, g_ref, k_ref, v_ref, qid_ref, kid_ref = refs[:6]
    dq_ref, both_ref, bias_ref, score_ref, grad_ref, prob_ref, back_ref = refs[-7:]
    before = refs[6:-7]
    columns = q_ref.shape[1]
    step = pl.program_id(0)
    start = pl.multiple_of(pick(step) * stride, BLOCK)
    scale = width ** (-0.5)
    masks = head_masks(width)

    @pl.when(step == 0)
    def _():
        both_ref[...] = before[0][...] if before else jnp.zeros_like(both_ref)

    near = pl.ds(start, window)
    bias_ref[...] = jnp.where(kid_ref[near, :] == qid_ref[...], 0.0, MASK_FILL)
    tiles = [slice(first, first + TALL) for first in range(0, window, TALL)]
    for group in range(q_ref.shape[1] // 128):
        lanes = slice(group * 128, (group + 1) * 128)
        slot = group % 2
        keys = k_ref[near, lanes]
        queries = spread_heads(q_ref[:, lanes], masks)
        outs = spread_heads(g_ref[:, lanes], masks)
        score_ref[slot] = mul_trans(keys, queries)
        grad_ref[slot] = mul_trans(v_ref[near, lanes], outs)
        for index in range(len(masks)):
            head = slice(index * BLOCK, (index + 1) * BLOCK)
            top = None
            for tile in tiles:
                part = score_ref[slot, tile, head] * scale + bias_ref[tile, :]
                score_ref[slot, tile, head] = part
                most = row_sums(part, jnp.max)
                top = most if top is None else jnp.maximum(top, most)
            top = jnp.max(top, axis=0, keepdims=True)
            whole = jnp.zeros((8, BLOCK), jnp.float32)
            for tile in tiles:
                powers = jnp.exp(score_ref[slot, tile, head] - top)
                score_ref[slot, tile, head] = powers
                whole += row_sums(powers, jnp.sum)
            inverse = 1.0 / jnp.sum(whole, axis=0, keepdims=True)
            shared = jnp.zeros((8, BLOCK), jnp.float32)
            for tile in tiles:
                probs = score_ref[slot, tile, head] * inverse
                prob_ref[slot, tile, head] = probs.astype(jnp.bfloat16)
                shared += row_sums(probs * grad_ref[slot, tile, head], jnp.sum)
            shared = jnp.sum(shared, axis=0, keepdims=True)
            for tile in tiles:
                probs = score_ref[slot, tile, head] * inverse
                back_ref[slot, tile, head] = (
                    probs * (grad_ref[slot, tile, head] - shared)
                ).astype(jnp.bfloat16)
        back = back_ref[slot]
        far_lanes = slice(columns + group * 128, columns + (group + 1) * 128)
        both_ref[near, far_lanes] += matmul(prob_ref[slot], outs)
        both_ref[near, lanes] += matmul(back, queries) * scale
        dq_ref[:, lanes] = pick_heads(trans_mul(back, keys), masks) * scale


def padded(cells, rows, fill=0):
    return jnp.pad(
        cells, [(0, rows - cells.shape[0])] + [(0, 0)] * (cells.ndim - 1), constant_values=fill
    )


def attend_sizes(query, keys, rim):
    steps = -(-query.shape[0] // BLOCK)
    if rim:
        return steps, BLOCK + 2 * rim, steps * BLOCK + 2 * rim, BLOCK
    return steps, keys.shape[0], keys.shape[0], 0


def whole_spec(dims):
    return pl.BlockSpec(dims, lambda i: (0, 0))


def step_spec(columns):
    return pl.BlockSpec((BLOCK, columns), lambda i: (i, 0))


def attend(query, keys, values, query_ids, key_ids, heads, rim):
    count, columns = query.shape
    steps, window, span, stride = attend_sizes(query, keys, rim)
    stack = 128 * heads // columns * BLOCK
    outcome = pl.pallas_call(
        functools.partial(attend_kernel, window, stride, columns // heads),
        grid=(steps,),
        in_specs=[
            step_spec(columns),
            whole_spec((span, columns)),
            whole_spec((span, columns)),
            step_spec(1),
            whole_spec((1, span)),
        ],
        out_specs=step_spec(columns),
        out_shape=jax.ShapeDtypeStruct((steps * BLOCK, columns), jnp.bfloat16),
        scratch_shapes=[
            pltpu.VMEM((BLOCK, window), jnp.float32),
            pltpu.VMEM((2, stack, window), jnp.float32),
            pltpu.VMEM((2, stack, window), jnp.bfloat16),
        ],
        compiler_params=pltpu.CompilerParams(vmem_limit_bytes=48 << 20),
        cost_estimate=pl.CostEstimate(
            flops=4 * steps * BLOCK * window * columns,
            bytes_accessed=8 * span * columns,
            transcendentals=steps * BLOCK * window * heads,
        ),
    )(
        padded(query, steps * BLOCK),
        padded(keys, span),
        padded(values, span),
        padded(query_ids, steps * BLOCK, -4)[:, None],
        padded(key_ids, span, -5)[None, :],
    )
    return outcome[:count]


def same_step(step):
    return step


def attend_back(
    query, keys, values, query_ids, key_ids, heads, rim, out_grad, steps=None, pick=same_step, before=()
):
    count, columns = query.shape
    all_steps, window, span, stride = attend_sizes(query, keys, rim)
    steps = all_steps if steps is None else steps
    stack = 128 * heads // columns * BLOCK
    block = pl.BlockSpec((BLOCK, columns), lambda i: (pick(i), 0))
    return pl.pallas_call(
        functools.partial(attend_back_kernel, window, stride, columns // heads, pick),
        grid=(steps,),
        in_specs=[
            block,
            block,
            whole_spec((span, columns)),
            whole_spec((span, columns)),
            pl.BlockSpec((1, BLOCK), lambda i: (0, pick(i))),
            whole_spec((span, 1)),
        ]
        + ([whole_spec((span, 2 * columns)), pl.BlockSpec(memory_space=pl.ANY)] if before else []),
        out_specs=[block, whole_spec((span, 2 * columns))],
        out_shape=[
            jax.ShapeDtypeStruct((all_steps * BLOCK, columns), jnp.float32),
            jax.ShapeDtypeStruct((span, 2 * columns), jnp.float32),
        ],
        input_output_aliases={7: 0} if before else {},
        scratch_shapes=[
            pltpu.VMEM((window, BLOCK), jnp.float32),
            pltpu.VMEM((2, window, stack), jnp.float32),
            pltpu.VMEM((2, window, stack), jnp.float32),
            pltpu.VMEM((2, window, stack), jnp.bfloat16),
            pltpu.VMEM((2, window, stack), jnp.bfloat16),
        ],
        compiler_params=pltpu.CompilerParams(vmem_limit_bytes=48 << 20),
        cost_estimate=pl.CostEstimate(
            flops=80 * steps * BLOCK * window * columns,
            bytes_accessed=20 * span * columns,
            transcendentals=steps * BLOCK * window * heads,
        ),
    )(
        padded(query, all_steps * BLOCK),
        padded(out_grad, all_steps * BLOCK),
        padded(keys, span),
        padded(values, span),
        padded(query_ids, all_steps * BLOCK, -4)[None, :],
        padded(key_ids, span, -5)[:, None],
        *before,
    )


def attend_back_slots(query, keys, values, query_ids, key_ids, heads, rim, out_grad):
    count = query.shape[0]
    steps, window, _, _ = attend_sizes(query, keys, rim)
    low = -(-rim // BLOCK)
    high = next(i for i in range(low, steps) if i * BLOCK + window > rim + count)
    args = (query, keys, values, query_ids, key_ids, heads, rim, out_grad)
    edges = attend_back(
        *args, steps=low + steps - high, pick=lambda i: i + (i // low) * (high - low)
    )
    from_upper = passed_along(edges[1][:rim], "grp", -1)
    from_lower = passed_along(edges[1][rim + count : 2 * rim + count], "grp", 1)
    inner = attend_back(
        *args, steps=high - low, pick=lambda i: i + low, before=(edges[1], edges[0])
    )
    rims = jnp.pad(from_lower, ((0, count - rim), (0, 0))) + jnp.pad(
        from_upper, ((count - rim, 0), (0, 0))
    )
    middle = (inner[1][rim : rim + count] + rims).astype(jnp.bfloat16)
    query_grad = inner[0][:count].astype(jnp.bfloat16)
    return jnp.concatenate([query_grad, middle], axis=1)


def gelu_pair(hidden):
    below = 0.5 * (1.0 + lax.erf(hidden * math.sqrt(0.5)))
    bell = jnp.exp(-0.5 * hidden * hidden) * (1.0 / math.sqrt(2.0 * math.pi))
    return lax.optimization_barrier(
        ((hidden * below).astype(jnp.bfloat16), below + hidden * bell)
    )


def block_forward(inputs, table, heads, rim, query_ids, key_ids, share_keys):
    gains = table["norm_g"].astype(jnp.float32)
    shifts = table["norm_b"].astype(jnp.float32)
    width = inputs.shape[1]
    normed_one = layer_norm(inputs, gains[0], shifts[0]).astype(jnp.bfloat16)
    qkv = matmul(normed_one, table["qkv_w"]).astype(jnp.bfloat16)
    query = qkv[:, :width]
    all_keys, all_values = share_keys((qkv[:, width : 2 * width], qkv[:, 2 * width :]))
    attended = attend(query, all_keys, all_values, query_ids, key_ids, heads, rim)
    mixed = inputs + (matmul(attended, table["out_w"]) + table["out_b"].astype(jnp.float32))
    normed_two = layer_norm(mixed, gains[1], shifts[1]).astype(jnp.bfloat16)
    hidden = matmul(normed_two, table["up_w"]) + table["up_b"].astype(jnp.float32)
    activated, slope = gelu_pair(hidden)
    result = mixed + (matmul(activated, table["down_w"]) + table["down_b"].astype(jnp.float32))
    saved = (
        inputs,
        normed_one,
        query,
        all_keys,
        all_values,
        attended,
        mixed,
        normed_two,
        slope,
        activated,
    )
    return (result, saved)


def block_backward(
    grad_out, table, heads, rim, query_ids, key_ids, saved
):
    (
        inputs,
        normed_one,
        query,
        all_keys,
        all_values,
        attended,
        mixed,
        normed_two,
        slope,
        activated,
    ) = saved
    gains = table["norm_g"].astype(jnp.float32)
    shifts = table["norm_b"].astype(jnp.float32)
    pairs = {}
    down_grad = grad_out.astype(jnp.bfloat16)
    pairs["down_w"] = (activated, down_grad)
    act_grad = mul_trans(down_grad, table["down_w"])
    hidden_grad = (act_grad * slope).astype(jnp.bfloat16)
    pairs["up_w"] = (normed_two, hidden_grad)
    mixed_part, gain_two, shift_two = norm_back(
        mixed, gains[1], shifts[1], mul_trans(hidden_grad, table["up_w"])
    )
    mixed_grad = grad_out + mixed_part
    branch_grad = mixed_grad.astype(jnp.bfloat16)
    pairs["out_w"] = (attended, branch_grad)
    attended_grad = mul_trans(branch_grad, table["out_w"]).astype(jnp.bfloat16)
    qkv_grad = attend_back_slots(
        query, all_keys, all_values, query_ids, key_ids, heads, rim, attended_grad
    )
    pairs["qkv_w"] = (normed_one, qkv_grad)
    input_part, gain_one, shift_one = norm_back(
        inputs, gains[0], shifts[0], mul_trans(qkv_grad, table["qkv_w"])
    )
    return (mixed_grad + input_part, (gain_one, shift_one, gain_two, shift_two), pairs)


def enc_forward(inputs, table, own, ids):
    gains = table["norm_g"].astype(jnp.float32)
    shifts = table["norm_b"].astype(jnp.float32)
    normed_one = layer_norm(inputs, gains[0], shifts[0]).astype(jnp.bfloat16)
    qkv = matmul(normed_one, table["qkv_w"]).astype(jnp.bfloat16)
    attended = attend(
        qkv[:own, :D], qkv[:, D : 2 * D], qkv[:, 2 * D :], ids[:own], ids, H, 0
    )
    mixed = inputs[:own] + (matmul(attended, table["out_w"]) + table["out_b"].astype(jnp.float32))
    normed_two = layer_norm(mixed, gains[1], shifts[1]).astype(jnp.bfloat16)
    hidden = matmul(normed_two, table["up_w"]) + table["up_b"].astype(jnp.float32)
    activated, slope = gelu_pair(hidden)
    result = mixed + (matmul(activated, table["down_w"]) + table["down_b"].astype(jnp.float32))
    return result, (normed_one, qkv, attended, mixed, normed_two, slope, activated)


def enc_backward(grad_out, table, inputs, ids, saved, pause):
    normed_one, qkv, attended, mixed, normed_two, slope, activated = saved
    gains = table["norm_g"].astype(jnp.float32)
    shifts = table["norm_b"].astype(jnp.float32)
    down_grad = grad_out.astype(jnp.bfloat16)
    hidden_grad = (mul_trans(down_grad, table["down_w"]) * slope).astype(jnp.bfloat16)
    hidden_grad = pause(hidden_grad)
    mixed_part, gain_two, shift_two = norm_back(
        mixed, gains[1], shifts[1], mul_trans(hidden_grad, table["up_w"])
    )
    mixed_grad = group_rows(grad_out + mixed_part)
    branch_grad = mixed_grad.astype(jnp.bfloat16)
    attended_grad = mul_trans(branch_grad, table["out_w"]).astype(jnp.bfloat16)
    parts = attend_back(
        qkv[:, :D], qkv[:, D : 2 * D], qkv[:, 2 * D :], ids, ids, H, 0, attended_grad
    )
    qkv_grad = jnp.concatenate(parts, axis=1).astype(jnp.bfloat16)
    input_part, gain_one, shift_one = norm_back(
        inputs, gains[0], shifts[0], mul_trans(qkv_grad, table["qkv_w"])
    )
    patch_grad = (mixed_grad + input_part).astype(jnp.bfloat16)
    return (
        (patch_grad, qkv_grad, branch_grad, jnp.concatenate([hidden_grad, down_grad], axis=1)),
        (gain_one, shift_one, gain_two, shift_two),
    )


def core_side():
    return (lax.axis_index("grp") % 2).astype(jnp.int32).reshape(1)


def store_vector(target, first, lane, vector):
    width = vector.shape[1]
    done = 0
    while done < width:
        size = min(128 - lane, width - done)
        target[first : first + 1, lane : lane + size] = vector[:, done : done + size]
        done += size
        lane += size
        first, lane = first + lane // 128, lane % 128
    return first, lane


def column_sums(ref, first=0, width=None):
    width = ref.shape[1] if width is None else width
    cells = ref[:, first : first + width].astype(jnp.float32)
    return jnp.sum(cells, axis=0, keepdims=True)


def store_flat(target, product):
    rows, blocks = product.shape[0], product.shape[1] // 128
    for index in range(blocks):
        target[pl.ds(index, rows, stride=blocks), :] = product[:, index * 128 : (index + 1) * 128]


def column_blocks(ref, blocks):
    parts = [ref[:, pl.ds(pl.multiple_of(index * 128, 128), 128)] for index in blocks]
    return parts[0] if len(parts) == 1 else jnp.concatenate(parts, axis=1)


def steps_of(rows, size):
    return [(start, min(size, rows - start)) for start in range(0, rows, size)]


def enc_grad_kernel(plan, place_ref, *refs):
    norm_ref, own_norm_ref, out_ref, stage_ref, product_ref, small_ref, quarter_ref, sems = refs[
        -8:
    ]
    side, far = place_ref[0], place_ref[1]
    offset = 0
    flight = [None, None]
    turn = 0
    for size, left, first, depth, right, column, blocks in plan:
        x_ref, y_ref = refs[left], refs[right]
        if blocks % 2:
            columns = [2 * block + side for block in range(blocks)]
        else:
            columns = [4 * block + 2 * far + side for block in range(blocks // 2)]
        factor = column_blocks(y_ref, [column // 128 + block for block in columns])
        for start, rows in steps_of(depth, size):
            if flight[turn % 2] is not None:
                flight[turn % 2].wait()
            target = stage_ref.at[turn % 2]
            product = trans_mul(x_ref[:, first + start : first + start + rows], factor)
            if blocks % 2 == 0:
                store_flat(target, product)
            else:
                for block in range(blocks):
                    product_ref[block, :rows] = product[:, block * 128 : (block + 1) * 128]
                    odd = (far + block) % 2
                    target[
                        pl.ds((odd * blocks + block - far) // 2, rows // 2, stride=blocks), :
                    ] = product_ref.at[block][pl.ds(odd, rows // 2, stride=2), :]
            amount = rows * blocks // 2
            copy = pltpu.make_async_copy(
                target.at[pl.ds(0, amount)], out_ref.at[pl.ds(offset, amount)], sems.at[turn % 2]
            )
            copy.start()
            flight[turn % 2] = copy
            turn += 1
            offset += amount
    small_ref[...] = jnp.zeros_like(small_ref)
    spot = 0, 0
    for _, _, _, _, right, column, blocks in plan[:1] + plan[2:]:
        spot = store_vector(
            small_ref, *spot, column_sums(refs[right], column, blocks * 256)
        )
    rows = norm_ref.shape[0] // 4
    norms = sum(norm_ref[index * rows : (index + 1) * rows] for index in range(4))
    for vector in (
        own_norm_ref[0:1],
        norms[0:1],
        norms[1:2],
        own_norm_ref[1:2],
        norms[2:3],
        norms[3:4],
    ):
        spot = store_vector(small_ref, *spot, vector)
    rows = quarter_ref.shape[0]
    quarter_ref[...] = small_ref[pl.ds(side + 2 * far, rows, stride=4), :]
    last = pltpu.make_async_copy(quarter_ref, out_ref.at[pl.ds(offset, rows)], sems.at[2])
    last.start()
    for copy in [last] + flight:
        copy.wait()


def member_place():
    place = lax.axis_index("grp").astype(jnp.int32)
    return jnp.stack([place % 2, place // 2])


def enc_grad_quarter(inputs, grads, norms, own_norms, total_rows):
    count = len(inputs)
    plan = [
        (640, 0, 0, PATCH, count, 0, D // 256),
        (256, 1, 0, D, count + 1, 0, 3 * D // 256),
        (384, 2, 0, D, count + 2, 0, D // 256),
        (256, 2, D, D, count + 3, 0, F // 256),
        (768, 2, 2 * D, F, count + 3, F, D // 256),
    ]
    whole = pl.BlockSpec(memory_space=pltpu.VMEM)
    return pl.pallas_call(
        functools.partial(enc_grad_kernel, plan),
        in_specs=[pl.BlockSpec(memory_space=pltpu.SMEM)] + [whole] * (count + len(grads) + 2),
        out_specs=pl.BlockSpec(memory_space=pl.ANY),
        out_shape=jax.ShapeDtypeStruct((total_rows // 4, 128), jnp.float32),
        scratch_shapes=[
            pltpu.VMEM((2, 1536, 128), jnp.float32),
            pltpu.VMEM((9, 768, 128), jnp.float32),
            pltpu.VMEM((384, 128), jnp.float32),
            pltpu.VMEM((96, 128), jnp.float32),
            pltpu.SemaphoreType.DMA((3,)),
        ],
        compiler_params=pltpu.CompilerParams(vmem_limit_bytes=48 << 20),
        cost_estimate=pl.CostEstimate(
            flops=total_rows * 128 * inputs[0].shape[0],
            bytes_accessed=total_rows * 128,
            transcendentals=0,
        ),
    )(member_place(), *inputs, *grads, norms, own_norms)


def store_pixels(product_ref, targets):
    groups = product_ref.shape[1] // 4

    def load(row, block):
        return product_ref.at[block][pl.ds(row, groups, stride=4), :]

    def piece(row, block):
        if block < 13:
            return load(row, block)
        if block == 13:
            left, right = load(row, 13)[:, :64], load(row + 1, 0)[:, :64]
        else:
            left, right = load(row + 1, block - 14)[:, 64:], load(row + 1, block - 13)[:, :64]
        return jnp.concatenate([left, right], axis=1)

    for index in range(54):
        block = piece(0, index) if index < 27 else piece(2, index - 27)
        targets[index % 2][pl.ds(index // 2, groups, stride=27), :] = block


def dec_grad_kernel(plan, side_ref, *refs):
    norm_ref, mine_ref, theirs_ref, stage_ref, pixel_ref, small_ref, halves_ref, sems = refs[-8:]
    side = side_ref[0]
    flight = [None, None]
    turn = 0
    for index, (size, offset) in enumerate(plan):
        x_ref, y_ref = refs[2 * index], refs[2 * index + 1]
        pixels = y_ref.shape[1] % 256 != 0
        for start, rows in steps_of(x_ref.shape[1], size):
            product = trans_mul(x_ref[:, start : start + rows], y_ref[...])
            slot = turn % 2
            for copy in flight[slot] or ():
                copy.wait()
            if pixels:
                for block in range(14):
                    part = product[:, block * 128 : (block + 1) * 128]
                    pixel_ref[block, :, : part.shape[1]] = part
                store_pixels(pixel_ref, [stage_ref.at[slot, 0], stage_ref.at[slot, 1]])
            else:
                blocks = y_ref.shape[1] // 128
                for block in range(blocks):
                    stage_ref.at[slot, block % 2][
                        pl.ds(block // 2, rows, stride=blocks // 2), :
                    ] = product[:, block * 128 : (block + 1) * 128]
            amount = rows * y_ref.shape[1] // 256
            flight[slot] = [
                pltpu.make_async_copy(
                    stage_ref.at[slot, parity, pl.ds(0, amount)],
                    target.at[pl.ds(offset, amount)],
                    sems.at[slot, order],
                )
                for order, (parity, target) in enumerate(
                    ((side, mine_ref), (1 - side, theirs_ref))
                )
            ]
            for copy in flight[slot]:
                copy.start()
            offset += amount
            turn += 1
    small_ref[...] = jnp.zeros_like(small_ref)
    spot = store_vector(small_ref, 0, 0, column_sums(refs[1]))
    spot = store_vector(small_ref, *spot, norm_ref[0:1])
    for index in (2, 3, 4, 5):
        spot = store_vector(small_ref, *spot, column_sums(refs[2 * index + 1]))
    for index in range(1, norm_ref.shape[0]):
        spot = store_vector(small_ref, *spot, norm_ref[index : index + 1])
    rows = halves_ref.shape[1]
    for parity in range(2):
        halves_ref[parity] = small_ref[pl.ds(parity, rows, stride=2), :]
    last = [
        pltpu.make_async_copy(
            halves_ref.at[parity], target.at[pl.ds(target.shape[0] - rows, rows)], sems.at[2, order]
        )
        for order, (parity, target) in enumerate(((side, mine_ref), (1 - side, theirs_ref)))
    ]
    for copy in last:
        copy.start()
    for copy in last + flight[0] + flight[1]:
        copy.wait()


def dec_grad_halves(pairs, norms, total_rows):
    plan = [(256, 0), (256, 1536), (256, 4608), (256, 5632), (512, 9728), (512, 13824)]
    operands = [part for pair in pairs for part in pair]
    whole = pl.BlockSpec(memory_space=pltpu.VMEM)
    anywhere = pl.BlockSpec(memory_space=pl.ANY)
    shape = jax.ShapeDtypeStruct((total_rows // 2, 128), jnp.float32)
    return pl.pallas_call(
        functools.partial(dec_grad_kernel, plan),
        in_specs=[pl.BlockSpec(memory_space=pltpu.SMEM)] + [whole] * (len(operands) + 1),
        out_specs=[anywhere, anywhere],
        out_shape=[shape, shape],
        scratch_shapes=[
            pltpu.VMEM((2, 2, 3456, 128), jnp.float32),
            pltpu.VMEM((14, 512, 128), jnp.float32),
            pltpu.VMEM((256, 128), jnp.float32),
            pltpu.VMEM((2, 128, 128), jnp.float32),
            pltpu.SemaphoreType.DMA((3, 2)),
        ],
        compiler_params=pltpu.CompilerParams(vmem_limit_bytes=56 << 20),
        cost_estimate=pl.CostEstimate(
            flops=total_rows * 256 * pairs[1][0].shape[0],
            bytes_accessed=total_rows * 512,
            transcendentals=0,
        ),
    )(core_side(), *operands, norms)


def adamw_kernel(parts, with_average, place_ref, scalar_ref, *refs):
    count = 4 if with_average else 3
    ins, outs, grad_ref = refs[parts : parts + count], refs[parts + count : -1], refs[-1]
    for index in range(parts):
        rows = refs[index].shape[0]
        grad_ref[pl.ds(place_ref[index], rows, stride=parts), :] = refs[index][...]
    weights = ins[0][...]
    clipped = grad_ref[...] * scalar_ref[0]
    first_new = BETA_ONE * ins[1][...] + (1.0 - BETA_ONE) * clipped
    second_new = BETA_TWO * ins[2][...] + (1.0 - BETA_TWO) * clipped * clipped
    first_hat = first_new / scalar_ref[1]
    second_hat = second_new / scalar_ref[2]
    weights_new = weights * (1.0 - LEARN_RATE * WEIGHT_DECAY) - LEARN_RATE * first_hat / (
        jnp.sqrt(second_hat) + ADAM_EPS
    )
    outs[0][...] = weights_new
    outs[1][...] = first_new
    outs[2][...] = second_new
    outs[3][...] = weights_new.astype(jnp.bfloat16)
    if with_average:
        outs[4][...] = EMA_RATE * ins[3][...] + (1.0 - EMA_RATE) * weights_new


def adamw(parts, arrays, factor, steps_done):
    count = len(parts)
    place = lax.axis_index("grp")
    places = jnp.stack([(place ^ index) % count for index in range(count)])
    rows = arrays[0].shape[0]
    steps = 1
    for split in (2, 3, 4, 6, 8):
        if rows % (split * 8 * count) == 0:
            steps = split
    block = pl.BlockSpec((rows // steps, 128), lambda i: (i, 0))
    share = pl.BlockSpec((rows // steps // count, 128), lambda i: (i, 0))
    scalar = pl.BlockSpec(memory_space=pltpu.SMEM)
    scalars = jnp.stack([factor, 1.0 - BETA_ONE**steps_done, 1.0 - BETA_TWO**steps_done])
    full = jax.ShapeDtypeStruct((rows, 128), jnp.float32)
    shapes = [full, full, full, jax.ShapeDtypeStruct((rows, 128), jnp.bfloat16)]
    if len(arrays) == 4:
        shapes.append(full)
    return pl.pallas_call(
        functools.partial(adamw_kernel, count, len(arrays) == 4),
        grid=(steps,),
        in_specs=[scalar, scalar] + [share] * count + [block] * len(arrays),
        out_specs=[block] * len(shapes),
        out_shape=shapes,
        scratch_shapes=[pltpu.VMEM((rows // steps, 128), jnp.float32)],
        compiler_params=pltpu.CompilerParams(vmem_limit_bytes=40 << 20),
    )(places.astype(jnp.int32), scalars, *parts, *arrays)


def per_device(
    patches,
    segments,
    visible,
    enc_params,
    enc_first,
    enc_second,
    enc_average,
    dec_params,
    dec_first,
    dec_second,
    step_count,
):
    my_index = lax.axis_index("grp")
    slot_dev = segments.shape[0]
    rim = TILE_HI
    counts = jnp.sum((segments >= 0).astype(jnp.float32)) - visible.shape[0]
    total_count = total(jnp.full((8, 128), counts))[0, 0]
    enc_copy = gather_quarters(enc_params.astype(jnp.bfloat16))
    group_vis = group_rows(visible)
    group_seg = double(double(segments, 0, "grp", 2), 1, "grp", 1).reshape(-1)
    group_ids = group_seg[group_vis]
    key_ids = extended(segments + 3, rim) - 3
    local_slot = group_vis - my_index * slot_dev
    chosen = (
        local_slot[:, None] == jnp.arange(slot_dev, dtype=jnp.int32)[None, :]
    ).astype(jnp.bfloat16)
    seen = jnp.sum(chosen.astype(jnp.float32), axis=0) > 0.5
    enc_input = group_rows(own_rows(matmul(chosen, patches).astype(jnp.bfloat16)))
    enc_waves = sincos(group_vis % L, D)
    positions = (my_index * slot_dev + jnp.arange(slot_dev, dtype=jnp.int32)) % L
    dec_waves = sincos(positions, E)
    pixels = patches.astype(jnp.float32)
    pixel_mean = jnp.mean(pixels, axis=1, keepdims=True)
    centered = pixels - pixel_mean
    pixel_rate = lax.rsqrt(jnp.mean(centered * centered, axis=1, keepdims=True) + NORM_EPS)
    (
        enc_copy,
        enc_input,
        enc_waves,
        dec_waves,
        pixel_mean,
        pixel_rate,
        seen,
        group_ids,
        key_ids,
        chosen,
        total_count,
    ) = lax.optimization_barrier(
        (
            enc_copy,
            enc_input,
            enc_waves,
            dec_waves,
            pixel_mean,
            pixel_rate,
            seen,
            group_ids,
            key_ids,
            chosen,
            total_count,
        )
    )
    enc_copy, dec_shard = lax.optimization_barrier((enc_copy, dec_params))
    dec_copy = gather_quarters(dec_shard.astype(jnp.bfloat16))
    enc_table = unpack(enc_copy, enc_pieces(), ENC_STEPS)
    dec_table = unpack(dec_copy, dec_pieces(), DEC_STEPS)
    enc_start = (
        matmul(enc_input, enc_table["patch_w"])
        + enc_table["patch_b"].astype(jnp.float32)
        + enc_waves
    )

    own = visible.shape[0]
    enc_out, enc_saved = enc_forward(enc_start, enc_table, own, group_ids)
    enc_gain = enc_table["norm_g"].astype(jnp.float32)
    enc_shift = enc_table["norm_b"].astype(jnp.float32)
    enc_final = layer_norm(enc_out, enc_gain[2], enc_shift[2]).astype(jnp.bfloat16)
    latent = (
        matmul(enc_final, dec_table["embed_w"]) + dec_table["embed_b"].astype(jnp.float32)
    ).astype(jnp.bfloat16)
    group_latent = group_rows(latent)
    enc_inputs = jnp.concatenate([enc_saved[2], enc_saved[4], enc_saved[6]], axis=1)
    group_latent, enc_inputs = lax.optimization_barrier((group_latent, enc_inputs))
    group_inputs = group_rows(enc_inputs)
    placed = trans_mul(chosen, group_latent)
    dec_start = jnp.where(
        seen[:, None], placed, dec_table["mask_token"].astype(jnp.float32)[None, :]
    ) + dec_waves
    counted = jnp.where((segments >= 0) & jnp.logical_not(seen), 1.0, 0.0)

    def dec_share(pair):
        joined = extended(jnp.concatenate(pair, axis=1), rim)
        return (joined[:, :E], joined[:, E:])

    dec_out, dec_saved = block_forward(
        dec_start, dec_table, EH, rim, segments, key_ids, dec_share
    )
    dec_gain = dec_table["norm_g"].astype(jnp.float32)
    dec_shift = dec_table["norm_b"].astype(jnp.float32)
    dec_final = layer_norm(dec_out, dec_gain[2], dec_shift[2]).astype(jnp.bfloat16)
    predicted = matmul(dec_final, dec_table["pix_w"]) + dec_table["pix_b"].astype(jnp.float32)
    target = (patches.astype(jnp.float32) - pixel_mean) * pixel_rate
    errors = predicted - target
    loss_part = jnp.sum(counted * jnp.mean(errors * errors, axis=1))
    errors, group_inputs = lax.optimization_barrier((errors, group_inputs))
    pred_grad = (counted[:, None] * errors * (2.0 / PATCH) / total_count).astype(jnp.bfloat16)
    dec_out_grad, dec_gain_last, dec_shift_last = norm_back(
        dec_out, dec_gain[2], dec_shift[2], mul_trans(pred_grad, dec_table["pix_w"])
    )
    start_grad, dec_small, dec_pairs = block_backward(
        dec_out_grad, dec_table, EH, rim, segments, key_ids, dec_saved
    )
    mask_grad = jnp.sum(jnp.where(seen[:, None], 0.0, start_grad), axis=0)
    latent_grad = own_rows(matmul(chosen, start_grad.astype(jnp.bfloat16)).astype(jnp.bfloat16))
    dec_pairs["embed_w"] = (enc_final, latent_grad)
    dec_pairs["pix_w"] = (dec_final, pred_grad)
    mine, theirs = dec_grad_halves(
        [dec_pairs[name] for name in ("embed_w", "qkv_w", "out_w", "up_w", "down_w", "pix_w")],
        jnp.stack(
            [
                mask_grad,
                dec_small[0],
                dec_small[2],
                dec_gain_last,
                dec_small[1],
                dec_small[3],
                dec_shift_last,
            ]
        ),
        DR,
    )
    arrived = swap(theirs, "grp", 1)
    latent_grad, mine = lax.optimization_barrier((latent_grad, mine))
    dec_blocks = None

    def enc_pause(grad):
        nonlocal dec_blocks
        grad, dec_half = lax.optimization_barrier((grad, mine + arrived))
        dec_blocks = reduce_first(dec_half, dec_routes(), (0.5,))
        return grad

    enc_out_grad, enc_gain_last, enc_shift_last = norm_back(
        enc_out, enc_gain[2], enc_shift[2], mul_trans(latent_grad, dec_table["embed_w"])
    )
    enc_grads, enc_small = enc_backward(
        enc_out_grad, enc_table, enc_start, group_ids, enc_saved, enc_pause
    )
    enc_norms = jnp.stack([enc_small[2], enc_gain_last, enc_small[3], enc_shift_last])
    branch_grad, far_grad, enc_norms = lax.optimization_barrier(
        (enc_grads[2], enc_grads[3], enc_norms)
    )
    enc_quarter = enc_grad_quarter(
        [enc_input, enc_saved[0], group_inputs],
        [*enc_grads[:2], branch_grad, group_rows(far_grad)],
        group_rows(enc_norms),
        jnp.stack([enc_small[0], enc_small[1]]),
        ER,
    )
    enc_quarter, dec_blocks = lax.optimization_barrier((enc_quarter, dec_blocks))
    enc_blocks = reduce_first(enc_quarter, dp_routes(), (0.5,))
    dec_blocks = reduce_rest(dec_blocks, dec_routes(), 1, 2)
    enc_blocks = reduce_rest(enc_blocks, dp_routes(), 1, 2)
    enc_blocks, dec_blocks = lax.optimization_barrier((enc_blocks, dec_blocks))
    enc_sum = reduce_rest(enc_blocks, dp_routes(), 2)
    enc_own = jnp.concatenate(enc_sum, axis=0)
    enc_across = swap(enc_own, "grp", 2)
    dec_sum = reduce_rest(dec_blocks, dec_routes(), 2)
    squares = sum(jnp.sum(part * part) for part in enc_sum + dec_sum)
    lane = lax.broadcasted_iota(jnp.int32, (8, 128), 1)
    sums = total(jnp.where(lane == 0, squares, jnp.where(lane == 1, loss_part, 0.0)))
    dec_wide = [double(piece, 0, "grp", 2).reshape(-1, 128) for piece in dec_sum]
    enc_quarters = (
        enc_own,
        swap(enc_own, "grp", 1),
        enc_across,
        swap(enc_across, "grp", 1),
    )
    dec_mine = jnp.concatenate(dec_wide, axis=0)
    dec_halves = dec_mine, swap(dec_mine, "grp", 1)
    loss_total = sums[0, 1]
    grad_norm = jnp.sqrt(sums[0, 0])
    factor = jnp.minimum(1.0, CLIP_LIMIT / (grad_norm + NORM_EPS))
    steps_done = step_count[0].astype(jnp.float32)
    enc_new, enc_first_new, enc_second_new, enc_copy_new, average_new = adamw(
        enc_quarters, (enc_params, enc_first, enc_second, enc_average), factor, steps_done
    )
    dec_new, dec_first_new, dec_second_new, dec_copy_new = adamw(
        dec_halves, (dec_params, dec_first, dec_second), factor, steps_done
    )
    return (
        enc_new,
        enc_first_new,
        enc_second_new,
        enc_copy_new,
        dec_new,
        dec_first_new,
        dec_second_new,
        dec_copy_new,
        average_new,
        grad_norm,
        loss_total,
        total_count,
    )


def solution(mesh):
    placed = (
        P(("dp", "grp"), None),
        P(("dp", "grp")),
        P(("dp", "grp")),
        P("dp", None),
        P("dp", None),
        P("dp", None),
        P("dp", None),
        P("dp", None),
        P("dp", None),
        P("dp", None),
        P(),
    )
    return jax.shard_map(
        per_device,
        mesh=mesh,
        in_specs=placed,
        out_specs=(
            P("dp", None),
            P("dp", None),
            P("dp", None),
            P("dp", None),
            P("dp", None),
            P("dp", None),
            P("dp", None),
            P("dp", None),
            P("dp", None),
            P(),
            P(),
            P(),
        ),
        check_vma=False,
    )
```
